32 devices in a mesh: parts: 2 (over y), row: 4 (over z), col: 4 (over x, core), sub: 1.
Axes of the slice: x: 2, y: 2, z: 4, core: 2. Of those that a mesh axis runs over, the one named last changes fastest.
Arguments:
- activations: bfloat16 [1024, 2048], P(('parts', 'row'), ('col', 'sub')), parts along dimension 0, may hold values from -6 to 6
- expert_ids: int32 [1024, 8], P(('parts', 'row')), parts along dimension 0, may hold values from 0 to 15, all different within a row; in each aligned block of 32 rows (0 to 31, 32 to 63, ...) at most 32 rows name the same one
- gate_scores: float32 [1024, 8], P(('parts', 'row')), parts along dimension 0, may hold values from 0.05 to 0.5
- gate_proj: bfloat16 [16, 2048, 768], P(('row', 'col'), None, 'sub'), may hold values from -0.125 to 0.125
- up_proj: bfloat16 [16, 2048, 768], P(('row', 'col'), None, 'sub'), may hold values from -0.125 to 0.125
- down_proj: bfloat16 [16, 768, 2048], P(('row', 'col'), 'sub'), may hold values from -0.21875 to 0.21875
Outputs:
- moe_output: bfloat16 [1024, 2048], P(('parts', 'row'), ('col', 'sub')), parts along dimension 0
The draws below stay inside these ranges and needn't reach their ends.
There are 2 independent parts, one for each index of `parts`. The reference program is written for one: setup_inputs(seed, part) draws one part's arguments, and reference() takes and returns one part's arrays. A program takes and returns all parts, laid end to end along the dimension named above; an argument that names none is the same for every part. Nothing has to cross between parts.
Inputs may be any that keep to these rules, and one draw needn't show every extreme that they name: `expert_ids`: each row names 8 different experts. In each aligned block of 32 rows no expert is named by more than 32 rows, a bound that some block reaches.
All inputs are finite; a program needn't handle non-finite values.
Results may differ from the reference program's by a relative error of at most 0.0057.
Values may be sent and summed in bfloat16 or wider, within the bound.
A program may use at most 64 MiB of HBM per device.

```python
import math
import jax
import jax.numpy as jnp
import numpy as np
from jax import lax

D = 2048
HID = 768
TOP = 8
E = 16
TOKENS = 512
BLOCK = 32
CAP = 32


def steps_of(own_key, extent, pieces, smallest, high):
    def one(position, shards_of):
        steps = jax.random.uniform(jax.random.fold_in(jax.random.fold_in(own_key, 6), position), (shards_of,), jnp.float32, smallest / len(pieces), high / len(pieces))
        return jnp.repeat(jnp.exp(steps), extent[position] // shards_of).reshape((-1,) + (1,) * (len(extent) - position - 1))

    gain = one(*pieces[0])
    for cut in pieces[1:]:
        gain = gain * one(*cut)
    return gain


def shared_out(stream_key, own, number, rows, number_of, top, reach, slope):
    ranking = jax.random.permutation(stream_key, number_of)
    heavy_load, usual = shares(number_of, rows * top, reach, slope, True), shares(number_of, rows * top, reach, slope, False)
    places = jnp.arange(number_of)

    def named(sizes, rotation):
        used = int((sizes > 0).sum())
        fixed = max(1, used // 4)
        passed = fixed + (places - fixed + rotation * (used - fixed)) % max(1, number_of - fixed)
        return jnp.zeros((number_of,), jnp.int32).at[ranking[jnp.where(places < fixed, places, passed)]].set(jnp.asarray(sizes, jnp.int32))

    sizes = jnp.where(number % 4 == 0, named(heavy_load, number // 4), named(usual, number - number // 4 - 1))
    mixed = jax.random.permutation(jax.random.fold_in(own, 3), number_of)
    giver, sink = mixed[0:number_of // 2 * 2:2], mixed[1:number_of // 2 * 2:2]
    slack = jnp.minimum(sizes[giver] - 1, reach - sizes[sink]) // 2
    slack = jnp.where((giver == ranking[0]) | (sink == ranking[0]) | (sizes[sink] == 0), 0, jnp.maximum(slack, 0))
    passed = jax.random.randint(jax.random.fold_in(own, 4), (number_of // 2,), 0, 1 << 20) % (slack + 1)
    sizes = sizes.at[giver].add(-passed).at[sink].add(passed)
    members = jnp.searchsorted(jnp.cumsum(sizes), jnp.arange(rows * top), side="right").astype(jnp.int32)
    grid = members.reshape(top, rows).T
    grid = grid[jax.random.permutation(jax.random.fold_in(own, 1), rows)]
    rotation = jax.random.randint(jax.random.fold_in(own, 2), (rows, 1), 0, top)
    return jnp.take_along_axis(grid, (jnp.arange(top)[None, :] + rotation) % top, axis=1)


def shares(amount, total, limit, lean, full):
    portions = [(1 << 20) // math.isqrt(grade ** lean) + 1 for grade in range(1, amount + 1)]
    largest = limit if full else min(limit, max(-(-total // amount), total * portions[0] // sum(portions)))
    least = 1 if total - largest >= amount - 1 else 0
    given, surplus = [largest] + [least] * (amount - 1), total - largest - least * (amount - 1)
    while surplus > 0:
        free = [i for i in range(1, amount) if given[i] < largest] or [i for i in range(1, amount) if given[i] < limit]
        mass, budget = sum([portions[i] for i in free]), surplus
        for i in free:
            more = min(limit - given[i], max(1, budget * portions[i] // mass), surplus)
            given[i] = given[i] + more
            surplus = surplus - more
    return np.array(given)


def normal_values(key, dims, deviation, limit, pieces=(), held_as=jnp.bfloat16):
    drawn = deviation * jax.random.normal(key, dims, jnp.float32)
    if pieces:
        drawn = drawn * steps_of(key, dims, pieces, -0.22, 0.18)
    return jnp.clip(drawn, -limit, limit).astype(held_as)


def setup_inputs(seed: int = 0, part: int = 0) -> dict:
    seeds = jax.random.split(jax.random.key(seed), 7)
    part_splits = jax.random.split(jax.random.fold_in(seeds[6], part), 7)
    activations = normal_values(part_splits[0], (TOKENS, D), 1.0, 6.0, ((0, 4), (1, 4)))
    expert_ids_keys = jax.random.split(jax.random.fold_in(part_splits[1], 1), TOKENS // BLOCK)
    expert_ids_turns = jax.random.permutation(jax.random.fold_in(part_splits[1], 3), TOKENS // BLOCK)
    expert_ids = jax.vmap(lambda own, number: shared_out(jax.random.fold_in(part_splits[1], 2), own, number, BLOCK, E, TOP, CAP, 2))(expert_ids_keys, expert_ids_turns).reshape((TOKENS, TOP))
    gate_scores = jnp.clip(jnp.exp(math.log(0.5) - 2.3025851 * jax.random.uniform(part_splits[2], (TOKENS, TOP), jnp.float32) ** steps_of(part_splits[2], (TOKENS, TOP), ((0, 4),), -0.2, 0.2)), 0.05, 0.5)
    gate_proj = normal_values(seeds[3], (E, D, HID), D ** -0.5, 0.125, ((0, 16),))
    up_proj = normal_values(seeds[4], (E, D, HID), D ** -0.5, 0.125, ((0, 16),))
    down_proj = normal_values(seeds[5], (E, HID, D), HID ** -0.5, 0.21875, ((0, 16),))
    return {"activations": activations, "expert_ids": expert_ids, "gate_scores": gate_scores, "gate_proj": gate_proj, "up_proj": up_proj, "down_proj": down_proj}


def reference(activations, expert_ids, gate_scores, gate_proj, up_proj, down_proj):
    blocks = TOKENS // BLOCK
    per_block = BLOCK * TOP
    grouped = expert_ids.reshape(blocks, per_block).astype(jnp.int32)
    numbers = jnp.arange(E, dtype=jnp.int32)
    onehot = (grouped[:, :, None] == numbers[None, None, :]).astype(jnp.int32)
    running = jnp.cumsum(onehot, axis=1).astype(jnp.int32) - 1
    slot_rank = jnp.sum(onehot * running, axis=2).astype(jnp.int32)
    block_ids = jnp.broadcast_to(jnp.arange(blocks, dtype=jnp.int32)[:, None], (blocks, per_block))
    assigned = jnp.arange(TOKENS * TOP, dtype=jnp.int32).reshape(blocks, per_block)
    slot_table = jnp.full((blocks, E, CAP), TOKENS * TOP, jnp.int32)
    slot_table = slot_table.at[block_ids, grouped, slot_rank].set(assigned)
    scores = jnp.concatenate([gate_scores.reshape(TOKENS * TOP), jnp.zeros((1,), jnp.float32)])
    padded = jnp.concatenate([activations, jnp.zeros((1, D), activations.dtype)], axis=0)

    def one_expert(summed, expert):
        slot_ids = lax.dynamic_index_in_dim(slot_table, expert, axis=1, keepdims=False).reshape(blocks * CAP)
        row_ids = (slot_ids // TOP).astype(jnp.int32)
        inputs = padded[row_ids]
        gate_val = jnp.dot(inputs, gate_proj[expert], preferred_element_type=jnp.float32)
        up_val = jnp.dot(inputs, up_proj[expert], preferred_element_type=jnp.float32)
        hidden = (jax.nn.silu(gate_val) * up_val).astype(jnp.bfloat16)
        rounded = jnp.dot(hidden, down_proj[expert], preferred_element_type=jnp.float32).astype(jnp.bfloat16)
        rounded = lax.optimization_barrier(rounded)
        result = rounded.astype(jnp.float32)
        summed = summed.at[row_ids].add(scores[slot_ids][:, None] * result)
        return summed, None

    summed, unused = lax.scan(one_expert, jnp.zeros((TOKENS + 1, D), jnp.float32), jnp.arange(E, dtype=jnp.int32))
    return summed[:TOKENS].astype(jnp.bfloat16)
```

```python
import functools

import jax
import jax.numpy as jnp
from jax import lax
from jax.experimental import pallas as pl
from jax.experimental.pallas import tpu as pltpu
from jax.sharding import PartitionSpec as P

TOP = 8
PAIR = 2
MESH = pl.DeviceIdType.MESH


def slot_places(chosen, experts, capacity):
    count = chosen.shape[0] * chosen.shape[1]
    flat_ids = chosen.reshape(count)
    onehot = (flat_ids[:, None] == jnp.arange(experts, dtype=jnp.int32)[None, :]).astype(jnp.int32)
    running = jnp.cumsum(onehot, axis=0) - 1
    ranking = jnp.sum(onehot * running, axis=1)
    return flat_ids * capacity + ranking


def fill_slots(row_block, places, experts, capacity, top_count):
    owners = jnp.full((experts * capacity,), row_block.shape[0], jnp.int32)
    owners = owners.at[places].set(jnp.arange(places.shape[0], dtype=jnp.int32) // top_count)
    padded = jnp.concatenate(
        [row_block, jnp.zeros((1, row_block.shape[1]), row_block.dtype)], axis=0
    )
    return padded[owners].reshape(experts, capacity, row_block.shape[1])


def run_expert(stacked, gate_proj, up_proj, down_proj):
    layout = stacked.shape
    inputs = stacked.reshape(-1, layout[-1])
    gate_val = jnp.dot(inputs, gate_proj[0], preferred_element_type=jnp.float32)
    up_val = jnp.dot(inputs, up_proj[0], preferred_element_type=jnp.float32)
    hidden = (jax.nn.silu(gate_val) * up_val).astype(jnp.bfloat16)
    partial_out = jnp.dot(hidden, down_proj[0], preferred_element_type=jnp.float32)
    return partial_out.reshape(layout)


def send_back(stacked, gate_proj, up_proj, down_proj):
    partial_out = run_expert(stacked, gate_proj, up_proj, down_proj)
    landed = lax.all_to_all(partial_out, ("row", "col"), split_axis=1, concat_axis=1, tiled=True)
    return lax.psum_scatter(landed, "sub", scatter_dimension=0, tiled=True).astype(jnp.bfloat16)


def per_device(activations, expert_ids, gate_scores, gate_proj, up_proj, down_proj):
    col_count = lax.axis_size("col")
    sub_count = lax.axis_size("sub")
    experts = lax.axis_size("row") * col_count
    group_rows = expert_ids.shape[0]
    block_rows = group_rows // (col_count * sub_count)
    capacity = max(2, min(block_rows, 2 * block_rows * TOP // experts))
    quarter = sub_count * block_rows
    width = activations.shape[1] * col_count * sub_count
    whole = lax.all_gather(activations, ("col", "sub"), axis=1, tiled=True)
    col_start = lax.axis_index("col") * quarter
    sub_index = lax.axis_index("sub")
    my_rows = lax.dynamic_slice_in_dim(whole, col_start, quarter, 0)
    my_ids = lax.dynamic_slice_in_dim(expert_ids, col_start, quarter, 0)
    own_scores = lax.dynamic_slice_in_dim(
        gate_scores, col_start + sub_index * block_rows, block_rows, 0
    )
    places = []
    for member in range(sub_count):
        lower = member * block_rows
        places.append(slot_places(my_ids[lower : lower + block_rows], experts, capacity))
    own_places = lax.dynamic_index_in_dim(jnp.stack(places), sub_index, 0, keepdims=False)
    buffers = []
    for member in range(sub_count):
        lower = member * block_rows
        buffers.append(
            fill_slots(my_rows[lower : lower + block_rows], places[member], experts, capacity, TOP)
        )
    outgoing = jnp.stack(buffers)
    returned = send_back(
        lax.all_to_all(outgoing, ("row", "col"), split_axis=1, concat_axis=1, tiled=True),
        gate_proj,
        up_proj,
        down_proj,
    )
    picked = returned.reshape(-1, width)[own_places].reshape(block_rows, TOP, width)
    share = jnp.sum(own_scores[:, :, None] * picked.astype(jnp.float32), axis=1)
    return lax.all_to_all(
        share.astype(jnp.bfloat16), ("col", "sub"), split_axis=1, concat_axis=0, tiled=True
    )


def dense_kernel(
    rows,
    acts_hbm,
    ids_ref,
    scores_ref,
    gate_hbm,
    up_hbm,
    down_hbm,
    out_ref,
    acts,
    meta,
    gate_w,
    up_w,
    down_w,
    kept,
    core_out,
    core_in,
    total,
    x_out,
    x_in,
    z_out,
    z_in,
    weight_sem,
    own_sem,
    ag_z_send,
    ag_z_recv,
    meta_send,
    meta_recv,
    ag_x_send,
    ag_x_recv,
    ag_core_send,
    ag_core_recv,
    rs_core_send,
    rs_core_recv,
    rs_x_send,
    rs_x_recv,
    rs_z_send,
    rs_z_recv,
):
    top = ids_ref.shape[0]
    width = acts_hbm.shape[1]
    z = lax.axis_index("row")
    col = lax.axis_index("col")
    x, core = col // PAIR, col % PAIR
    expert = z * lax.axis_size("col") + col
    sibling = {"col": x * PAIR + (1 - core)}
    across = {"col": (1 - x) * PAIR + core}
    last = rows - 1

    def column(x_of, core_of):
        return pl.ds(pl.multiple_of((x_of * PAIR + core_of) * width, width), width)

    def nth_row(s):
        both = jnp.minimum(z, last - z)
        far = (s + 1) // 2
        near = jnp.where(s % 2 == 1, z - far, z + far)
        rest = jnp.where(z <= last - z, s, last - s)
        return jnp.where(s <= 2 * both, near, rest)

    def remote(src, dst, send, recv, device):
        return pltpu.make_async_remote_copy(
            src_ref=src, dst_ref=dst, send_sem=send, recv_sem=recv, device_id=device, device_id_type=MESH
        )

    def place(r, x_of, core_of):
        return acts.at[r, :, column(x_of, core_of)]

    def gather_z(r, side, src=None):
        there = place(r, x, core)
        return remote(
            there if src is None else src, there, ag_z_send.at[side, r], ag_z_recv.at[r], {"row": z + 2 * side - 1}
        )

    def gather_meta(r, side):
        return remote(
            meta.at[r], meta.at[r], meta_send.at[side, r], meta_recv.at[r], {"row": z + 2 * side - 1}
        )

    def gather_x(r, src=None):
        there = place(r, x, core)
        return remote(there if src is None else src, there, ag_x_send.at[r], ag_x_recv.at[r], across)

    def gather_core(r, which, src=None):
        x_of = x if which == 0 else 1 - x
        there = place(r, x_of, core)
        return remote(
            there if src is None else src, there, ag_core_send.at[r, which], ag_core_recv.at[r, which], sibling
        )

    def reduce_core(r):
        return remote(core_out.at[r], core_in.at[r], rs_core_send.at[r], rs_core_recv.at[r], sibling)

    def reduce_x(r):
        return remote(x_out.at[r], x_in.at[r], rs_x_send.at[r], rs_x_recv.at[r], across)

    def reduce_z(r, side):
        return remote(
            z_out.at[r],
            z_in.at[side, r],
            rs_z_send.at[r],
            rs_z_recv.at[side, r],
            {"row": z + 2 * side - 1},
        )

    def weight_copies():
        return [
            pltpu.make_async_copy(src.at[0], dst, weight_sem.at[i])
            for i, (src, dst) in enumerate(((gate_hbm, gate_w), (up_hbm, up_w), (down_hbm, down_w)))
        ]

    own = pltpu.make_async_copy(acts_hbm, place(z, x, core), own_sem)
    own.start()
    meta[z, :top] = ids_ref[...].astype(jnp.float32)
    meta[z, top:] = scores_ref[...]

    barrier = pltpu.get_barrier_semaphore()
    pl.semaphore_signal(barrier, inc=1, device_id=sibling, device_id_type=MESH)
    pl.semaphore_signal(barrier, inc=1, device_id=across, device_id_type=MESH)

    @pl.when(z > 0)
    def _():
        pl.semaphore_signal(barrier, inc=1, device_id={"row": z - 1}, device_id_type=MESH)

    @pl.when(z < last)
    def _():
        pl.semaphore_signal(barrier, inc=1, device_id={"row": z + 1}, device_id_type=MESH)

    pl.semaphore_wait(barrier, 2 + jnp.where(z > 0, 1, 0) + jnp.where(z < last, 1, 0))

    gather_x(z, acts_hbm).start()

    @pl.when(z > 0)
    def _():
        gather_meta(z, 0).start()
        gather_z(z, 0, acts_hbm).start()

    @pl.when(z < last)
    def _():
        gather_meta(z, 1).start()
        gather_z(z, 1, acts_hbm).start()

    gather_core(z, 0, acts_hbm).start()
    for copy in weight_copies():
        copy.start()

    def pass_on(r):
        gather_z(r, 0).wait_recv()
        gather_meta(r, 0).wait_recv()

        @pl.when((r < z) & (z < last))
        def _():
            gather_meta(r, 1).start()
            gather_z(r, 1).start()

        @pl.when((r > z) & (z > 0))
        def _():
            gather_meta(r, 0).start()
            gather_z(r, 0).start()

        gather_x(r).start()
        gather_core(r, 0).start()

    def cross(r):
        reduce_core(r).wait_recv()
        total[r] = kept[r, x] + core_in[r, x].astype(jnp.float32)
        x_out[r] = (kept[r, 1 - x] + core_in[r, 1 - x].astype(jnp.float32)).astype(x_out.dtype)
        reduce_x(r).start()

    if rows > 1:
        pass_on(nth_row(1))
    own.wait()

    def expert_step(s, carry):
        @pl.when(s + 2 < rows)
        def _():
            pass_on(nth_row(s + 2))

        r = nth_row(s)
        gather_x(r).wait_recv()
        gather_core(r, 1, place(r, 1 - x, core)).start()

        @pl.when(s == 0)
        def _():
            for copy in weight_copies():
                copy.wait()

        gather_core(r, 0).wait_recv()
        gather_core(r, 1).wait_recv()

        if rows > 1:

            @pl.when(s == last)
            def _():
                cross(z)

        chosen = jnp.where(
            meta[r, :top] == expert.astype(jnp.float32), meta[r, top:], 0.0
        )
        weight = jnp.sum(jnp.transpose(chosen), axis=1, keepdims=True)
        block = acts[r]
        gate_val = jnp.dot(block, gate_w[...], preferred_element_type=jnp.float32)
        up_val = jnp.dot(block, up_w[...], preferred_element_type=jnp.float32)
        hidden = (gate_val / (1.0 + jnp.exp(-gate_val)) * up_val * weight).astype(jnp.bfloat16)
        for x_of in range(PAIR):
            core_out[r, x_of] = jnp.dot(
                hidden, down_w[:, column(x_of, 1 - core)], preferred_element_type=jnp.float32
            ).astype(core_out.dtype)
        reduce_core(r).start()
        for x_of in range(PAIR):
            kept[r, x_of] = jnp.dot(
                hidden, down_w[:, column(x_of, core)], preferred_element_type=jnp.float32
            )
        return carry

    lax.fori_loop(0, rows, expert_step, 0)

    if rows == 1:
        cross(z)

    def cross_step(t, carry):
        cross(nth_row(last - t))
        return carry

    lax.fori_loop(0, last, cross_step, 0)

    def line_step(t, carry):
        r = nth_row(last - t)
        reduce_x(r).wait_recv()
        total[r] += x_in[r].astype(jnp.float32)

        @pl.when((r < z) & (z < last))
        def _():
            reduce_z(r, 0).wait_recv()
            total[r] += z_in[0, r].astype(jnp.float32)

        @pl.when((r > z) & (z > 0))
        def _():
            reduce_z(r, 1).wait_recv()
            total[r] += z_in[1, r].astype(jnp.float32)

        z_out[r] = total[r].astype(z_out.dtype)

        @pl.when(r < z)
        def _():
            reduce_z(r, 0).start()

        @pl.when(r > z)
        def _():
            reduce_z(r, 1).start()

        return carry

    lax.fori_loop(0, last, line_step, 0)
    reduce_x(z).wait_recv()
    total[z] += x_in[z].astype(jnp.float32)

    @pl.when(z < last)
    def _():
        reduce_z(z, 0).wait_recv()
        total[z] += z_in[0, z].astype(jnp.float32)

    @pl.when(z > 0)
    def _():
        reduce_z(z, 1).wait_recv()
        total[z] += z_in[1, z].astype(jnp.float32)

    out_ref[...] = total[z].astype(out_ref.dtype)

    def drain(r, carry):
        gather_x(r).wait_send()
        gather_core(r, 0).wait_send()
        gather_core(r, 1).wait_send()
        reduce_core(r).wait_send()
        reduce_x(r).wait_send()

        @pl.when(r != z)
        def _():
            reduce_z(r, 0).wait_send()

        @pl.when((r >= z) & (z > 0))
        def _():
            gather_meta(r, 0).wait_send()
            gather_z(r, 0).wait_send()

        @pl.when((r <= z) & (z < last))
        def _():
            gather_meta(r, 1).wait_send()
            gather_z(r, 1).wait_send()

        return carry

    lax.fori_loop(0, rows, drain, 0)


def dense_layer(activations, expert_ids, gate_scores, gate_proj, up_proj, down_proj):
    rows = lax.axis_size("row")
    group_rows, width = activations.shape
    model, hidden = gate_proj.shape[1:]
    top = expert_ids.shape[1]
    dtype = activations.dtype
    vmem = pl.BlockSpec(memory_space=pltpu.VMEM)
    anywhere = pl.BlockSpec(memory_space=pl.ANY)
    dma = pltpu.SemaphoreType.DMA
    flops = 6 * rows * group_rows * model * hidden
    return pl.pallas_call(
        functools.partial(dense_kernel, rows),
        out_shape=jax.ShapeDtypeStruct((group_rows, width), dtype),
        in_specs=[anywhere, vmem, vmem, anywhere, anywhere, anywhere],
        out_specs=vmem,
        scratch_shapes=[
            pltpu.VMEM((rows, group_rows, model), dtype),
            pltpu.VMEM((rows, 2 * top, group_rows), jnp.float32),
            pltpu.VMEM((model, hidden), dtype),
            pltpu.VMEM((model, hidden), dtype),
            pltpu.VMEM((hidden, model), dtype),
            pltpu.VMEM((rows, PAIR, group_rows, width), jnp.float32),
            pltpu.VMEM((rows, PAIR, group_rows, width), dtype),
            pltpu.VMEM((rows, PAIR, group_rows, width), dtype),
            pltpu.VMEM((rows, group_rows, width), jnp.float32),
            pltpu.VMEM((rows, group_rows, width), dtype),
            pltpu.VMEM((rows, group_rows, width), dtype),
            pltpu.VMEM((rows, group_rows, width), dtype),
            pltpu.VMEM((PAIR, rows, group_rows, width), dtype),
            dma((3,)),
            dma(()),
            dma((2, rows)),
            dma((rows,)),
            dma((2, rows)),
            dma((rows,)),
            dma((rows,)),
            dma((rows,)),
            dma((rows, 2)),
            dma((rows, 2)),
            dma((rows,)),
            dma((rows,)),
            dma((rows,)),
            dma((rows,)),
            dma((rows,)),
            dma((2, rows)),
        ],
        compiler_params=pltpu.CompilerParams(
            collective_id=0, has_side_effects=True, vmem_limit_bytes=48 * 1024 * 1024
        ),
        cost_estimate=pl.CostEstimate(
            flops=flops, bytes_accessed=6 * model * hidden, transcendentals=rows * group_rows * hidden
        ),
    )(activations, expert_ids.T, gate_scores.T, gate_proj, up_proj, down_proj)


def either_way(*arrays):
    activations, expert_ids = arrays[:2]
    col_count, sub_count = lax.axis_size("col"), lax.axis_size("sub")
    experts = lax.axis_size("row") * col_count
    block_rows = expert_ids.shape[0] // (col_count * sub_count)
    every_row = 2 * block_rows * TOP // experts >= block_rows
    if every_row and sub_count == 1 and col_count == PAIR * PAIR:
        return dense_layer(*arrays)
    return per_device(*arrays)


def solution(mesh):
    placed = (
        P(("parts", "row"), ("col", "sub")),
        P(("parts", "row"), None),
        P(("parts", "row"), None),
        P(("row", "col"), None, "sub"),
        P(("row", "col"), None, "sub"),
        P(("row", "col"), "sub", None),
    )
    return jax.shard_map(
        either_way,
        mesh=mesh,
        in_specs=placed,
        out_specs=P(("parts", "row"), ("col", "sub")),
        check_vma=False,
    )
```

```python
import functools

import jax
import jax.numpy as jnp
from jax import lax
from jax.experimental import pallas as pl
from jax.experimental.pallas import tpu as pltpu
from jax.sharding import PartitionSpec as P

TOP = 8
PAIR = 2
CHUNKS = 2
MESH = pl.DeviceIdType.MESH


def slot_places(chosen, experts, capacity):
    count = chosen.shape[0] * chosen.shape[1]
    flat_ids = chosen.reshape(count)
    onehot = (flat_ids[:, None] == jnp.arange(experts, dtype=jnp.int32)[None, :]).astype(jnp.int32)
    running = jnp.cumsum(onehot, axis=0) - 1
    ranking = jnp.sum(onehot * running, axis=1)
    return flat_ids * capacity + ranking


def fill_slots(row_block, places, experts, capacity, top_count):
    owners = jnp.full((experts * capacity,), row_block.shape[0], jnp.int32)
    owners = owners.at[places].set(jnp.arange(places.shape[0], dtype=jnp.int32) // top_count)
    padded = jnp.concatenate(
        [row_block, jnp.zeros((1, row_block.shape[1]), row_block.dtype)], axis=0
    )
    return padded[owners].reshape(experts, capacity, row_block.shape[1])


def run_expert(stacked, gate_proj, up_proj, down_proj):
    layout = stacked.shape
    inputs = stacked.reshape(-1, layout[-1])
    gate_val = jnp.dot(inputs, gate_proj[0], preferred_element_type=jnp.float32)
    up_val = jnp.dot(inputs, up_proj[0], preferred_element_type=jnp.float32)
    hidden = (jax.nn.silu(gate_val) * up_val).astype(jnp.bfloat16)
    partial_out = jnp.dot(hidden, down_proj[0], preferred_element_type=jnp.float32)
    return partial_out.reshape(layout)


def send_back(stacked, gate_proj, up_proj, down_proj):
    partial_out = run_expert(stacked, gate_proj, up_proj, down_proj)
    landed = lax.all_to_all(partial_out, ("row", "col"), split_axis=1, concat_axis=1, tiled=True)
    return lax.psum_scatter(landed, "sub", scatter_dimension=0, tiled=True).astype(jnp.bfloat16)


def per_device(activations, expert_ids, gate_scores, gate_proj, up_proj, down_proj):
    col_count = lax.axis_size("col")
    sub_count = lax.axis_size("sub")
    experts = lax.axis_size("row") * col_count
    group_rows = expert_ids.shape[0]
    block_rows = group_rows // (col_count * sub_count)
    capacity = max(2, min(block_rows, 2 * block_rows * TOP // experts))
    quarter = sub_count * block_rows
    width = activations.shape[1] * col_count * sub_count
    whole = lax.all_gather(activations, ("col", "sub"), axis=1, tiled=True)
    col_start = lax.axis_index("col") * quarter
    sub_index = lax.axis_index("sub")
    my_rows = lax.dynamic_slice_in_dim(whole, col_start, quarter, 0)
    my_ids = lax.dynamic_slice_in_dim(expert_ids, col_start, quarter, 0)
    own_scores = lax.dynamic_slice_in_dim(
        gate_scores, col_start + sub_index * block_rows, block_rows, 0
    )
    places = []
    for member in range(sub_count):
        lower = member * block_rows
        places.append(slot_places(my_ids[lower : lower + block_rows], experts, capacity))
    own_places = lax.dynamic_index_in_dim(jnp.stack(places), sub_index, 0, keepdims=False)
    buffers = []
    for member in range(sub_count):
        lower = member * block_rows
        buffers.append(
            fill_slots(my_rows[lower : lower + block_rows], places[member], experts, capacity, TOP)
        )
    outgoing = jnp.stack(buffers)
    returned = send_back(
        lax.all_to_all(outgoing, ("row", "col"), split_axis=1, concat_axis=1, tiled=True),
        gate_proj,
        up_proj,
        down_proj,
    )
    picked = returned.reshape(-1, width)[own_places].reshape(block_rows, TOP, width)
    share = jnp.sum(own_scores[:, :, None] * picked.astype(jnp.float32), axis=1)
    return lax.all_to_all(
        share.astype(jnp.bfloat16), ("col", "sub"), split_axis=1, concat_axis=0, tiled=True
    )


def dense_kernel(
    rows,
    acts_hbm,
    ids_hbm,
    scores_hbm,
    gate_hbm,
    up_hbm,
    down_hbm,
    out_ref,
    acts,
    ids,
    meta,
    gate_w,
    up_w,
    down_w,
    kept,
    core_out,
    core_in,
    total,
    x_out,
    x_in,
    z_out,
    z_in,
    weight_sem,
    own_sem,
    ag_z_send,
    ag_z_recv,
    meta_send,
    meta_recv,
    ag_x_send,
    ag_x_recv,
    ag_core_send,
    ag_core_recv,
    rs_core_send,
    rs_core_recv,
    rs_x_send,
    rs_x_recv,
    rs_z_send,
    rs_z_recv,
):
    top, group_rows = ids_hbm.shape
    part = group_rows // CHUNKS
    width = acts_hbm.shape[1]
    z = lax.axis_index("row")
    col = lax.axis_index("col")
    x, core = col // PAIR, col % PAIR
    expert = z * lax.axis_size("col") + col
    sibling = {"col": x * PAIR + (1 - core)}
    across = {"col": (1 - x) * PAIR + core}
    last = rows - 1

    def column(x_of, core_of):
        return pl.ds(pl.multiple_of((x_of * PAIR + core_of) * width, width), width)

    def nth_row(s):
        both = jnp.minimum(z, last - z)
        ahead = jnp.where(z <= last - z, 1, -1)
        near = z + ahead * jnp.where(s % 2 == 1, (s + 1) // 2, -(s // 2))
        rest = jnp.where(z <= last - z, s, last - s)
        return jnp.where(s <= 2 * both, near, rest)

    def remote(src, dst, send, recv, device):
        return pltpu.make_async_remote_copy(
            src_ref=src, dst_ref=dst, send_sem=send, recv_sem=recv, device_id=device, device_id_type=MESH
        )

    def tokens(q):
        return pl.ds(q * part, part)

    def place(r, q, x_of, core_of):
        return acts.at[r, tokens(q), column(x_of, core_of)]

    def chunk_of(q):
        return acts_hbm.at[tokens(q)]

    def gather_z(r, q, side, src=None):
        there = place(r, q, x, core)
        return remote(
            there if src is None else src,
            there,
            ag_z_send.at[side, r, q],
            ag_z_recv.at[r, q],
            {"row": z + 2 * side - 1},
        )

    def gather_meta(r, side):
        return remote(
            meta.at[r], meta.at[r], meta_send.at[side, r], meta_recv.at[r], {"row": z + 2 * side - 1}
        )

    def gather_x(r, q, src=None):
        there = place(r, q, x, core)
        return remote(there if src is None else src, there, ag_x_send.at[r, q], ag_x_recv.at[r, q], across)

    def gather_core(r, q, which, src=None):
        there = place(r, q, x if which == 0 else 1 - x, core)
        return remote(
            there if src is None else src,
            there,
            ag_core_send.at[r, which, q],
            ag_core_recv.at[r, which, q],
            sibling,
        )

    def reduce_core(r):
        return remote(core_out.at[r], core_in.at[r], rs_core_send.at[r], rs_core_recv.at[r], sibling)

    def reduce_x(r, q):
        return remote(
            x_out.at[r, tokens(q)], x_in.at[r, tokens(q)], rs_x_send.at[r, q], rs_x_recv.at[r, q], across
        )

    def reduce_z(r, q, side):
        return remote(
            z_out.at[r, tokens(q)],
            z_in.at[side, r, tokens(q)],
            rs_z_send.at[r, q],
            rs_z_recv.at[side, r, q],
            {"row": z + 2 * side - 1},
        )

    def weight_copies():
        return [
            pltpu.make_async_copy(src.at[0], dst, weight_sem.at[i])
            for i, (src, dst) in enumerate(((gate_hbm, gate_w), (up_hbm, up_w), (down_hbm, down_w)))
        ]

    own = pltpu.make_async_copy(acts_hbm, acts.at[z, :, column(x, core)], own_sem.at[0])
    own_ids = pltpu.make_async_copy(ids_hbm, ids, own_sem.at[1])
    own_scores = pltpu.make_async_copy(scores_hbm, meta.at[z, pl.ds(top, top)], own_sem.at[2])
    for copy in (own, own_ids, own_scores):
        copy.start()

    barrier = pltpu.get_barrier_semaphore()
    pl.semaphore_signal(barrier, inc=1, device_id=sibling, device_id_type=MESH)
    pl.semaphore_signal(barrier, inc=1, device_id=across, device_id_type=MESH)

    @pl.when(z > 0)
    def _():
        pl.semaphore_signal(barrier, inc=1, device_id={"row": z - 1}, device_id_type=MESH)

    @pl.when(z < last)
    def _():
        pl.semaphore_signal(barrier, inc=1, device_id={"row": z + 1}, device_id_type=MESH)

    pl.semaphore_wait(barrier, 2 + jnp.where(z > 0, 1, 0) + jnp.where(z < last, 1, 0))

    for q in range(CHUNKS):
        gather_x(z, q, chunk_of(q)).start()

        @pl.when(z > 0)
        def _():
            gather_z(z, q, 0, chunk_of(q)).start()

        @pl.when(z < last)
        def _():
            gather_z(z, q, 1, chunk_of(q)).start()

    for q in range(CHUNKS):
        gather_core(z, q, 0, chunk_of(q)).start()
    for copy in weight_copies():
        copy.start()
    own_ids.wait()
    own_scores.wait()
    meta[z, :top] = ids[...].astype(jnp.float32)

    @pl.when(z > 0)
    def _():
        gather_meta(z, 0).start()

    @pl.when(z < last)
    def _():
        gather_meta(z, 1).start()

    own.wait()

    def pass_on(r, q, side, more):
        gather_z(r, q, side).wait_recv()

        @pl.when(more)
        def _():
            gather_z(r, q, side).start()

        gather_x(r, q).start()
        gather_core(r, q, 0).start()

    def pass_meta(r, side, more):
        gather_meta(r, side).wait_recv()

        @pl.when(more)
        def _():
            gather_meta(r, side).start()

    def cross(r):
        reduce_core(r).wait_recv()
        for q in range(CHUNKS):
            here = tokens(q)
            given = kept[r, 1 - x, here] + core_in[r, 1 - x, here].astype(jnp.float32)
            x_out[r, here] = given.astype(x_out.dtype)
            reduce_x(r, q).start()
        total[r] = kept[r, x] + core_in[r, x].astype(jnp.float32)

    def expert_step(s, carry):
        below, above = z - 1 - s, z + 1 + s
        for q in range(CHUNKS):

            @pl.when(below >= 0)
            def _():
                pass_on(below, q, 1, z < last)

            @pl.when(above <= last)
            def _():
                pass_on(above, q, 0, z > 0)

        @pl.when(below >= 0)
        def _():
            pass_meta(below, 1, z < last)

        @pl.when(above <= last)
        def _():
            pass_meta(above, 0, z > 0)

        r = nth_row(s)
        for q in range(CHUNKS):
            gather_x(r, q).wait_recv()
            gather_core(r, q, 1, place(r, q, 1 - x, core)).start()

        @pl.when(s == 0)
        def _():
            for copy in weight_copies():
                copy.wait()

        for q in range(CHUNKS):
            gather_core(r, q, 0).wait_recv()
            gather_core(r, q, 1).wait_recv()

        if rows > 1:

            @pl.when(s == last)
            def _():
                cross(z)

        chosen = jnp.where(meta[r, :top] == expert.astype(jnp.float32), meta[r, top:], 0.0)
        weight = jnp.sum(jnp.transpose(chosen), axis=1, keepdims=True)
        block = acts[r]
        gate_val = jnp.dot(block, gate_w[...], preferred_element_type=jnp.float32)
        up_val = jnp.dot(block, up_w[...], preferred_element_type=jnp.float32)
        hidden = (gate_val / (1.0 + jnp.exp(-gate_val)) * up_val).astype(jnp.bfloat16)

        def weighted(x_of, core_of):
            product = jnp.dot(hidden, down_w[:, column(x_of, core_of)], preferred_element_type=jnp.float32)
            return product * weight

        for x_of in range(PAIR):
            core_out[r, x_of] = weighted(x_of, 1 - core).astype(core_out.dtype)
        reduce_core(r).start()
        for x_of in range(PAIR):
            kept[r, x_of] = weighted(x_of, core)
        return carry

    lax.fori_loop(0, rows, expert_step, 0)

    if rows == 1:
        cross(z)

    def cross_step(t, carry):
        cross(nth_row(last - t))
        return carry

    lax.fori_loop(0, last, cross_step, 0)

    def line_step(t, carry):
        r = nth_row(last - t)
        for q in range(CHUNKS):
            here = tokens(q)
            reduce_x(r, q).wait_recv()
            total[r, here] += x_in[r, here].astype(jnp.float32)

            @pl.when((r < z) & (z < last))
            def _():
                reduce_z(r, q, 0).wait_recv()
                total[r, here] += z_in[0, r, here].astype(jnp.float32)

            @pl.when((r > z) & (z > 0))
            def _():
                reduce_z(r, q, 1).wait_recv()
                total[r, here] += z_in[1, r, here].astype(jnp.float32)

            z_out[r, here] = total[r, here].astype(z_out.dtype)

            @pl.when(r < z)
            def _():
                reduce_z(r, q, 0).start()

            @pl.when(r > z)
            def _():
                reduce_z(r, q, 1).start()

        return carry

    lax.fori_loop(0, last, line_step, 0)
    for q in range(CHUNKS):
        here = tokens(q)
        reduce_x(z, q).wait_recv()
        total[z, here] += x_in[z, here].astype(jnp.float32)

        @pl.when(z < last)
        def _():
            reduce_z(z, q, 0).wait_recv()
            total[z, here] += z_in[0, z, here].astype(jnp.float32)

        @pl.when(z > 0)
        def _():
            reduce_z(z, q, 1).wait_recv()
            total[z, here] += z_in[1, z, here].astype(jnp.float32)

        out_ref[here] = total[z, here].astype(out_ref.dtype)

    def drain(r, carry):
        reduce_core(r).wait_send()
        for q in range(CHUNKS):
            gather_x(r, q).wait_send()
            gather_core(r, q, 0).wait_send()
            gather_core(r, q, 1).wait_send()
            reduce_x(r, q).wait_send()

            @pl.when(r != z)
            def _():
                reduce_z(r, q, 0).wait_send()

        for side, sent in ((0, (r >= z) & (z > 0)), (1, (r <= z) & (z < last))):

            @pl.when(sent)
            def _():
                gather_meta(r, side).wait_send()
                for q in range(CHUNKS):
                    gather_z(r, q, side).wait_send()

        return carry

    lax.fori_loop(0, rows, drain, 0)


def dense_layer(activations, expert_ids, gate_scores, gate_proj, up_proj, down_proj):
    rows = lax.axis_size("row")
    group_rows, width = activations.shape
    model, hidden = gate_proj.shape[1:]
    top = expert_ids.shape[1]
    dtype = activations.dtype
    vmem = pl.BlockSpec(memory_space=pltpu.VMEM)
    anywhere = pl.BlockSpec(memory_space=pl.ANY)
    dma = pltpu.SemaphoreType.DMA
    flops = 6 * rows * group_rows * model * hidden
    return pl.pallas_call(
        functools.partial(dense_kernel, rows),
        out_shape=jax.ShapeDtypeStruct((group_rows, width), dtype),
        in_specs=[anywhere] * 6,
        out_specs=vmem,
        scratch_shapes=[
            pltpu.VMEM((rows, group_rows, model), dtype),
            pltpu.VMEM((top, group_rows), jnp.int32),
            pltpu.VMEM((rows, 2 * top, group_rows), jnp.float32),
            pltpu.VMEM((model, hidden), dtype),
            pltpu.VMEM((model, hidden), dtype),
            pltpu.VMEM((hidden, model), dtype),
            pltpu.VMEM((rows, PAIR, group_rows, width), jnp.float32),
            pltpu.VMEM((rows, PAIR, group_rows, width), dtype),
            pltpu.VMEM((rows, PAIR, group_rows, width), dtype),
            pltpu.VMEM((rows, group_rows, width), jnp.float32),
            pltpu.VMEM((rows, group_rows, width), dtype),
            pltpu.VMEM((rows, group_rows, width), dtype),
            pltpu.VMEM((rows, group_rows, width), dtype),
            pltpu.VMEM((PAIR, rows, group_rows, width), dtype),
            dma((3,)),
            dma((3,)),
            dma((2, rows, CHUNKS)),
            dma((rows, CHUNKS)),
            dma((2, rows)),
            dma((rows,)),
            dma((rows, CHUNKS)),
            dma((rows, CHUNKS)),
            dma((rows, 2, CHUNKS)),
            dma((rows, 2, CHUNKS)),
            dma((rows,)),
            dma((rows,)),
            dma((rows, CHUNKS)),
            dma((rows, CHUNKS)),
            dma((rows, CHUNKS)),
            dma((2, rows, CHUNKS)),
        ],
        compiler_params=pltpu.CompilerParams(
            collective_id=0, has_side_effects=True, vmem_limit_bytes=64 * 1024 * 1024
        ),
        cost_estimate=pl.CostEstimate(
            flops=flops, bytes_accessed=6 * model * hidden, transcendentals=rows * group_rows * hidden
        ),
    )(activations, expert_ids.T, gate_scores.T, gate_proj, up_proj, down_proj)


def either_way(*arrays):
    activations, expert_ids = arrays[:2]
    col_count, sub_count = lax.axis_size("col"), lax.axis_size("sub")
    experts = lax.axis_size("row") * col_count
    block_rows = expert_ids.shape[0] // (col_count * sub_count)
    every_row = 2 * block_rows * TOP // experts >= block_rows
    if every_row and sub_count == 1 and col_count == PAIR * PAIR:
        return dense_layer(*arrays)
    return per_device(*arrays)


def solution(mesh):
    placed = (
        P(("parts", "row"), ("col", "sub")),
        P(("parts", "row"), None),
        P(("parts", "row"), None),
        P(("row", "col"), None, "sub"),
        P(("row", "col"), None, "sub"),
        P(("row", "col"), "sub", None),
    )
    return jax.shard_map(
        either_way,
        mesh=mesh,
        in_specs=placed,
        out_specs=P(("parts", "row"), ("col", "sub")),
        check_vma=False,
    )
```

```python
import functools

import jax
import jax.numpy as jnp
from jax import lax
from jax.experimental import pallas as pl
from jax.experimental.pallas import tpu as pltpu
from jax.sharding import PartitionSpec as P

TOP = 8
PAIR = 2
CHUNKS = 2
MESH = pl.DeviceIdType.MESH


def slot_places(chosen, experts, capacity):
    count = chosen.shape[0] * chosen.shape[1]
    flat_ids = chosen.reshape(count)
    onehot = (flat_ids[:, None] == jnp.arange(experts, dtype=jnp.int32)[None, :]).astype(jnp.int32)
    running = jnp.cumsum(onehot, axis=0) - 1
    ranking = jnp.sum(onehot * running, axis=1)
    return flat_ids * capacity + ranking


def fill_slots(row_block, places, experts, capacity, top_count):
    owners = jnp.full((experts * capacity,), row_block.shape[0], jnp.int32)
    owners = owners.at[places].set(jnp.arange(places.shape[0], dtype=jnp.int32) // top_count)
    padded = jnp.concatenate(
        [row_block, jnp.zeros((1, row_block.shape[1]), row_block.dtype)], axis=0
    )
    return padded[owners].reshape(experts, capacity, row_block.shape[1])


def run_expert(stacked, gate_proj, up_proj, down_proj):
    layout = stacked.shape
    inputs = stacked.reshape(-1, layout[-1])
    gate_val = jnp.dot(inputs, gate_proj[0], preferred_element_type=jnp.float32)
    up_val = jnp.dot(inputs, up_proj[0], preferred_element_type=jnp.float32)
    hidden = (jax.nn.silu(gate_val) * up_val).astype(jnp.bfloat16)
    partial_out = jnp.dot(hidden, down_proj[0], preferred_element_type=jnp.float32)
    return partial_out.reshape(layout)


def send_back(stacked, gate_proj, up_proj, down_proj):
    partial_out = run_expert(stacked, gate_proj, up_proj, down_proj)
    landed = lax.all_to_all(partial_out, ("row", "col"), split_axis=1, concat_axis=1, tiled=True)
    return lax.psum_scatter(landed, "sub", scatter_dimension=0, tiled=True).astype(jnp.bfloat16)


def per_device(activations, expert_ids, gate_scores, gate_proj, up_proj, down_proj):
    col_count = lax.axis_size("col")
    sub_count = lax.axis_size("sub")
    experts = lax.axis_size("row") * col_count
    group_rows = expert_ids.shape[0]
    block_rows = group_rows // (col_count * sub_count)
    capacity = max(2, min(block_rows, 2 * block_rows * TOP // experts))
    quarter = sub_count * block_rows
    width = activations.shape[1] * col_count * sub_count
    whole = lax.all_gather(activations, ("col", "sub"), axis=1, tiled=True)
    col_start = lax.axis_index("col") * quarter
    sub_index = lax.axis_index("sub")
    my_rows = lax.dynamic_slice_in_dim(whole, col_start, quarter, 0)
    my_ids = lax.dynamic_slice_in_dim(expert_ids, col_start, quarter, 0)
    own_scores = lax.dynamic_slice_in_dim(
        gate_scores, col_start + sub_index * block_rows, block_rows, 0
    )
    places = []
    for member in range(sub_count):
        lower = member * block_rows
        places.append(slot_places(my_ids[lower : lower + block_rows], experts, capacity))
    own_places = lax.dynamic_index_in_dim(jnp.stack(places), sub_index, 0, keepdims=False)
    buffers = []
    for member in range(sub_count):
        lower = member * block_rows
        buffers.append(
            fill_slots(my_rows[lower : lower + block_rows], places[member], experts, capacity, TOP)
        )
    outgoing = jnp.stack(buffers)
    returned = send_back(
        lax.all_to_all(outgoing, ("row", "col"), split_axis=1, concat_axis=1, tiled=True),
        gate_proj,
        up_proj,
        down_proj,
    )
    picked = returned.reshape(-1, width)[own_places].reshape(block_rows, TOP, width)
    share = jnp.sum(own_scores[:, :, None] * picked.astype(jnp.float32), axis=1)
    return lax.all_to_all(
        share.astype(jnp.bfloat16), ("col", "sub"), split_axis=1, concat_axis=0, tiled=True
    )


def dense_kernel(
    rows,
    acts_hbm,
    ids_hbm,
    scores_hbm,
    gate_hbm,
    up_hbm,
    down_hbm,
    out_ref,
    acts,
    ids,
    meta,
    gate_w,
    up_w,
    down_w,
    gate_sum,
    up_sum,
    kept,
    core_out,
    core_in,
    total,
    x_out,
    x_in,
    z_out,
    z_in,
    weight_sem,
    own_sem,
    ag_z_send,
    ag_z_recv,
    meta_send,
    meta_recv,
    ag_x_send,
    ag_x_recv,
    ag_core_send,
    ag_core_recv,
    rs_core_send,
    rs_core_recv,
    rs_x_send,
    rs_x_recv,
    rs_z_send,
    rs_z_recv,
):
    top, group_rows = ids_hbm.shape
    part = group_rows // CHUNKS
    width = acts_hbm.shape[1]
    z = lax.axis_index("row")
    col = lax.axis_index("col")
    x, core = col // PAIR, col % PAIR
    expert = z * lax.axis_size("col") + col
    sibling = {"col": x * PAIR + (1 - core)}
    across = {"col": (1 - x) * PAIR + core}
    last = rows - 1

    def column(x_of, core_of):
        return pl.ds(pl.multiple_of((x_of * PAIR + core_of) * width, width), width)

    def nth_row(s):
        both = jnp.minimum(z, last - z)
        ahead = jnp.where(z <= last - z, 1, -1)
        near = z + ahead * jnp.where(s % 2 == 1, (s + 1) // 2, -(s // 2))
        rest = jnp.where(z <= last - z, s, last - s)
        return jnp.where(s <= 2 * both, near, rest)

    def remote(src, dst, send, recv, device):
        return pltpu.make_async_remote_copy(
            src_ref=src, dst_ref=dst, send_sem=send, recv_sem=recv, device_id=device, device_id_type=MESH
        )

    def tokens(q):
        return pl.ds(q * part, part)

    def place(r, q, x_of, core_of):
        return acts.at[r, tokens(q), column(x_of, core_of)]

    def chunk_of(q):
        return acts_hbm.at[tokens(q)]

    def gather_z(r, q, side, src=None):
        there = place(r, q, x, core)
        return remote(
            there if src is None else src,
            there,
            ag_z_send.at[side, r, q],
            ag_z_recv.at[r, q],
            {"row": z + 2 * side - 1},
        )

    def gather_meta(r, side):
        return remote(
            meta.at[r], meta.at[r], meta_send.at[side, r], meta_recv.at[r], {"row": z + 2 * side - 1}
        )

    def gather_x(r, q, src=None):
        there = place(r, q, x, core)
        return remote(there if src is None else src, there, ag_x_send.at[r, q], ag_x_recv.at[r, q], across)

    def gather_core(r, q, which, src=None):
        there = place(r, q, x if which == 0 else 1 - x, core)
        return remote(
            there if src is None else src,
            there,
            ag_core_send.at[r, which, q],
            ag_core_recv.at[r, which, q],
            sibling,
        )

    def reduce_core(r, which):
        x_of = 1 - x if which == 0 else x
        return remote(
            core_out.at[r, x_of],
            core_in.at[r, x_of],
            rs_core_send.at[r, which],
            rs_core_recv.at[r, which],
            sibling,
        )

    def reduce_x(r, q):
        return remote(
            x_out.at[r, tokens(q)], x_in.at[r, tokens(q)], rs_x_send.at[r, q], rs_x_recv.at[r, q], across
        )

    def reduce_z(r, q, side):
        return remote(
            z_out.at[r, tokens(q)],
            z_in.at[side, r, tokens(q)],
            rs_z_send.at[r, q],
            rs_z_recv.at[side, r, q],
            {"row": z + 2 * side - 1},
        )

    weights = [
        pltpu.make_async_copy(src.at[0], dst, weight_sem.at[i])
        for i, (src, dst) in enumerate(((gate_hbm, gate_w), (up_hbm, up_w), (down_hbm, down_w)))
    ]

    own = pltpu.make_async_copy(acts_hbm, acts.at[z, :, column(x, core)], own_sem.at[0])
    own_ids = pltpu.make_async_copy(ids_hbm, ids, own_sem.at[1])
    own_scores = pltpu.make_async_copy(scores_hbm, meta.at[z, pl.ds(top, top)], own_sem.at[2])
    for copy in [own, own_ids, own_scores] + weights:
        copy.start()

    barrier = pltpu.get_barrier_semaphore()
    pl.semaphore_signal(barrier, inc=1, device_id=sibling, device_id_type=MESH)
    pl.semaphore_signal(barrier, inc=1, device_id=across, device_id_type=MESH)

    @pl.when(z > 0)
    def _():
        pl.semaphore_signal(barrier, inc=1, device_id={"row": z - 1}, device_id_type=MESH)

    @pl.when(z < last)
    def _():
        pl.semaphore_signal(barrier, inc=1, device_id={"row": z + 1}, device_id_type=MESH)

    pl.semaphore_wait(barrier, 2 + jnp.where(z > 0, 1, 0) + jnp.where(z < last, 1, 0))

    for q in range(CHUNKS):
        gather_x(z, q, chunk_of(q)).start()

        @pl.when(z > 0)
        def _():
            gather_z(z, q, 0, chunk_of(q)).start()

        @pl.when(z < last)
        def _():
            gather_z(z, q, 1, chunk_of(q)).start()

    for q in range(CHUNKS):
        gather_core(z, q, 0, chunk_of(q)).start()
    own_ids.wait()
    own_scores.wait()
    meta[z, :top] = ids[...].astype(jnp.float32)

    @pl.when(z > 0)
    def _():
        gather_meta(z, 0).start()

    @pl.when(z < last)
    def _():
        gather_meta(z, 1).start()

    own.wait()

    def pass_on(r, q, side, more):
        gather_z(r, q, side).wait_recv()

        @pl.when(more)
        def _():
            gather_z(r, q, side).start()

        gather_x(r, q).start()
        gather_core(r, q, 0).start()

    def pass_meta(r, side, more):
        gather_meta(r, side).wait_recv()

        @pl.when(more)
        def _():
            gather_meta(r, side).start()

    def cross(r):
        reduce_core(r, 0).wait_recv()
        for q in range(CHUNKS):
            here = tokens(q)
            given = kept[r, 1 - x, here] + core_in[r, 1 - x, here].astype(jnp.float32)
            x_out[r, here] = given.astype(x_out.dtype)
            reduce_x(r, q).start()
        reduce_core(r, 1).wait_recv()
        total[r] = kept[r, x] + core_in[r, x].astype(jnp.float32)

    def product(r, x_of, core_of, table):
        features = column(x_of, core_of)
        return jnp.dot(acts[r, :, features], table[features, :], preferred_element_type=jnp.float32)

    def first_half(r):
        gate_sum[r] = product(r, x, core, gate_w)
        up_sum[r] = product(r, x, core, up_w)
        for q in range(CHUNKS):
            gather_core(r, q, 0).wait_recv()
        gate_sum[r] += product(r, x, 1 - core, gate_w)
        up_sum[r] += product(r, x, 1 - core, up_w)

    def second_half(r):
        gate_sum[r] += product(r, 1 - x, core, gate_w)
        up_sum[r] += product(r, 1 - x, core, up_w)
        for q in range(CHUNKS):
            gather_core(r, q, 1).wait_recv()
        gate_val = gate_sum[r] + product(r, 1 - x, 1 - core, gate_w)
        up_val = up_sum[r] + product(r, 1 - x, 1 - core, up_w)
        hidden = (gate_val / (1.0 + jnp.exp(-gate_val)) * up_val).astype(jnp.bfloat16)
        chosen = jnp.where(meta[r, :top] == expert.astype(jnp.float32), meta[r, top:], 0.0)
        weight = jnp.sum(jnp.transpose(chosen), axis=1, keepdims=True)

        def weighted(x_of, core_of):
            result = jnp.dot(hidden, down_w[:, column(x_of, core_of)], preferred_element_type=jnp.float32)
            return result * weight

        for which, x_of in enumerate((1 - x, x)):
            core_out[r, x_of] = weighted(x_of, 1 - core).astype(core_out.dtype)
            reduce_core(r, which).start()
        for x_of in (1 - x, x):
            kept[r, x_of] = weighted(x_of, core)

    def expert_step(s, carry):
        below, above = z - 1 - s, z + 1 + s
        from_below, from_above = below >= 0, above <= last
        for q in range(CHUNKS):

            @pl.when(from_below)
            def _():
                pass_on(below, q, 1, z < last)

            @pl.when(from_above)
            def _():
                pass_on(above, q, 0, z > 0)

        @pl.when(from_below)
        def _():
            pass_meta(below, 1, z < last)

        @pl.when(from_above)
        def _():
            pass_meta(above, 0, z > 0)

        r = nth_row(s)
        for q in range(CHUNKS):
            gather_x(r, q).wait_recv()
            gather_core(r, q, 1, place(r, q, 1 - x, core)).start()

        @pl.when(s == 0)
        def _():
            weights[2].wait()

        if rows > 1:

            @pl.when(s == last)
            def _():
                cross(z)

        second_half(r)

        @pl.when(s < last)
        def _():
            first_half(nth_row(s + 1))

        return carry

    for copy in weights[:2]:
        copy.wait()
    first_half(z)
    lax.fori_loop(0, rows, expert_step, 0)

    if rows == 1:
        cross(z)

    def cross_step(t, carry):
        cross(nth_row(last - t))
        return carry

    lax.fori_loop(0, last, cross_step, 0)

    def line_step(t, carry):
        r = nth_row(last - t)
        for q in range(CHUNKS):
            here = tokens(q)
            reduce_x(r, q).wait_recv()
            total[r, here] += x_in[r, here].astype(jnp.float32)

            @pl.when((r < z) & (z < last))
            def _():
                reduce_z(r, q, 0).wait_recv()
                total[r, here] += z_in[0, r, here].astype(jnp.float32)

            @pl.when((r > z) & (z > 0))
            def _():
                reduce_z(r, q, 1).wait_recv()
                total[r, here] += z_in[1, r, here].astype(jnp.float32)

            z_out[r, here] = total[r, here].astype(z_out.dtype)

            @pl.when(r < z)
            def _():
                reduce_z(r, q, 0).start()

            @pl.when(r > z)
            def _():
                reduce_z(r, q, 1).start()

        return carry

    lax.fori_loop(0, last, line_step, 0)
    for q in range(CHUNKS):
        here = tokens(q)
        reduce_x(z, q).wait_recv()
        total[z, here] += x_in[z, here].astype(jnp.float32)

        @pl.when(z < last)
        def _():
            reduce_z(z, q, 0).wait_recv()
            total[z, here] += z_in[0, z, here].astype(jnp.float32)

        @pl.when(z > 0)
        def _():
            reduce_z(z, q, 1).wait_recv()
            total[z, here] += z_in[1, z, here].astype(jnp.float32)

        out_ref[here] = total[z, here].astype(out_ref.dtype)

    def drain(r, carry):
        for which in range(2):
            reduce_core(r, which).wait_send()
        for q in range(CHUNKS):
            gather_x(r, q).wait_send()
            gather_core(r, q, 0).wait_send()
            gather_core(r, q, 1).wait_send()
            reduce_x(r, q).wait_send()

            @pl.when(r != z)
            def _():
                reduce_z(r, q, 0).wait_send()

        for side, sent in ((0, (r >= z) & (z > 0)), (1, (r <= z) & (z < last))):

            @pl.when(sent)
            def _():
                gather_meta(r, side).wait_send()
                for q in range(CHUNKS):
                    gather_z(r, q, side).wait_send()

        return carry

    lax.fori_loop(0, rows, drain, 0)


def dense_layer(activations, expert_ids, gate_scores, gate_proj, up_proj, down_proj):
    rows = lax.axis_size("row")
    group_rows, width = activations.shape
    model, hidden = gate_proj.shape[1:]
    top = expert_ids.shape[1]
    dtype = activations.dtype
    vmem = pl.BlockSpec(memory_space=pltpu.VMEM)
    hbm = pl.BlockSpec(memory_space=pltpu.HBM)
    dma = pltpu.SemaphoreType.DMA
    flops = 6 * rows * group_rows * model * hidden
    return pl.pallas_call(
        functools.partial(dense_kernel, rows),
        out_shape=jax.ShapeDtypeStruct((group_rows, width), dtype),
        in_specs=[hbm] * 6,
        out_specs=vmem,
        scratch_shapes=[
            pltpu.VMEM((rows, group_rows, model), dtype),
            pltpu.VMEM((top, group_rows), jnp.int32),
            pltpu.VMEM((rows, 2 * top, group_rows), jnp.float32),
            pltpu.VMEM((model, hidden), dtype),
            pltpu.VMEM((model, hidden), dtype),
            pltpu.VMEM((hidden, model), dtype),
            pltpu.VMEM((rows, group_rows, hidden), jnp.float32),
            pltpu.VMEM((rows, group_rows, hidden), jnp.float32),
            pltpu.VMEM((rows, PAIR, group_rows, width), jnp.float32),
            pltpu.VMEM((rows, PAIR, group_rows, width), dtype),
            pltpu.VMEM((rows, PAIR, group_rows, width), dtype),
            pltpu.VMEM((rows, group_rows, width), jnp.float32),
            pltpu.VMEM((rows, group_rows, width), dtype),
            pltpu.VMEM((rows, group_rows, width), dtype),
            pltpu.VMEM((rows, group_rows, width), dtype),
            pltpu.VMEM((PAIR, rows, group_rows, width), dtype),
            dma((3,)),
            dma((3,)),
            dma((2, rows, CHUNKS)),
            dma((rows, CHUNKS)),
            dma((2, rows)),
            dma((rows,)),
            dma((rows, CHUNKS)),
            dma((rows, CHUNKS)),
            dma((rows, 2, CHUNKS)),
            dma((rows, 2, CHUNKS)),
            dma((rows, 2)),
            dma((rows, 2)),
            dma((rows, CHUNKS)),
            dma((rows, CHUNKS)),
            dma((rows, CHUNKS)),
            dma((2, rows, CHUNKS)),
        ],
        compiler_params=pltpu.CompilerParams(
            collective_id=0, has_side_effects=True, vmem_limit_bytes=48 * 1024 * 1024
        ),
        cost_estimate=pl.CostEstimate(
            flops=flops, bytes_accessed=6 * model * hidden, transcendentals=rows * group_rows * hidden
        ),
    )(activations, expert_ids.T, gate_scores.T, gate_proj, up_proj, down_proj)


def either_way(*arrays):
    activations, expert_ids = arrays[:2]
    col_count, sub_count = lax.axis_size("col"), lax.axis_size("sub")
    experts = lax.axis_size("row") * col_count
    block_rows = expert_ids.shape[0] // (col_count * sub_count)
    every_row = 2 * block_rows * TOP // experts >= block_rows
    if every_row and sub_count == 1 and col_count == PAIR * PAIR:
        return dense_layer(*arrays)
    return per_device(*arrays)


def solution(mesh):
    placed = (
        P(("parts", "row"), ("col", "sub")),
        P(("parts", "row"), None),
        P(("parts", "row"), None),
        P(("row", "col"), None, "sub"),
        P(("row", "col"), None, "sub"),
        P(("row", "col"), "sub", None),
    )
    return jax.shard_map(
        either_way,
        mesh=mesh,
        in_specs=placed,
        out_specs=P(("parts", "row"), ("col", "sub")),
        check_vma=False,
    )
```

```python
import functools

import jax
import jax.numpy as jnp
from jax import lax
from jax.experimental import pallas as pl
from jax.experimental.pallas import tpu as pltpu
from jax.sharding import PartitionSpec as P

TOP = 8
PAIR = 2
CHUNKS = 2
MESH = pl.DeviceIdType.MESH


def slot_places(chosen, experts, capacity):
    count = chosen.shape[0] * chosen.shape[1]
    flat_ids = chosen.reshape(count)
    onehot = (flat_ids[:, None] == jnp.arange(experts, dtype=jnp.int32)[None, :]).astype(jnp.int32)
    running = jnp.cumsum(onehot, axis=0) - 1
    ranking = jnp.sum(onehot * running, axis=1)
    return flat_ids * capacity + ranking


def fill_slots(row_block, places, experts, capacity, top_count):
    owners = jnp.full((experts * capacity,), row_block.shape[0], jnp.int32)
    owners = owners.at[places].set(jnp.arange(places.shape[0], dtype=jnp.int32) // top_count)
    padded = jnp.concatenate(
        [row_block, jnp.zeros((1, row_block.shape[1]), row_block.dtype)], axis=0
    )
    return padded[owners].reshape(experts, capacity, row_block.shape[1])


def run_expert(stacked, gate_proj, up_proj, down_proj):
    layout = stacked.shape
    inputs = stacked.reshape(-1, layout[-1])
    gate_val = jnp.dot(inputs, gate_proj[0], preferred_element_type=jnp.float32)
    up_val = jnp.dot(inputs, up_proj[0], preferred_element_type=jnp.float32)
    hidden = (jax.nn.silu(gate_val) * up_val).astype(jnp.bfloat16)
    partial_out = jnp.dot(hidden, down_proj[0], preferred_element_type=jnp.float32)
    return partial_out.reshape(layout)


def send_back(stacked, gate_proj, up_proj, down_proj):
    partial_out = run_expert(stacked, gate_proj, up_proj, down_proj)
    landed = lax.all_to_all(partial_out, ("row", "col"), split_axis=1, concat_axis=1, tiled=True)
    return lax.psum_scatter(landed, "sub", scatter_dimension=0, tiled=True).astype(jnp.bfloat16)


def per_device(activations, expert_ids, gate_scores, gate_proj, up_proj, down_proj):
    col_count = lax.axis_size("col")
    sub_count = lax.axis_size("sub")
    experts = lax.axis_size("row") * col_count
    group_rows = expert_ids.shape[0]
    block_rows = group_rows // (col_count * sub_count)
    capacity = max(2, min(block_rows, 2 * block_rows * TOP // experts))
    quarter = sub_count * block_rows
    width = activations.shape[1] * col_count * sub_count
    whole = lax.all_gather(activations, ("col", "sub"), axis=1, tiled=True)
    col_start = lax.axis_index("col") * quarter
    sub_index = lax.axis_index("sub")
    my_rows = lax.dynamic_slice_in_dim(whole, col_start, quarter, 0)
    my_ids = lax.dynamic_slice_in_dim(expert_ids, col_start, quarter, 0)
    own_scores = lax.dynamic_slice_in_dim(
        gate_scores, col_start + sub_index * block_rows, block_rows, 0
    )
    places = []
    for member in range(sub_count):
        lower = member * block_rows
        places.append(slot_places(my_ids[lower : lower + block_rows], experts, capacity))
    own_places = lax.dynamic_index_in_dim(jnp.stack(places), sub_index, 0, keepdims=False)
    buffers = []
    for member in range(sub_count):
        lower = member * block_rows
        buffers.append(
            fill_slots(my_rows[lower : lower + block_rows], places[member], experts, capacity, TOP)
        )
    outgoing = jnp.stack(buffers)
    returned = send_back(
        lax.all_to_all(outgoing, ("row", "col"), split_axis=1, concat_axis=1, tiled=True),
        gate_proj,
        up_proj,
        down_proj,
    )
    picked = returned.reshape(-1, width)[own_places].reshape(block_rows, TOP, width)
    share = jnp.sum(own_scores[:, :, None] * picked.astype(jnp.float32), axis=1)
    return lax.all_to_all(
        share.astype(jnp.bfloat16), ("col", "sub"), split_axis=1, concat_axis=0, tiled=True
    )


def dense_kernel(
    rows,
    acts_hbm,
    ids_hbm,
    scores_hbm,
    gate_hbm,
    up_hbm,
    down_hbm,
    out_ref,
    acts,
    ids,
    meta,
    gate_w,
    up_w,
    down_w,
    gate_sum,
    up_sum,
    kept,
    core_out,
    core_in,
    total,
    x_out,
    x_in,
    z_out,
    z_in,
    weight_sem,
    own_sem,
    ag_z_send,
    ag_z_recv,
    meta_send,
    meta_recv,
    ag_x_send,
    ag_x_recv,
    ag_core_send,
    ag_core_recv,
    rs_core_send,
    rs_core_recv,
    rs_x_send,
    rs_x_recv,
    rs_z_send,
    rs_z_recv,
):
    top, group_rows = ids_hbm.shape
    part = group_rows // CHUNKS
    width = acts_hbm.shape[1]
    z = lax.axis_index("row")
    col = lax.axis_index("col")
    x, core = col // PAIR, col % PAIR
    expert = z * lax.axis_size("col") + col
    sibling = {"col": x * PAIR + (1 - core)}
    across = {"col": (1 - x) * PAIR + core}
    last = rows - 1

    def column(x_of, core_of):
        return pl.ds(pl.multiple_of((x_of * PAIR + core_of) * width, width), width)

    def nth_row(s):
        both = jnp.minimum(z, last - z)
        ahead = jnp.where(z <= last - z, 1, -1)
        near = z + ahead * jnp.where(s % 2 == 1, (s + 1) // 2, -(s // 2))
        rest = jnp.where(z <= last - z, s, last - s)
        return jnp.where(s <= 2 * both, near, rest)

    def remote(src, dst, send, recv, device):
        return pltpu.make_async_remote_copy(
            src_ref=src, dst_ref=dst, send_sem=send, recv_sem=recv, device_id=device, device_id_type=MESH
        )

    def tokens(q):
        return pl.ds(q * part, part)

    def place(r, q, x_of, core_of):
        return acts.at[r, tokens(q), column(x_of, core_of)]

    def chunk_of(q):
        return acts_hbm.at[tokens(q)]

    def gather_z(r, q, side, src=None):
        there = place(r, q, x, core)
        return remote(
            there if src is None else src,
            there,
            ag_z_send.at[side, r, q],
            ag_z_recv.at[r, q],
            {"row": z + 2 * side - 1},
        )

    def gather_meta(r, side):
        return remote(
            meta.at[r], meta.at[r], meta_send.at[side, r], meta_recv.at[r], {"row": z + 2 * side - 1}
        )

    def gather_x(r, q, src=None):
        there = place(r, q, x, core)
        return remote(there if src is None else src, there, ag_x_send.at[r, q], ag_x_recv.at[r, q], across)

    def gather_core(r, q, which, src=None):
        there = place(r, q, x if which == 0 else 1 - x, core)
        return remote(
            there if src is None else src,
            there,
            ag_core_send.at[r, which, q],
            ag_core_recv.at[r, which, q],
            sibling,
        )

    def reduce_core(r, which):
        x_of = 1 - x if which == 0 else x
        return remote(
            core_out.at[r, x_of],
            core_in.at[r, x_of],
            rs_core_send.at[r, which],
            rs_core_recv.at[r, which],
            sibling,
        )

    def reduce_x(r, q):
        return remote(
            x_out.at[r, tokens(q)], x_in.at[r, tokens(q)], rs_x_send.at[r, q], rs_x_recv.at[r, q], across
        )

    def reduce_z(r, q, side):
        return remote(
            z_out.at[r, tokens(q)],
            z_in.at[side, r, tokens(q)],
            rs_z_send.at[r, q],
            rs_z_recv.at[side, r, q],
            {"row": z + 2 * side - 1},
        )

    weights = [
        pltpu.make_async_copy(src.at[0], dst, weight_sem.at[i])
        for i, (src, dst) in enumerate(((gate_hbm, gate_w), (up_hbm, up_w), (down_hbm, down_w)))
    ]

    own = pltpu.make_async_copy(acts_hbm, acts.at[z, :, column(x, core)], own_sem.at[0])
    own_ids = pltpu.make_async_copy(ids_hbm, ids, own_sem.at[1])
    own_scores = pltpu.make_async_copy(scores_hbm, meta.at[z, pl.ds(top, top)], own_sem.at[2])
    for copy in [own, own_ids, own_scores] + weights:
        copy.start()

    barrier = pltpu.get_barrier_semaphore()
    pl.semaphore_signal(barrier, inc=1, device_id=sibling, device_id_type=MESH)
    pl.semaphore_signal(barrier, inc=1, device_id=across, device_id_type=MESH)

    @pl.when(z > 0)
    def _():
        pl.semaphore_signal(barrier, inc=1, device_id={"row": z - 1}, device_id_type=MESH)

    @pl.when(z < last)
    def _():
        pl.semaphore_signal(barrier, inc=1, device_id={"row": z + 1}, device_id_type=MESH)

    pl.semaphore_wait(barrier, 2 + jnp.where(z > 0, 1, 0) + jnp.where(z < last, 1, 0))

    for q in range(CHUNKS):
        gather_x(z, q, chunk_of(q)).start()

        @pl.when(z > 0)
        def _():
            gather_z(z, q, 0, chunk_of(q)).start()

        @pl.when(z < last)
        def _():
            gather_z(z, q, 1, chunk_of(q)).start()

    for q in range(CHUNKS):
        gather_core(z, q, 0, chunk_of(q)).start()
    own_ids.wait()
    own_scores.wait()
    meta[z, :top] = ids[...].astype(jnp.float32)

    @pl.when(z > 0)
    def _():
        gather_meta(z, 0).start()

    @pl.when(z < last)
    def _():
        gather_meta(z, 1).start()

    own.wait()

    def pass_on(r, q, side, more):
        gather_z(r, q, side).wait_recv()

        @pl.when(more)
        def _():
            gather_z(r, q, side).start()

        gather_x(r, q).start()
        gather_core(r, q, 0).start()

    def pass_meta(r, side, more):
        gather_meta(r, side).wait_recv()

        @pl.when(more)
        def _():
            gather_meta(r, side).start()

    def cross(r, q):
        here = tokens(q)
        given = kept[r, 1 - x, here] + core_in[r, 1 - x, here].astype(jnp.float32)
        x_out[r, here] = given.astype(x_out.dtype)
        reduce_x(r, q).start()

    def begin_cross(r):
        reduce_core(r, 0).wait_recv()
        for q in range(CHUNKS):
            cross(r, q)
        reduce_core(r, 1).wait_recv()
        total[r] = kept[r, x] + core_in[r, x].astype(jnp.float32)

    def product(r, x_of, core_of, table):
        features = column(x_of, core_of)
        return jnp.dot(acts[r, :, features], table[features, :], preferred_element_type=jnp.float32)

    def first_half(r):
        gate_sum[r] = product(r, x, core, gate_w)
        up_sum[r] = product(r, x, core, up_w)
        for q in range(CHUNKS):
            gather_core(r, q, 0).wait_recv()
        gate_sum[r] += product(r, x, 1 - core, gate_w)
        up_sum[r] += product(r, x, 1 - core, up_w)

    def second_half(r):
        gate_sum[r] += product(r, 1 - x, core, gate_w)
        up_sum[r] += product(r, 1 - x, core, up_w)
        for q in range(CHUNKS):
            gather_core(r, q, 1).wait_recv()
        gate_val = gate_sum[r] + product(r, 1 - x, 1 - core, gate_w)
        up_val = up_sum[r] + product(r, 1 - x, 1 - core, up_w)
        hidden = (gate_val / (1.0 + jnp.exp(-gate_val)) * up_val).astype(jnp.bfloat16)
        chosen = jnp.where(meta[r, :top] == expert.astype(jnp.float32), meta[r, top:], 0.0)
        weight = jnp.sum(jnp.transpose(chosen), axis=1, keepdims=True)

        def weighted(x_of, core_of):
            result = jnp.dot(hidden, down_w[:, column(x_of, core_of)], preferred_element_type=jnp.float32)
            return result * weight

        for which, x_of in enumerate((1 - x, x)):
            core_out[r, x_of] = weighted(x_of, 1 - core).astype(core_out.dtype)
            reduce_core(r, which).start()
        for x_of in (1 - x, x):
            kept[r, x_of] = weighted(x_of, core)

    def expert_step(s, carry):
        below, above = z - 1 - s, z + 1 + s
        from_below, from_above = below >= 0, above <= last
        for q in range(CHUNKS):

            @pl.when(from_below)
            def _():
                pass_on(below, q, 1, z < last)

            @pl.when(from_above)
            def _():
                pass_on(above, q, 0, z > 0)

        @pl.when(from_below)
        def _():
            pass_meta(below, 1, z < last)

        @pl.when(from_above)
        def _():
            pass_meta(above, 0, z > 0)

        r = nth_row(s)
        for q in range(CHUNKS):
            gather_x(r, q).wait_recv()
            gather_core(r, q, 1, place(r, q, 1 - x, core)).start()

        @pl.when(s == 0)
        def _():
            weights[2].wait()

        if rows > 1:

            @pl.when(s == last)
            def _():
                begin_cross(z)

        second_half(r)

        @pl.when(s < last)
        def _():
            first_half(nth_row(s + 1))

        return carry

    for copy in weights[:2]:
        copy.wait()
    first_half(z)
    lax.fori_loop(0, rows, expert_step, 0)

    begin_cross(nth_row(last))

    def line_step(t, carry):
        r = nth_row(last - t)
        following = nth_row(last - t - 1)
        down, up = r < z, r > z
        first = (down & (z == last)) | (up & (z == 0))

        def send_on(q):
            z_out[r, tokens(q)] = total[r, tokens(q)].astype(z_out.dtype)

            @pl.when(down)
            def _():
                reduce_z(r, q, 0).start()

            @pl.when(up)
            def _():
                reduce_z(r, q, 1).start()

        @pl.when(t < last - 1)
        def _():
            reduce_core(following, 0).wait_recv()
            reduce_core(following, 1).wait_recv()

        for q in range(CHUNKS):
            here = tokens(q)
            reduce_x(r, q).wait_recv()

            @pl.when(t < last - 1)
            def _():
                cross(following, q)

            total[r, here] += x_in[r, here].astype(jnp.float32)

            @pl.when(first)
            def _():
                send_on(q)

        @pl.when(t < last - 1)
        def _():
            total[following] = kept[following, x] + core_in[following, x].astype(jnp.float32)

        for q in range(CHUNKS):
            here = tokens(q)

            @pl.when(down & (z < last))
            def _():
                reduce_z(r, q, 0).wait_recv()
                total[r, here] += z_in[0, r, here].astype(jnp.float32)
                send_on(q)

            @pl.when(up & (z > 0))
            def _():
                reduce_z(r, q, 1).wait_recv()
                total[r, here] += z_in[1, r, here].astype(jnp.float32)
                send_on(q)

        return carry

    lax.fori_loop(0, last, line_step, 0)
    for q in range(CHUNKS):
        here = tokens(q)
        reduce_x(z, q).wait_recv()
        total[z, here] += x_in[z, here].astype(jnp.float32)

        @pl.when(z < last)
        def _():
            reduce_z(z, q, 0).wait_recv()
            total[z, here] += z_in[0, z, here].astype(jnp.float32)

        @pl.when(z > 0)
        def _():
            reduce_z(z, q, 1).wait_recv()
            total[z, here] += z_in[1, z, here].astype(jnp.float32)

        out_ref[here] = total[z, here].astype(out_ref.dtype)

    def drain(r, carry):
        for which in range(2):
            reduce_core(r, which).wait_send()
        for q in range(CHUNKS):
            gather_x(r, q).wait_send()
            gather_core(r, q, 0).wait_send()
            gather_core(r, q, 1).wait_send()
            reduce_x(r, q).wait_send()

            @pl.when(r != z)
            def _():
                reduce_z(r, q, 0).wait_send()

        for side, sent in ((0, (r >= z) & (z > 0)), (1, (r <= z) & (z < last))):

            @pl.when(sent)
            def _():
                gather_meta(r, side).wait_send()
                for q in range(CHUNKS):
                    gather_z(r, q, side).wait_send()

        return carry

    lax.fori_loop(0, rows, drain, 0)


def dense_layer(activations, expert_ids, gate_scores, gate_proj, up_proj, down_proj):
    rows = lax.axis_size("row")
    group_rows, width = activations.shape
    model, hidden = gate_proj.shape[1:]
    top = expert_ids.shape[1]
    dtype = activations.dtype
    vmem = pl.BlockSpec(memory_space=pltpu.VMEM)
    anywhere = pl.BlockSpec(memory_space=pl.ANY)
    dma = pltpu.SemaphoreType.DMA
    flops = 6 * rows * group_rows * model * hidden
    return pl.pallas_call(
        functools.partial(dense_kernel, rows),
        out_shape=jax.ShapeDtypeStruct((group_rows, width), dtype),
        in_specs=[anywhere] * 6,
        out_specs=vmem,
        scratch_shapes=[
            pltpu.VMEM((rows, group_rows, model), dtype),
            pltpu.VMEM((top, group_rows), jnp.int32),
            pltpu.VMEM((rows, 2 * top, group_rows), jnp.float32),
            pltpu.VMEM((model, hidden), dtype),
            pltpu.VMEM((model, hidden), dtype),
            pltpu.VMEM((hidden, model), dtype),
            pltpu.VMEM((rows, group_rows, hidden), jnp.float32),
            pltpu.VMEM((rows, group_rows, hidden), jnp.float32),
            pltpu.VMEM((rows, PAIR, group_rows, width), jnp.float32),
            pltpu.VMEM((rows, PAIR, group_rows, width), dtype),
            pltpu.VMEM((rows, PAIR, group_rows, width), dtype),
            pltpu.VMEM((rows, group_rows, width), jnp.float32),
            pltpu.VMEM((rows, group_rows, width), dtype),
            pltpu.VMEM((rows, group_rows, width), dtype),
            pltpu.VMEM((rows, group_rows, width), dtype),
            pltpu.VMEM((PAIR, rows, group_rows, width), dtype),
            dma((3,)),
            dma((3,)),
            dma((2, rows, CHUNKS)),
            dma((rows, CHUNKS)),
            dma((2, rows)),
            dma((rows,)),
            dma((rows, CHUNKS)),
            dma((rows, CHUNKS)),
            dma((rows, 2, CHUNKS)),
            dma((rows, 2, CHUNKS)),
            dma((rows, 2)),
            dma((rows, 2)),
            dma((rows, CHUNKS)),
            dma((rows, CHUNKS)),
            dma((rows, CHUNKS)),
            dma((2, rows, CHUNKS)),
        ],
        compiler_params=pltpu.CompilerParams(
            collective_id=0, has_side_effects=True, vmem_limit_bytes=64 * 1024 * 1024
        ),
        cost_estimate=pl.CostEstimate(
            flops=flops, bytes_accessed=6 * model * hidden, transcendentals=rows * group_rows * hidden
        ),
    )(activations, expert_ids.T, gate_scores.T, gate_proj, up_proj, down_proj)


def either_way(*arrays):
    activations, expert_ids = arrays[:2]
    col_count, sub_count = lax.axis_size("col"), lax.axis_size("sub")
    experts = lax.axis_size("row") * col_count
    block_rows = expert_ids.shape[0] // (col_count * sub_count)
    every_row = 2 * block_rows * TOP // experts >= block_rows
    if every_row and sub_count == 1 and col_count == PAIR * PAIR:
        return dense_layer(*arrays)
    return per_device(*arrays)


def solution(mesh):
    placed = (
        P(("parts", "row"), ("col", "sub")),
        P(("parts", "row"), None),
        P(("parts", "row"), None),
        P(("row", "col"), None, "sub"),
        P(("row", "col"), None, "sub"),
        P(("row", "col"), "sub", None),
    )
    return jax.shard_map(
        either_way,
        mesh=mesh,
        in_specs=placed,
        out_specs=P(("parts", "row"), ("col", "sub")),
        check_vma=False,
    )
```

```python
import functools

import jax
import jax.numpy as jnp
from jax import lax
from jax.experimental import pallas as pl
from jax.experimental.pallas import tpu as pltpu
from jax.sharding import PartitionSpec as P

TOP = 8
PAIR = 2
CHUNKS = 2
MESH = pl.DeviceIdType.MESH


def slot_places(chosen, experts, capacity):
    count = chosen.shape[0] * chosen.shape[1]
    flat_ids = chosen.reshape(count)
    onehot = (flat_ids[:, None] == jnp.arange(experts, dtype=jnp.int32)[None, :]).astype(jnp.int32)
    running = jnp.cumsum(onehot, axis=0) - 1
    ranking = jnp.sum(onehot * running, axis=1)
    return flat_ids * capacity + ranking


def fill_slots(row_block, places, experts, capacity, top_count):
    owners = jnp.full((experts * capacity,), row_block.shape[0], jnp.int32)
    owners = owners.at[places].set(jnp.arange(places.shape[0], dtype=jnp.int32) // top_count)
    padded = jnp.concatenate(
        [row_block, jnp.zeros((1, row_block.shape[1]), row_block.dtype)], axis=0
    )
    return padded[owners].reshape(experts, capacity, row_block.shape[1])


def run_expert(stacked, gate_proj, up_proj, down_proj):
    layout = stacked.shape
    inputs = stacked.reshape(-1, layout[-1])
    gate_val = jnp.dot(inputs, gate_proj[0], preferred_element_type=jnp.float32)
    up_val = jnp.dot(inputs, up_proj[0], preferred_element_type=jnp.float32)
    hidden = (jax.nn.silu(gate_val) * up_val).astype(jnp.bfloat16)
    partial_out = jnp.dot(hidden, down_proj[0], preferred_element_type=jnp.float32)
    return partial_out.reshape(layout)


def send_back(stacked, gate_proj, up_proj, down_proj):
    partial_out = run_expert(stacked, gate_proj, up_proj, down_proj)
    landed = lax.all_to_all(partial_out, ("row", "col"), split_axis=1, concat_axis=1, tiled=True)
    return lax.psum_scatter(landed, "sub", scatter_dimension=0, tiled=True).astype(jnp.bfloat16)


def per_device(activations, expert_ids, gate_scores, gate_proj, up_proj, down_proj):
    col_count = lax.axis_size("col")
    sub_count = lax.axis_size("sub")
    experts = lax.axis_size("row") * col_count
    group_rows = expert_ids.shape[0]
    block_rows = group_rows // (col_count * sub_count)
    capacity = max(2, min(block_rows, 2 * block_rows * TOP // experts))
    quarter = sub_count * block_rows
    width = activations.shape[1] * col_count * sub_count
    whole = lax.all_gather(activations, ("col", "sub"), axis=1, tiled=True)
    col_start = lax.axis_index("col") * quarter
    sub_index = lax.axis_index("sub")
    my_rows = lax.dynamic_slice_in_dim(whole, col_start, quarter, 0)
    my_ids = lax.dynamic_slice_in_dim(expert_ids, col_start, quarter, 0)
    own_scores = lax.dynamic_slice_in_dim(
        gate_scores, col_start + sub_index * block_rows, block_rows, 0
    )
    places = []
    for member in range(sub_count):
        lower = member * block_rows
        places.append(slot_places(my_ids[lower : lower + block_rows], experts, capacity))
    own_places = lax.dynamic_index_in_dim(jnp.stack(places), sub_index, 0, keepdims=False)
    buffers = []
    for member in range(sub_count):
        lower = member * block_rows
        buffers.append(
            fill_slots(my_rows[lower : lower + block_rows], places[member], experts, capacity, TOP)
        )
    outgoing = jnp.stack(buffers)
    returned = send_back(
        lax.all_to_all(outgoing, ("row", "col"), split_axis=1, concat_axis=1, tiled=True),
        gate_proj,
        up_proj,
        down_proj,
    )
    picked = returned.reshape(-1, width)[own_places].reshape(block_rows, TOP, width)
    share = jnp.sum(own_scores[:, :, None] * picked.astype(jnp.float32), axis=1)
    return lax.all_to_all(
        share.astype(jnp.bfloat16), ("col", "sub"), split_axis=1, concat_axis=0, tiled=True
    )


def dense_kernel(
    rows,
    acts_hbm,
    ids_hbm,
    scores_hbm,
    gate_hbm,
    up_hbm,
    down_hbm,
    out_ref,
    acts,
    ids,
    meta,
    gate_w,
    up_w,
    down_w,
    gate_sum,
    up_sum,
    kept,
    core_out,
    core_in,
    total,
    x_out,
    x_in,
    z_out,
    z_in,
    far_out,
    far_in,
    weight_sem,
    own_sem,
    ag_z_send,
    ag_z_recv,
    meta_send,
    meta_recv,
    ag_x_send,
    ag_x_recv,
    ag_core_send,
    ag_core_recv,
    rs_core_send,
    rs_core_recv,
    rs_x_send,
    rs_x_recv,
    rs_z_send,
    rs_z_recv,
    ag_far_send,
    ag_far_recv,
    rs_far_send,
    rs_far_recv,
):
    top, group_rows = ids_hbm.shape
    part = group_rows // CHUNKS
    width = acts_hbm.shape[1]
    z = lax.axis_index("row")
    col = lax.axis_index("col")
    x, core = col // PAIR, col % PAIR
    expert = z * lax.axis_size("col") + col
    sibling = {"col": x * PAIR + (1 - core)}
    across = {"col": (1 - x) * PAIR + core}
    last = rows - 1

    far_chunk = CHUNKS - 1
    ends = ((0, z < last, z > 0), (last, z > 0, z < last))

    def at_end(r):
        return (r == 0) | (r == last)

    def by_x(r, q):
        return jnp.logical_not(at_end(r)) | (r == z) if q == far_chunk else r >= 0

    def column(x_of, core_of):
        return pl.ds(pl.multiple_of((x_of * PAIR + core_of) * width, width), width)

    def nth_row(s):
        both = jnp.minimum(z, last - z)
        ahead = jnp.where(z <= last - z, 1, -1)
        near = z + ahead * jnp.where(s % 2 == 1, (s + 1) // 2, -(s // 2))
        rest = jnp.where(z <= last - z, s, last - s)
        return jnp.where(s <= 2 * both, near, rest)

    def remote(src, dst, send, recv, device):
        return pltpu.make_async_remote_copy(
            src_ref=src, dst_ref=dst, send_sem=send, recv_sem=recv, device_id=device, device_id_type=MESH
        )

    def tokens(q):
        return pl.ds(q * part, part)

    def place(r, q, x_of, core_of):
        return acts.at[r, tokens(q), column(x_of, core_of)]

    def chunk_of(q):
        return acts_hbm.at[tokens(q)]

    def gather_z(r, q, side, src=None):
        there = place(r, q, x, core)
        return remote(
            there if src is None else src,
            there,
            ag_z_send.at[side, r, q],
            ag_z_recv.at[r, q],
            {"row": z + 2 * side - 1},
        )

    def gather_meta(r, side):
        return remote(
            meta.at[r], meta.at[r], meta_send.at[side, r], meta_recv.at[r], {"row": z + 2 * side - 1}
        )

    def gather_x(r, q, src=None):
        there = place(r, q, x, core)
        return remote(there if src is None else src, there, ag_x_send.at[r, q], ag_x_recv.at[r, q], across)

    def gather_core(r, q, which, src=None):
        there = place(r, q, x if which == 0 else 1 - x, core)
        return remote(
            there if src is None else src,
            there,
            ag_core_send.at[r, which, q],
            ag_core_recv.at[r, which, q],
            sibling,
        )

    def reduce_core(r, which):
        x_of = 1 - x if which == 0 else x
        return remote(
            core_out.at[r, x_of],
            core_in.at[r, x_of],
            rs_core_send.at[r, which],
            rs_core_recv.at[r, which],
            sibling,
        )

    def reduce_x(r, q):
        return remote(
            x_out.at[r, tokens(q)], x_in.at[r, tokens(q)], rs_x_send.at[r, q], rs_x_recv.at[r, q], across
        )

    def reduce_z(r, q, side):
        return remote(
            z_out.at[r, tokens(q)],
            z_in.at[side, r, tokens(q)],
            rs_z_send.at[r, q],
            rs_z_recv.at[side, r, q],
            {"row": z + 2 * side - 1},
        )

    def gather_far(i):
        there = place(ends[i][0], far_chunk, 1 - x, core)
        return remote(there, there, ag_far_send.at[i], ag_far_recv.at[i], {"row": z + 1 - 2 * i})

    def reduce_far(i):
        return remote(
            far_out.at[i], far_in.at[i], rs_far_send.at[i], rs_far_recv.at[i], {"row": z + 2 * i - 1}
        )

    weights = [
        pltpu.make_async_copy(src.at[0], dst, weight_sem.at[i])
        for i, (src, dst) in enumerate(((gate_hbm, gate_w), (up_hbm, up_w), (down_hbm, down_w)))
    ]

    own = pltpu.make_async_copy(acts_hbm, acts.at[z, :, column(x, core)], own_sem.at[0])
    own_ids = pltpu.make_async_copy(ids_hbm, ids, own_sem.at[1])
    own_scores = pltpu.make_async_copy(scores_hbm, meta.at[z, pl.ds(top, top)], own_sem.at[2])
    for copy in [own, own_ids, own_scores] + weights:
        copy.start()

    barrier = pltpu.get_barrier_semaphore()
    pl.semaphore_signal(barrier, inc=1, device_id=sibling, device_id_type=MESH)
    pl.semaphore_signal(barrier, inc=1, device_id=across, device_id_type=MESH)

    @pl.when(z > 0)
    def _():
        pl.semaphore_signal(barrier, inc=1, device_id={"row": z - 1}, device_id_type=MESH)

    @pl.when(z < last)
    def _():
        pl.semaphore_signal(barrier, inc=1, device_id={"row": z + 1}, device_id_type=MESH)

    pl.semaphore_wait(barrier, 2 + jnp.where(z > 0, 1, 0) + jnp.where(z < last, 1, 0))

    for q in range(CHUNKS):
        gather_x(z, q, chunk_of(q)).start()

        @pl.when(z > 0)
        def _():
            gather_z(z, q, 0, chunk_of(q)).start()

        @pl.when(z < last)
        def _():
            gather_z(z, q, 1, chunk_of(q)).start()

    for q in range(CHUNKS):
        gather_core(z, q, 0, chunk_of(q)).start()
    own_ids.wait()
    own_scores.wait()
    meta[z, :top] = ids[...].astype(jnp.float32)

    @pl.when(z > 0)
    def _():
        gather_meta(z, 0).start()

    @pl.when(z < last)
    def _():
        gather_meta(z, 1).start()

    own.wait()

    def pass_on(r, q, side, more):
        gather_z(r, q, side).wait_recv()

        @pl.when(more)
        def _():
            gather_z(r, q, side).start()

        @pl.when(by_x(r, q))
        def _():
            gather_x(r, q).start()

        gather_core(r, q, 0).start()

    def pass_meta(r, side, more):
        gather_meta(r, side).wait_recv()

        @pl.when(more)
        def _():
            gather_meta(r, side).start()

    def cross(r, q):
        here = tokens(q)
        given = kept[r, 1 - x, here] + core_in[r, 1 - x, here].astype(jnp.float32)
        x_out[r, here] = given.astype(x_out.dtype)
        reduce_x(r, q).start()

    def begin_cross(r, skip):
        reduce_core(r, 0).wait_recv()
        for q in reversed(range(CHUNKS)):

            @pl.when(jnp.logical_not(skip) if q == far_chunk else r >= 0)
            def _():
                cross(r, q)

        reduce_core(r, 1).wait_recv()
        total[r] = kept[r, x] + core_in[r, x].astype(jnp.float32)

    def product(r, x_of, core_of, table):
        features = column(x_of, core_of)
        return jnp.dot(acts[r, :, features], table[features, :], preferred_element_type=jnp.float32)

    def first_half(r):
        gate_sum[r] = product(r, x, core, gate_w)
        up_sum[r] = product(r, x, core, up_w)
        for q in range(CHUNKS):
            gather_core(r, q, 0).wait_recv()
        gate_sum[r] += product(r, x, 1 - core, gate_w)
        up_sum[r] += product(r, x, 1 - core, up_w)

    def second_half(r):
        gate_sum[r] += product(r, 1 - x, core, gate_w)
        up_sum[r] += product(r, 1 - x, core, up_w)
        for q in range(CHUNKS):
            gather_core(r, q, 1).wait_recv()
        gate_val = gate_sum[r] + product(r, 1 - x, 1 - core, gate_w)
        up_val = up_sum[r] + product(r, 1 - x, 1 - core, up_w)
        hidden = (gate_val / (1.0 + jnp.exp(-gate_val)) * up_val).astype(jnp.bfloat16)
        chosen = jnp.where(meta[r, :top] == expert.astype(jnp.float32), meta[r, top:], 0.0)
        weight = jnp.sum(jnp.transpose(chosen), axis=1, keepdims=True)

        def weighted(x_of, core_of):
            result = jnp.dot(hidden, down_w[:, column(x_of, core_of)], preferred_element_type=jnp.float32)
            return result * weight

        for which, x_of in enumerate((1 - x, x)):
            core_out[r, x_of] = weighted(x_of, 1 - core).astype(core_out.dtype)
            reduce_core(r, which).start()
        for x_of in (1 - x, x):
            kept[r, x_of] = weighted(x_of, core)

    def expert_step(s, carry):
        below, above = z - 1 - s, z + 1 + s
        from_below, from_above = below >= 0, above <= last
        for q in range(CHUNKS):

            @pl.when(from_below)
            def _():
                pass_on(below, q, 1, z < last)

            @pl.when(from_above)
            def _():
                pass_on(above, q, 0, z > 0)

        @pl.when(from_below)
        def _():
            pass_meta(below, 1, z < last)

        @pl.when(from_above)
        def _():
            pass_meta(above, 0, z > 0)

        r = nth_row(s)
        for q in range(CHUNKS):

            @pl.when(by_x(r, q))
            def _():
                gather_x(r, q).wait_recv()

                if q == far_chunk:
                    for i, (end, sends, _) in enumerate(ends):

                        @pl.when((s == 0) & (z == end) & sends)
                        def _():
                            gather_far(i).start()

                gather_core(r, q, 1, place(r, q, 1 - x, core)).start()

        for i, (end, sends, _) in enumerate(ends):

            @pl.when((s > 0) & ((z - s == end) if i == 0 else (z + s == end)))
            def _():
                gather_far(i).wait_recv()

                @pl.when(sends)
                def _():
                    gather_far(i).start()

                gather_core(end, far_chunk, 1, place(end, far_chunk, 1 - x, core)).start()

        @pl.when(s == 0)
        def _():
            weights[2].wait()

        if rows > 1:

            @pl.when(s == last)
            def _():
                begin_cross(z, at_end(z))

        second_half(r)

        @pl.when(s < last)
        def _():
            first_half(nth_row(s + 1))

        return carry

    for copy in weights[:2]:
        copy.wait()
    first_half(z)
    lax.fori_loop(0, rows, expert_step, 0)

    furthest = nth_row(last)
    begin_cross(furthest, furthest != z if rows > 1 else furthest < 0)

    def drain_gather(r, carry):
        for q in range(CHUNKS):

            @pl.when(by_x(r, q))
            def _():
                gather_x(r, q).wait_send()

            gather_core(r, q, 0).wait_send()
            gather_core(r, q, 1).wait_send()

        for side, sent in ((0, (r >= z) & (z > 0)), (1, (r <= z) & (z < last))):

            @pl.when(sent)
            def _():
                gather_meta(r, side).wait_send()
                for q in range(CHUNKS):
                    gather_z(r, q, side).wait_send()

        return carry

    def line_step(t, carry):
        r = nth_row(last - t)
        following = nth_row(last - t - 1)
        down, up = r < z, r > z
        first = (down & (z == last)) | (up & (z == 0))
        is_end = at_end(r)
        here_far = tokens(far_chunk)

        def send_on(q):
            z_out[r, tokens(q)] = total[r, tokens(q)].astype(z_out.dtype)

            @pl.when(down)
            def _():
                reduce_z(r, q, 0).start()

            @pl.when(up)
            def _():
                reduce_z(r, q, 1).start()

        def far_share():
            return kept[r, 1 - x, here_far] + core_in[r, 1 - x, here_far].astype(jnp.float32)

        for i, (end, _, _) in enumerate(ends):

            @pl.when(first & (r == end))
            def _():
                far_out[i] = far_share().astype(far_out.dtype)
                reduce_far(i).start()

        @pl.when(first & is_end)
        def _():
            send_on(far_chunk)

        @pl.when(t < last - 1)
        def _():
            reduce_core(following, 0).wait_recv()
            reduce_core(following, 1).wait_recv()

        for q in reversed(range(CHUNKS)):
            here = tokens(q)
            crosses = by_x(r, q)

            @pl.when(crosses)
            def _():
                reduce_x(r, q).wait_recv()

            @pl.when((t < last - 1) & by_x(following, q))
            def _():
                cross(following, q)

            @pl.when(crosses)
            def _():
                total[r, here] += x_in[r, here].astype(jnp.float32)

            @pl.when(first & crosses)
            def _():
                send_on(q)

        @pl.when(t < last - 1)
        def _():
            total[following] = kept[following, x] + core_in[following, x].astype(jnp.float32)

        for i, (end, _, _) in enumerate(ends):

            @pl.when((r == end) & jnp.logical_not(first))
            def _():
                reduce_far(i).wait_recv()
                far_out[i] = (far_share() + far_in[i].astype(jnp.float32)).astype(far_out.dtype)
                reduce_far(i).start()

        for q in reversed(range(CHUNKS)):
            here = tokens(q)

            @pl.when(down & (z < last))
            def _():
                reduce_z(r, q, 0).wait_recv()
                total[r, here] += z_in[0, r, here].astype(jnp.float32)
                send_on(q)

            @pl.when(up & (z > 0))
            def _():
                reduce_z(r, q, 1).wait_recv()
                total[r, here] += z_in[1, r, here].astype(jnp.float32)
                send_on(q)

        return carry

    lax.fori_loop(0, rows, drain_gather, 0)
    for i, (_, sends, _) in enumerate(ends):

        @pl.when(sends)
        def _():
            gather_far(i).wait_send()

    lax.fori_loop(0, last, line_step, 0)

    if rows > 1:
        here_far = tokens(far_chunk)
        for i, (end, _, _) in enumerate(ends):

            @pl.when(z == end)
            def _():
                reduce_far(i).wait_recv()
                given = kept[z, 1 - x, here_far] + core_in[z, 1 - x, here_far].astype(jnp.float32)
                x_out[z, here_far] = (given + far_in[i].astype(jnp.float32)).astype(x_out.dtype)
                reduce_x(z, far_chunk).start()

    for q in range(CHUNKS):
        here = tokens(q)
        reduce_x(z, q).wait_recv()
        total[z, here] += x_in[z, here].astype(jnp.float32)

        @pl.when(z < last)
        def _():
            reduce_z(z, q, 0).wait_recv()
            total[z, here] += z_in[0, z, here].astype(jnp.float32)

        @pl.when(z > 0)
        def _():
            reduce_z(z, q, 1).wait_recv()
            total[z, here] += z_in[1, z, here].astype(jnp.float32)

        out_ref[here] = total[z, here].astype(out_ref.dtype)

    def drain(r, carry):
        for which in range(2):
            reduce_core(r, which).wait_send()
        for q in range(CHUNKS):

            @pl.when(by_x(r, q))
            def _():
                reduce_x(r, q).wait_send()

            @pl.when(r != z)
            def _():
                reduce_z(r, q, 0).wait_send()

        return carry

    lax.fori_loop(0, rows, drain, 0)
    for i, (_, _, sends) in enumerate(ends):

        @pl.when(sends)
        def _():
            reduce_far(i).wait_send()


def dense_layer(activations, expert_ids, gate_scores, gate_proj, up_proj, down_proj):
    rows = lax.axis_size("row")
    group_rows, width = activations.shape
    model, hidden = gate_proj.shape[1:]
    top = expert_ids.shape[1]
    dtype = activations.dtype
    vmem = pl.BlockSpec(memory_space=pltpu.VMEM)
    anywhere = pl.BlockSpec(memory_space=pl.ANY)
    dma = pltpu.SemaphoreType.DMA
    flops = 6 * rows * group_rows * model * hidden
    return pl.pallas_call(
        functools.partial(dense_kernel, rows),
        out_shape=jax.ShapeDtypeStruct((group_rows, width), dtype),
        in_specs=[anywhere] * 6,
        out_specs=vmem,
        scratch_shapes=[
            pltpu.VMEM((rows, group_rows, model), dtype),
            pltpu.VMEM((top, group_rows), jnp.int32),
            pltpu.VMEM((rows, 2 * top, group_rows), jnp.float32),
            pltpu.VMEM((model, hidden), dtype),
            pltpu.VMEM((model, hidden), dtype),
            pltpu.VMEM((hidden, model), dtype),
            pltpu.VMEM((rows, group_rows, hidden), jnp.float32),
            pltpu.VMEM((rows, group_rows, hidden), jnp.float32),
            pltpu.VMEM((rows, PAIR, group_rows, width), jnp.float32),
            pltpu.VMEM((rows, PAIR, group_rows, width), dtype),
            pltpu.VMEM((rows, PAIR, group_rows, width), dtype),
            pltpu.VMEM((rows, group_rows, width), jnp.float32),
            pltpu.VMEM((rows, group_rows, width), dtype),
            pltpu.VMEM((rows, group_rows, width), dtype),
            pltpu.VMEM((rows, group_rows, width), dtype),
            pltpu.VMEM((PAIR, rows, group_rows, width), dtype),
            pltpu.VMEM((2, group_rows // CHUNKS, width), dtype),
            pltpu.VMEM((2, group_rows // CHUNKS, width), dtype),
            dma((3,)),
            dma((3,)),
            dma((2, rows, CHUNKS)),
            dma((rows, CHUNKS)),
            dma((2, rows)),
            dma((rows,)),
            dma((rows, CHUNKS)),
            dma((rows, CHUNKS)),
            dma((rows, 2, CHUNKS)),
            dma((rows, 2, CHUNKS)),
            dma((rows, 2)),
            dma((rows, 2)),
            dma((rows, CHUNKS)),
            dma((rows, CHUNKS)),
            dma((rows, CHUNKS)),
            dma((2, rows, CHUNKS)),
            dma((2,)),
            dma((2,)),
            dma((2,)),
            dma((2,)),
        ],
        compiler_params=pltpu.CompilerParams(
            collective_id=0, has_side_effects=True, vmem_limit_bytes=64 * 1024 * 1024
        ),
        cost_estimate=pl.CostEstimate(
            flops=flops, bytes_accessed=6 * model * hidden, transcendentals=rows * group_rows * hidden
        ),
    )(activations, expert_ids.T, gate_scores.T, gate_proj, up_proj, down_proj)


def either_way(*arrays):
    activations, expert_ids = arrays[:2]
    col_count, sub_count = lax.axis_size("col"), lax.axis_size("sub")
    experts = lax.axis_size("row") * col_count
    block_rows = expert_ids.shape[0] // (col_count * sub_count)
    every_row = 2 * block_rows * TOP // experts >= block_rows
    if every_row and sub_count == 1 and col_count == PAIR * PAIR:
        return dense_layer(*arrays)
    return per_device(*arrays)


def solution(mesh):
    placed = (
        P(("parts", "row"), ("col", "sub")),
        P(("parts", "row"), None),
        P(("parts", "row"), None),
        P(("row", "col"), None, "sub"),
        P(("row", "col"), None, "sub"),
        P(("row", "col"), "sub", None),
    )
    return jax.shard_map(
        either_way,
        mesh=mesh,
        in_specs=placed,
        out_specs=P(("parts", "row"), ("col", "sub")),
        check_vma=False,
    )
```

```python
import functools

import jax
import jax.numpy as jnp
from jax import lax
from jax.experimental import pallas as pl
from jax.experimental.pallas import tpu as pltpu
from jax.sharding import PartitionSpec as P

TOP = 8
PAIR = 2
CHUNKS = 4
MESH = pl.DeviceIdType.MESH


def slot_places(chosen, experts, capacity):
    count = chosen.shape[0] * chosen.shape[1]
    flat_ids = chosen.reshape(count)
    onehot = (flat_ids[:, None] == jnp.arange(experts, dtype=jnp.int32)[None, :]).astype(jnp.int32)
    running = jnp.cumsum(onehot, axis=0) - 1
    ranking = jnp.sum(onehot * running, axis=1)
    return flat_ids * capacity + ranking


def fill_slots(row_block, places, experts, capacity, top_count):
    owners = jnp.full((experts * capacity,), row_block.shape[0], jnp.int32)
    owners = owners.at[places].set(jnp.arange(places.shape[0], dtype=jnp.int32) // top_count)
    padded = jnp.concatenate(
        [row_block, jnp.zeros((1, row_block.shape[1]), row_block.dtype)], axis=0
    )
    return padded[owners].reshape(experts, capacity, row_block.shape[1])


def run_expert(stacked, gate_proj, up_proj, down_proj):
    layout = stacked.shape
    inputs = stacked.reshape(-1, layout[-1])
    gate_val = jnp.dot(inputs, gate_proj[0], preferred_element_type=jnp.float32)
    up_val = jnp.dot(inputs, up_proj[0], preferred_element_type=jnp.float32)
    hidden = (jax.nn.silu(gate_val) * up_val).astype(jnp.bfloat16)
    partial_out = jnp.dot(hidden, down_proj[0], preferred_element_type=jnp.float32)
    return partial_out.reshape(layout)


def send_back(stacked, gate_proj, up_proj, down_proj):
    partial_out = run_expert(stacked, gate_proj, up_proj, down_proj)
    landed = lax.all_to_all(partial_out, ("row", "col"), split_axis=1, concat_axis=1, tiled=True)
    return lax.psum_scatter(landed, "sub", scatter_dimension=0, tiled=True).astype(jnp.bfloat16)


def per_device(activations, expert_ids, gate_scores, gate_proj, up_proj, down_proj):
    col_count = lax.axis_size("col")
    sub_count = lax.axis_size("sub")
    experts = lax.axis_size("row") * col_count
    group_rows = expert_ids.shape[0]
    block_rows = group_rows // (col_count * sub_count)
    capacity = max(2, min(block_rows, 2 * block_rows * TOP // experts))
    quarter = sub_count * block_rows
    width = activations.shape[1] * col_count * sub_count
    whole = lax.all_gather(activations, ("col", "sub"), axis=1, tiled=True)
    col_start = lax.axis_index("col") * quarter
    sub_index = lax.axis_index("sub")
    my_rows = lax.dynamic_slice_in_dim(whole, col_start, quarter, 0)
    my_ids = lax.dynamic_slice_in_dim(expert_ids, col_start, quarter, 0)
    own_scores = lax.dynamic_slice_in_dim(
        gate_scores, col_start + sub_index * block_rows, block_rows, 0
    )
    places = []
    for member in range(sub_count):
        lower = member * block_rows
        places.append(slot_places(my_ids[lower : lower + block_rows], experts, capacity))
    own_places = lax.dynamic_index_in_dim(jnp.stack(places), sub_index, 0, keepdims=False)
    buffers = []
    for member in range(sub_count):
        lower = member * block_rows
        buffers.append(
            fill_slots(my_rows[lower : lower + block_rows], places[member], experts, capacity, TOP)
        )
    outgoing = jnp.stack(buffers)
    returned = send_back(
        lax.all_to_all(outgoing, ("row", "col"), split_axis=1, concat_axis=1, tiled=True),
        gate_proj,
        up_proj,
        down_proj,
    )
    picked = returned.reshape(-1, width)[own_places].reshape(block_rows, TOP, width)
    share = jnp.sum(own_scores[:, :, None] * picked.astype(jnp.float32), axis=1)
    return lax.all_to_all(
        share.astype(jnp.bfloat16), ("col", "sub"), split_axis=1, concat_axis=0, tiled=True
    )


def dense_kernel(
    rows,
    acts_hbm,
    ids_hbm,
    scores_hbm,
    gate_hbm,
    up_hbm,
    down_hbm,
    out_ref,
    acts,
    ids,
    meta,
    gate_w,
    up_w,
    down_w,
    gate_sum,
    up_sum,
    kept,
    core_out,
    core_in,
    total,
    x_out,
    x_in,
    z_out,
    z_in,
    far_out,
    far_in,
    weight_sem,
    own_sem,
    ag_z_send,
    ag_z_recv,
    meta_send,
    meta_recv,
    ag_x_send,
    ag_x_recv,
    ag_core_send,
    ag_core_recv,
    rs_core_send,
    rs_core_recv,
    rs_x_send,
    rs_x_recv,
    rs_z_send,
    rs_z_recv,
    ag_far_send,
    ag_far_recv,
    rs_far_send,
    rs_far_recv,
):
    top, group_rows = ids_hbm.shape
    part = group_rows // CHUNKS
    width = acts_hbm.shape[1]
    z = lax.axis_index("row")
    col = lax.axis_index("col")
    x, core = col // PAIR, col % PAIR
    expert = z * lax.axis_size("col") + col
    sibling = {"col": x * PAIR + (1 - core)}
    across = {"col": (1 - x) * PAIR + core}
    last = rows - 1

    far_chunk = CHUNKS - 1
    ends = ((0, z < last, z > 0), (last, z > 0, z < last))

    def at_end(r):
        return (r == 0) | (r == last)

    def by_x(r, q):
        return jnp.logical_not(at_end(r)) | (r == z) if q == far_chunk else r >= 0

    def column(x_of, core_of):
        return pl.ds(pl.multiple_of((x_of * PAIR + core_of) * width, width), width)

    def nth_row(s):
        both = jnp.minimum(z, last - z)
        ahead = jnp.where(z <= last - z, 1, -1)
        near = z + ahead * jnp.where(s % 2 == 1, (s + 1) // 2, -(s // 2))
        rest = jnp.where(z <= last - z, s, last - s)
        return jnp.where(s <= 2 * both, near, rest)

    def remote(src, dst, send, recv, device):
        return pltpu.make_async_remote_copy(
            src_ref=src, dst_ref=dst, send_sem=send, recv_sem=recv, device_id=device, device_id_type=MESH
        )

    def tokens(q):
        return pl.ds(q * part, part)

    def place(r, q, x_of, core_of):
        return acts.at[r, tokens(q), column(x_of, core_of)]

    def chunk_of(q):
        return acts_hbm.at[tokens(q)]

    def gather_z(r, q, side, src=None):
        there = place(r, q, x, core)
        return remote(
            there if src is None else src,
            there,
            ag_z_send.at[side, r, q],
            ag_z_recv.at[r, q],
            {"row": z + 2 * side - 1},
        )

    def gather_meta(r, side):
        return remote(
            meta.at[r], meta.at[r], meta_send.at[side, r], meta_recv.at[r], {"row": z + 2 * side - 1}
        )

    def gather_x(r, q, src=None):
        there = place(r, q, x, core)
        return remote(there if src is None else src, there, ag_x_send.at[r, q], ag_x_recv.at[r, q], across)

    def gather_core(r, q, which, src=None):
        there = place(r, q, x if which == 0 else 1 - x, core)
        return remote(
            there if src is None else src,
            there,
            ag_core_send.at[r, which, q],
            ag_core_recv.at[r, which, q],
            sibling,
        )

    def reduce_core(r, which):
        x_of = 1 - x if which == 0 else x
        return remote(
            core_out.at[r, x_of],
            core_in.at[r, x_of],
            rs_core_send.at[r, which],
            rs_core_recv.at[r, which],
            sibling,
        )

    def reduce_x(r, q):
        return remote(
            x_out.at[r, tokens(q)], x_in.at[r, tokens(q)], rs_x_send.at[r, q], rs_x_recv.at[r, q], across
        )

    def reduce_z(r, q, side):
        return remote(
            z_out.at[r, tokens(q)],
            z_in.at[side, r, tokens(q)],
            rs_z_send.at[r, q],
            rs_z_recv.at[side, r, q],
            {"row": z + 2 * side - 1},
        )

    def gather_far(i):
        there = place(ends[i][0], far_chunk, 1 - x, core)
        return remote(there, there, ag_far_send.at[i], ag_far_recv.at[i], {"row": z + 1 - 2 * i})

    def reduce_far(i):
        return remote(
            far_out.at[i], far_in.at[i], rs_far_send.at[i], rs_far_recv.at[i], {"row": z + 2 * i - 1}
        )

    weights = [
        pltpu.make_async_copy(src.at[0], dst, weight_sem.at[i])
        for i, (src, dst) in enumerate(((gate_hbm, gate_w), (up_hbm, up_w), (down_hbm, down_w)))
    ]

    own = pltpu.make_async_copy(acts_hbm, acts.at[z, :, column(x, core)], own_sem.at[0])
    own_ids = pltpu.make_async_copy(ids_hbm, ids, own_sem.at[1])
    own_scores = pltpu.make_async_copy(scores_hbm, meta.at[z, pl.ds(top, top)], own_sem.at[2])
    for copy in [own, own_ids, own_scores] + weights:
        copy.start()

    barrier = pltpu.get_barrier_semaphore()
    pl.semaphore_signal(barrier, inc=1, device_id=sibling, device_id_type=MESH)
    pl.semaphore_signal(barrier, inc=1, device_id=across, device_id_type=MESH)

    @pl.when(z > 0)
    def _():
        pl.semaphore_signal(barrier, inc=1, device_id={"row": z - 1}, device_id_type=MESH)

    @pl.when(z < last)
    def _():
        pl.semaphore_signal(barrier, inc=1, device_id={"row": z + 1}, device_id_type=MESH)

    pl.semaphore_wait(barrier, 2 + jnp.where(z > 0, 1, 0) + jnp.where(z < last, 1, 0))

    for q in range(CHUNKS):
        gather_x(z, q, chunk_of(q)).start()

        @pl.when(z > 0)
        def _():
            gather_z(z, q, 0, chunk_of(q)).start()

        @pl.when(z < last)
        def _():
            gather_z(z, q, 1, chunk_of(q)).start()

    for q in range(CHUNKS):
        gather_core(z, q, 0, chunk_of(q)).start()
    own_ids.wait()
    own_scores.wait()
    meta[z, :top] = ids[...].astype(jnp.float32)

    @pl.when(z > 0)
    def _():
        gather_meta(z, 0).start()

    @pl.when(z < last)
    def _():
        gather_meta(z, 1).start()

    own.wait()

    def pass_on(r, q, side, more):
        gather_z(r, q, side).wait_recv()

        @pl.when(more)
        def _():
            gather_z(r, q, side).start()

        @pl.when(by_x(r, q))
        def _():
            gather_x(r, q).start()

        gather_core(r, q, 0).start()

    def pass_meta(r, side, more):
        gather_meta(r, side).wait_recv()

        @pl.when(more)
        def _():
            gather_meta(r, side).start()

    def cross(r, q):
        here = tokens(q)
        given = kept[r, 1 - x, here] + core_in[r, 1 - x, here].astype(jnp.float32)
        x_out[r, here] = given.astype(x_out.dtype)
        reduce_x(r, q).start()

    def begin_cross(r, skip):
        reduce_core(r, 0).wait_recv()
        for q in reversed(range(CHUNKS)):

            @pl.when(jnp.logical_not(skip) if q == far_chunk else r >= 0)
            def _():
                cross(r, q)

        reduce_core(r, 1).wait_recv()
        total[r] = kept[r, x] + core_in[r, x].astype(jnp.float32)

    def product(r, x_of, core_of, table):
        features = column(x_of, core_of)
        return jnp.dot(acts[r, :, features], table[features, :], preferred_element_type=jnp.float32)

    def first_half(r):
        gate_sum[r] = product(r, x, core, gate_w)
        up_sum[r] = product(r, x, core, up_w)
        for q in range(CHUNKS):
            gather_core(r, q, 0).wait_recv()
        gate_sum[r] += product(r, x, 1 - core, gate_w)
        up_sum[r] += product(r, x, 1 - core, up_w)

    def second_half(r):
        gate_sum[r] += product(r, 1 - x, core, gate_w)
        up_sum[r] += product(r, 1 - x, core, up_w)
        for q in range(CHUNKS):
            gather_core(r, q, 1).wait_recv()
        gate_val = gate_sum[r] + product(r, 1 - x, 1 - core, gate_w)
        up_val = up_sum[r] + product(r, 1 - x, 1 - core, up_w)
        hidden = (gate_val / (1.0 + jnp.exp(-gate_val)) * up_val).astype(jnp.bfloat16)
        chosen = jnp.where(meta[r, :top] == expert.astype(jnp.float32), meta[r, top:], 0.0)
        weight = jnp.sum(jnp.transpose(chosen), axis=1, keepdims=True)

        def weighted(x_of, core_of):
            result = jnp.dot(hidden, down_w[:, column(x_of, core_of)], preferred_element_type=jnp.float32)
            return result * weight

        for which, x_of in enumerate((1 - x, x)):
            core_out[r, x_of] = weighted(x_of, 1 - core).astype(core_out.dtype)
            reduce_core(r, which).start()
        for x_of in (1 - x, x):
            kept[r, x_of] = weighted(x_of, core)

    def expert_step(s, carry):
        below, above = z - 1 - s, z + 1 + s
        from_below, from_above = below >= 0, above <= last
        for q in range(CHUNKS):

            @pl.when(from_below)
            def _():
                pass_on(below, q, 1, z < last)

            @pl.when(from_above)
            def _():
                pass_on(above, q, 0, z > 0)

        @pl.when(from_below)
        def _():
            pass_meta(below, 1, z < last)

        @pl.when(from_above)
        def _():
            pass_meta(above, 0, z > 0)

        r = nth_row(s)
        for q in range(CHUNKS):

            @pl.when(by_x(r, q))
            def _():
                gather_x(r, q).wait_recv()

                if q == far_chunk:
                    for i, (end, sends, _) in enumerate(ends):

                        @pl.when((s == 0) & (z == end) & sends)
                        def _():
                            gather_far(i).start()

                gather_core(r, q, 1, place(r, q, 1 - x, core)).start()

        for i, (end, sends, _) in enumerate(ends):

            @pl.when((s > 0) & ((z - s == end) if i == 0 else (z + s == end)))
            def _():
                gather_far(i).wait_recv()

                @pl.when(sends)
                def _():
                    gather_far(i).start()

                gather_core(end, far_chunk, 1, place(end, far_chunk, 1 - x, core)).start()

        @pl.when(s == 0)
        def _():
            weights[2].wait()

        if rows > 1:

            @pl.when(s == last)
            def _():
                begin_cross(z, at_end(z))

        second_half(r)

        @pl.when(s < last)
        def _():
            first_half(nth_row(s + 1))

        return carry

    for copy in weights[:2]:
        copy.wait()
    first_half(z)
    lax.fori_loop(0, rows, expert_step, 0)

    furthest = nth_row(last)
    begin_cross(furthest, furthest != z if rows > 1 else furthest < 0)

    def drain_gather(r, carry):
        for q in range(CHUNKS):

            @pl.when(by_x(r, q))
            def _():
                gather_x(r, q).wait_send()

            gather_core(r, q, 0).wait_send()
            gather_core(r, q, 1).wait_send()

        for side, sent in ((0, (r >= z) & (z > 0)), (1, (r <= z) & (z < last))):

            @pl.when(sent)
            def _():
                gather_meta(r, side).wait_send()
                for q in range(CHUNKS):
                    gather_z(r, q, side).wait_send()

        return carry

    def line_step(t, carry):
        r = nth_row(last - t)
        following = nth_row(last - t - 1)
        down, up = r < z, r > z
        first = (down & (z == last)) | (up & (z == 0))
        is_end = at_end(r)
        here_far = tokens(far_chunk)

        def send_on(q):
            z_out[r, tokens(q)] = total[r, tokens(q)].astype(z_out.dtype)

            @pl.when(down)
            def _():
                reduce_z(r, q, 0).start()

            @pl.when(up)
            def _():
                reduce_z(r, q, 1).start()

        def far_share():
            return kept[r, 1 - x, here_far] + core_in[r, 1 - x, here_far].astype(jnp.float32)

        for i, (end, _, _) in enumerate(ends):

            @pl.when(first & (r == end))
            def _():
                far_out[i] = far_share().astype(far_out.dtype)
                reduce_far(i).start()

        @pl.when(first & is_end)
        def _():
            send_on(far_chunk)

        @pl.when(t < last - 1)
        def _():
            reduce_core(following, 0).wait_recv()
            reduce_core(following, 1).wait_recv()

        for q in reversed(range(CHUNKS)):
            here = tokens(q)
            crosses = by_x(r, q)

            @pl.when(crosses)
            def _():
                reduce_x(r, q).wait_recv()

            @pl.when((t < last - 1) & by_x(following, q))
            def _():
                cross(following, q)

            @pl.when(crosses)
            def _():
                total[r, here] += x_in[r, here].astype(jnp.float32)

            @pl.when(first & crosses)
            def _():
                send_on(q)

        @pl.when(t < last - 1)
        def _():
            total[following] = kept[following, x] + core_in[following, x].astype(jnp.float32)

        for i, (end, _, _) in enumerate(ends):

            @pl.when((r == end) & jnp.logical_not(first))
            def _():
                reduce_far(i).wait_recv()
                far_out[i] = (far_share() + far_in[i].astype(jnp.float32)).astype(far_out.dtype)
                reduce_far(i).start()

        for q in reversed(range(CHUNKS)):
            here = tokens(q)

            @pl.when(down & (z < last))
            def _():
                reduce_z(r, q, 0).wait_recv()
                total[r, here] += z_in[0, r, here].astype(jnp.float32)
                send_on(q)

            @pl.when(up & (z > 0))
            def _():
                reduce_z(r, q, 1).wait_recv()
                total[r, here] += z_in[1, r, here].astype(jnp.float32)
                send_on(q)

        return carry

    lax.fori_loop(0, rows, drain_gather, 0)
    for i, (_, sends, _) in enumerate(ends):

        @pl.when(sends)
        def _():
            gather_far(i).wait_send()

    lax.fori_loop(0, last, line_step, 0)

    if rows > 1:
        here_far = tokens(far_chunk)
        for i, (end, _, _) in enumerate(ends):

            @pl.when(z == end)
            def _():
                reduce_far(i).wait_recv()
                given = kept[z, 1 - x, here_far] + core_in[z, 1 - x, here_far].astype(jnp.float32)
                x_out[z, here_far] = (given + far_in[i].astype(jnp.float32)).astype(x_out.dtype)
                reduce_x(z, far_chunk).start()

    for q in range(CHUNKS):
        here = tokens(q)
        reduce_x(z, q).wait_recv()
        total[z, here] += x_in[z, here].astype(jnp.float32)

        @pl.when(z < last)
        def _():
            reduce_z(z, q, 0).wait_recv()
            total[z, here] += z_in[0, z, here].astype(jnp.float32)

        @pl.when(z > 0)
        def _():
            reduce_z(z, q, 1).wait_recv()
            total[z, here] += z_in[1, z, here].astype(jnp.float32)

        out_ref[here] = total[z, here].astype(out_ref.dtype)

    def drain(r, carry):
        for which in range(2):
            reduce_core(r, which).wait_send()
        for q in range(CHUNKS):

            @pl.when(by_x(r, q))
            def _():
                reduce_x(r, q).wait_send()

            @pl.when(r != z)
            def _():
                reduce_z(r, q, 0).wait_send()

        return carry

    lax.fori_loop(0, rows, drain, 0)
    for i, (_, _, sends) in enumerate(ends):

        @pl.when(sends)
        def _():
            reduce_far(i).wait_send()


def dense_layer(activations, expert_ids, gate_scores, gate_proj, up_proj, down_proj):
    rows = lax.axis_size("row")
    group_rows, width = activations.shape
    model, hidden = gate_proj.shape[1:]
    top = expert_ids.shape[1]
    dtype = activations.dtype
    vmem = pl.BlockSpec(memory_space=pltpu.VMEM)
    anywhere = pl.BlockSpec(memory_space=pl.ANY)
    dma = pltpu.SemaphoreType.DMA
    flops = 6 * rows * group_rows * model * hidden
    return pl.pallas_call(
        functools.partial(dense_kernel, rows),
        out_shape=jax.ShapeDtypeStruct((group_rows, width), dtype),
        in_specs=[anywhere] * 6,
        out_specs=vmem,
        scratch_shapes=[
            pltpu.VMEM((rows, group_rows, model), dtype),
            pltpu.VMEM((top, group_rows), jnp.int32),
            pltpu.VMEM((rows, 2 * top, group_rows), jnp.float32),
            pltpu.VMEM((model, hidden), dtype),
            pltpu.VMEM((model, hidden), dtype),
            pltpu.VMEM((hidden, model), dtype),
            pltpu.VMEM((rows, group_rows, hidden), jnp.float32),
            pltpu.VMEM((rows, group_rows, hidden), jnp.float32),
            pltpu.VMEM((rows, PAIR, group_rows, width), jnp.float32),
            pltpu.VMEM((rows, PAIR, group_rows, width), dtype),
            pltpu.VMEM((rows, PAIR, group_rows, width), dtype),
            pltpu.VMEM((rows, group_rows, width), jnp.float32),
            pltpu.VMEM((rows, group_rows, width), dtype),
            pltpu.VMEM((rows, group_rows, width), dtype),
            pltpu.VMEM((rows, group_rows, width), dtype),
            pltpu.VMEM((PAIR, rows, group_rows, width), dtype),
            pltpu.VMEM((2, group_rows // CHUNKS, width), dtype),
            pltpu.VMEM((2, group_rows // CHUNKS, width), dtype),
            dma((3,)),
            dma((3,)),
            dma((2, rows, CHUNKS)),
            dma((rows, CHUNKS)),
            dma((2, rows)),
            dma((rows,)),
            dma((rows, CHUNKS)),
            dma((rows, CHUNKS)),
            dma((rows, 2, CHUNKS)),
            dma((rows, 2, CHUNKS)),
            dma((rows, 2)),
            dma((rows, 2)),
            dma((rows, CHUNKS)),
            dma((rows, CHUNKS)),
            dma((rows, CHUNKS)),
            dma((2, rows, CHUNKS)),
            dma((2,)),
            dma((2,)),
            dma((2,)),
            dma((2,)),
        ],
        compiler_params=pltpu.CompilerParams(
            collective_id=0, has_side_effects=True, vmem_limit_bytes=64 * 1024 * 1024
        ),
        cost_estimate=pl.CostEstimate(
            flops=flops, bytes_accessed=6 * model * hidden, transcendentals=rows * group_rows * hidden
        ),
    )(activations, expert_ids.T, gate_scores.T, gate_proj, up_proj, down_proj)


def either_way(*arrays):
    activations, expert_ids = arrays[:2]
    col_count, sub_count = lax.axis_size("col"), lax.axis_size("sub")
    experts = lax.axis_size("row") * col_count
    block_rows = expert_ids.shape[0] // (col_count * sub_count)
    every_row = 2 * block_rows * TOP // experts >= block_rows
    if every_row and sub_count == 1 and col_count == PAIR * PAIR:
        return dense_layer(*arrays)
    return per_device(*arrays)


def solution(mesh):
    placed = (
        P(("parts", "row"), ("col", "sub")),
        P(("parts", "row"), None),
        P(("parts", "row"), None),
        P(("row", "col"), None, "sub"),
        P(("row", "col"), None, "sub"),
        P(("row", "col"), "sub", None),
    )
    return jax.shard_map(
        either_way,
        mesh=mesh,
        in_specs=placed,
        out_specs=P(("parts", "row"), ("col", "sub")),
        check_vma=False,
    )
```

```python
import functools

import jax
import jax.numpy as jnp
from jax import lax
from jax.experimental import pallas as pl
from jax.experimental.pallas import tpu as pltpu
from jax.sharding import PartitionSpec as P

TOP = 8
PAIR = 2
CHUNKS = 2
MESH = pl.DeviceIdType.MESH


def slot_places(chosen, experts, capacity):
    count = chosen.shape[0] * chosen.shape[1]
    flat_ids = chosen.reshape(count)
    onehot = (flat_ids[:, None] == jnp.arange(experts, dtype=jnp.int32)[None, :]).astype(jnp.int32)
    running = jnp.cumsum(onehot, axis=0) - 1
    ranking = jnp.sum(onehot * running, axis=1)
    return flat_ids * capacity + ranking


def fill_slots(row_block, places, experts, capacity, top_count):
    owners = jnp.full((experts * capacity,), row_block.shape[0], jnp.int32)
    owners = owners.at[places].set(jnp.arange(places.shape[0], dtype=jnp.int32) // top_count)
    padded = jnp.concatenate(
        [row_block, jnp.zeros((1, row_block.shape[1]), row_block.dtype)], axis=0
    )
    return padded[owners].reshape(experts, capacity, row_block.shape[1])


def run_expert(stacked, gate_proj, up_proj, down_proj):
    layout = stacked.shape
    inputs = stacked.reshape(-1, layout[-1])
    gate_val = jnp.dot(inputs, gate_proj[0], preferred_element_type=jnp.float32)
    up_val = jnp.dot(inputs, up_proj[0], preferred_element_type=jnp.float32)
    hidden = (jax.nn.silu(gate_val) * up_val).astype(jnp.bfloat16)
    partial_out = jnp.dot(hidden, down_proj[0], preferred_element_type=jnp.float32)
    return partial_out.reshape(layout)


def send_back(stacked, gate_proj, up_proj, down_proj):
    partial_out = run_expert(stacked, gate_proj, up_proj, down_proj)
    landed = lax.all_to_all(partial_out, ("row", "col"), split_axis=1, concat_axis=1, tiled=True)
    return lax.psum_scatter(landed, "sub", scatter_dimension=0, tiled=True).astype(jnp.bfloat16)


def per_device(activations, expert_ids, gate_scores, gate_proj, up_proj, down_proj):
    col_count = lax.axis_size("col")
    sub_count = lax.axis_size("sub")
    experts = lax.axis_size("row") * col_count
    group_rows = expert_ids.shape[0]
    block_rows = group_rows // (col_count * sub_count)
    capacity = max(2, min(block_rows, 2 * block_rows * TOP // experts))
    quarter = sub_count * block_rows
    width = activations.shape[1] * col_count * sub_count
    whole = lax.all_gather(activations, ("col", "sub"), axis=1, tiled=True)
    col_start = lax.axis_index("col") * quarter
    sub_index = lax.axis_index("sub")
    my_rows = lax.dynamic_slice_in_dim(whole, col_start, quarter, 0)
    my_ids = lax.dynamic_slice_in_dim(expert_ids, col_start, quarter, 0)
    own_scores = lax.dynamic_slice_in_dim(
        gate_scores, col_start + sub_index * block_rows, block_rows, 0
    )
    places = []
    for member in range(sub_count):
        lower = member * block_rows
        places.append(slot_places(my_ids[lower : lower + block_rows], experts, capacity))
    own_places = lax.dynamic_index_in_dim(jnp.stack(places), sub_index, 0, keepdims=False)
    buffers = []
    for member in range(sub_count):
        lower = member * block_rows
        buffers.append(
            fill_slots(my_rows[lower : lower + block_rows], places[member], experts, capacity, TOP)
        )
    outgoing = jnp.stack(buffers)
    returned = send_back(
        lax.all_to_all(outgoing, ("row", "col"), split_axis=1, concat_axis=1, tiled=True),
        gate_proj,
        up_proj,
        down_proj,
    )
    picked = returned.reshape(-1, width)[own_places].reshape(block_rows, TOP, width)
    share = jnp.sum(own_scores[:, :, None] * picked.astype(jnp.float32), axis=1)
    return lax.all_to_all(
        share.astype(jnp.bfloat16), ("col", "sub"), split_axis=1, concat_axis=0, tiled=True
    )


def dense_kernel(
    rows,
    acts_hbm,
    ids_hbm,
    scores_hbm,
    gate_hbm,
    up_hbm,
    down_hbm,
    out_ref,
    acts,
    ids,
    meta,
    gate_w,
    up_w,
    down_w,
    gate_sum,
    up_sum,
    kept,
    core_out,
    core_in,
    total,
    x_out,
    x_in,
    z_out,
    z_in,
    far_out,
    far_in,
    weight_sem,
    own_sem,
    ag_z_send,
    ag_z_recv,
    meta_send,
    meta_recv,
    ag_x_send,
    ag_x_recv,
    ag_core_send,
    ag_core_recv,
    rs_core_send,
    rs_core_recv,
    rs_x_send,
    rs_x_recv,
    rs_z_send,
    rs_z_recv,
    ag_far_send,
    ag_far_recv,
    rs_far_send,
    rs_far_recv,
):
    top, group_rows = ids_hbm.shape
    part = group_rows // CHUNKS
    width = acts_hbm.shape[1]
    z = lax.axis_index("row")
    col = lax.axis_index("col")
    x, core = col // PAIR, col % PAIR
    expert = z * lax.axis_size("col") + col
    sibling = {"col": x * PAIR + (1 - core)}
    across = {"col": (1 - x) * PAIR + core}
    last = rows - 1

    far_chunk = CHUNKS - 1
    ends = ((0, z < last, z > 0), (last, z > 0, z < last))

    def at_end(r):
        return (r == 0) | (r == last)

    def by_x(r, q):
        return jnp.logical_not(at_end(r)) | (r == z) if q == far_chunk else r >= 0

    def column(x_of, core_of):
        return pl.ds(pl.multiple_of((x_of * PAIR + core_of) * width, width), width)

    def nth_row(s):
        both = jnp.minimum(z, last - z)
        ahead = jnp.where(z <= last - z, 1, -1)
        near = z + ahead * jnp.where(s % 2 == 1, (s + 1) // 2, -(s // 2))
        rest = jnp.where(z <= last - z, s, last - s)
        return jnp.where(s <= 2 * both, near, rest)

    def remote(src, dst, send, recv, device):
        return pltpu.make_async_remote_copy(
            src_ref=src, dst_ref=dst, send_sem=send, recv_sem=recv, device_id=device, device_id_type=MESH
        )

    def position(r, at):
        lower = at <= last - at
        away = jnp.abs(r - at)
        forward = jnp.where(lower, r > at, r < at)
        both = 2 * away - jnp.where(forward, 1, 0)
        return jnp.where(away <= jnp.minimum(at, last - at), both, jnp.where(lower, r, last - r))

    def tokens(q):
        return pl.ds(q * part, part)

    def place(r, q, x_of, core_of, at=None):
        slot = position(r, z if at is None else at)
        return acts.at[slot, tokens(q), column(x_of, core_of)]

    def chunk_of(q):
        return acts_hbm.at[tokens(q)]

    def gather_z(r, q, side, src=None):
        to = jnp.clip(z + 2 * side - 1, 0, last)
        return remote(
            place(r, q, x, core) if src is None else src,
            place(r, q, x, core, to),
            ag_z_send.at[side, r, q],
            ag_z_recv.at[r, q],
            {"row": z + 2 * side - 1},
        )

    def gather_meta(r, side):
        return remote(
            meta.at[r], meta.at[r], meta_send.at[side, r], meta_recv.at[r], {"row": z + 2 * side - 1}
        )

    def gather_x(r, q, src=None):
        there = place(r, q, x, core)
        return remote(there if src is None else src, there, ag_x_send.at[r, q], ag_x_recv.at[r, q], across)

    def gather_core(r, q, which, src=None):
        there = place(r, q, x if which == 0 else 1 - x, core)
        return remote(
            there if src is None else src,
            there,
            ag_core_send.at[r, which, q],
            ag_core_recv.at[r, which, q],
            sibling,
        )

    def reduce_core(r, which):
        x_of = 1 - x if which == 0 else x
        return remote(
            core_out.at[r, x_of],
            core_in.at[r, x_of],
            rs_core_send.at[r, which],
            rs_core_recv.at[r, which],
            sibling,
        )

    def reduce_x(r, q):
        return remote(
            x_out.at[r, tokens(q)], x_in.at[r, tokens(q)], rs_x_send.at[r, q], rs_x_recv.at[r, q], across
        )

    def reduce_z(r, q, side):
        return remote(
            z_out.at[r, tokens(q)],
            z_in.at[side, r, tokens(q)],
            rs_z_send.at[r, q],
            rs_z_recv.at[side, r, q],
            {"row": z + 2 * side - 1},
        )

    def gather_far(i):
        end, to = ends[i][0], jnp.clip(z + 1 - 2 * i, 0, last)
        here, there = place(end, far_chunk, 1 - x, core), place(end, far_chunk, 1 - x, core, to)
        return remote(here, there, ag_far_send.at[i], ag_far_recv.at[i], {"row": z + 1 - 2 * i})

    def reduce_far(i):
        return remote(
            far_out.at[i], far_in.at[i], rs_far_send.at[i], rs_far_recv.at[i], {"row": z + 2 * i - 1}
        )

    weights = [
        pltpu.make_async_copy(src.at[0], dst, weight_sem.at[i])
        for i, (src, dst) in enumerate(((gate_hbm, gate_w), (up_hbm, up_w), (down_hbm, down_w)))
    ]

    own = pltpu.make_async_copy(acts_hbm, acts.at[0, :, column(x, core)], own_sem.at[0])
    own_ids = pltpu.make_async_copy(ids_hbm, ids, own_sem.at[1])
    own_scores = pltpu.make_async_copy(scores_hbm, meta.at[z, pl.ds(top, top)], own_sem.at[2])
    for copy in [own, own_ids, own_scores] + weights:
        copy.start()

    barrier = pltpu.get_barrier_semaphore()
    pl.semaphore_signal(barrier, inc=1, device_id=sibling, device_id_type=MESH)
    pl.semaphore_signal(barrier, inc=1, device_id=across, device_id_type=MESH)

    @pl.when(z > 0)
    def _():
        pl.semaphore_signal(barrier, inc=1, device_id={"row": z - 1}, device_id_type=MESH)

    @pl.when(z < last)
    def _():
        pl.semaphore_signal(barrier, inc=1, device_id={"row": z + 1}, device_id_type=MESH)

    pl.semaphore_wait(barrier, 2 + jnp.where(z > 0, 1, 0) + jnp.where(z < last, 1, 0))

    for q in range(CHUNKS):
        gather_x(z, q, chunk_of(q)).start()

        @pl.when(z > 0)
        def _():
            gather_z(z, q, 0, chunk_of(q)).start()

        @pl.when(z < last)
        def _():
            gather_z(z, q, 1, chunk_of(q)).start()

    for q in range(CHUNKS):
        gather_core(z, q, 0, chunk_of(q)).start()
    own_ids.wait()
    own_scores.wait()
    meta[z, :top] = ids[...].astype(jnp.float32)

    @pl.when(z > 0)
    def _():
        gather_meta(z, 0).start()

    @pl.when(z < last)
    def _():
        gather_meta(z, 1).start()

    own.wait()

    def pass_on(r, q, side, more):
        gather_z(r, q, side).wait_recv()

        @pl.when(more)
        def _():
            gather_z(r, q, side).start()

        @pl.when(by_x(r, q))
        def _():
            gather_x(r, q).start()

        gather_core(r, q, 0).start()

    def pass_meta(r, side, more):
        gather_meta(r, side).wait_recv()

        @pl.when(more)
        def _():
            gather_meta(r, side).start()

    def cross(r, q):
        here = tokens(q)
        given = kept[r, 1 - x, here] + core_in[r, 1 - x, here].astype(jnp.float32)
        x_out[r, here] = given.astype(x_out.dtype)
        reduce_x(r, q).start()

    def begin_cross(r, skip):
        reduce_core(r, 0).wait_recv()
        for q in reversed(range(CHUNKS)):

            @pl.when(jnp.logical_not(skip) if q == far_chunk else r >= 0)
            def _():
                cross(r, q)

        reduce_core(r, 1).wait_recv()
        total[r] = kept[r, x] + core_in[r, x].astype(jnp.float32)

    batch = 2 if rows % 2 == 0 else 1
    half = PAIR * width

    def product(b, x_of, table):
        features = pl.ds(pl.multiple_of(x_of * half, half), half)
        block = acts[pl.ds(b * batch, batch), :, features].reshape(batch * group_rows, half)
        return jnp.dot(block, table[features, :], preferred_element_type=jnp.float32)

    def first_half(b):
        for j in range(batch):
            for q in range(CHUNKS):
                gather_core(nth_row(b * batch + j), q, 0).wait_recv()
        gate_sum[...] = product(b, x, gate_w)
        up_sum[...] = product(b, x, up_w)

    def second_half(b):
        members = [nth_row(b * batch + j) for j in range(batch)]
        for r in members:
            for q in range(CHUNKS):
                gather_core(r, q, 1).wait_recv()
        gate_val = gate_sum[...] + product(b, 1 - x, gate_w)
        up_val = up_sum[...] + product(b, 1 - x, up_w)
        hidden = (gate_val / (1.0 + jnp.exp(-gate_val)) * up_val).astype(jnp.bfloat16)
        scales = []
        for r in members:
            chosen = jnp.where(meta[r, :top] == expert.astype(jnp.float32), meta[r, top:], 0.0)
            scales.append(jnp.sum(jnp.transpose(chosen), axis=1, keepdims=True))

        def weighted(x_of, core_of):
            result = jnp.dot(hidden, down_w[:, column(x_of, core_of)], preferred_element_type=jnp.float32)
            result = result.reshape(batch, group_rows, width)
            return [(r, result[j] * scales[j]) for j, r in enumerate(members)]

        for which, x_of in enumerate((1 - x, x)):
            for r, result in weighted(x_of, 1 - core):
                core_out[r, x_of] = result.astype(core_out.dtype)
            for r in reversed(members):
                reduce_core(r, which).start()
        for x_of in (1 - x, x):
            for r, result in weighted(x_of, core):
                kept[r, x_of] = result

    def arrivals(s):
        below, above = z - 1 - s, z + 1 + s
        from_below, from_above = below >= 0, above <= last
        for q in range(CHUNKS):

            @pl.when(from_below)
            def _():
                pass_on(below, q, 1, z < last)

            @pl.when(from_above)
            def _():
                pass_on(above, q, 0, z > 0)

        @pl.when(from_below)
        def _():
            pass_meta(below, 1, z < last)

        @pl.when(from_above)
        def _():
            pass_meta(above, 0, z > 0)

        r = nth_row(s)
        for q in range(CHUNKS):

            @pl.when(by_x(r, q))
            def _():
                gather_x(r, q).wait_recv()

                if q == far_chunk:
                    for i, (end, sends, _) in enumerate(ends):

                        @pl.when((s == 0) & (z == end) & sends)
                        def _():
                            gather_far(i).start()

                gather_core(r, q, 1, place(r, q, 1 - x, core)).start()

        for i, (end, sends, _) in enumerate(ends):

            @pl.when((s > 0) & ((z - s == end) if i == 0 else (z + s == end)))
            def _():
                gather_far(i).wait_recv()

                @pl.when(sends)
                def _():
                    gather_far(i).start()

                gather_core(end, far_chunk, 1, place(end, far_chunk, 1 - x, core)).start()

    def expert_step(b, carry):
        for j in range(batch):
            arrivals(b * batch + j)
            if j == max(0, batch - 2):

                @pl.when(b == 0)
                def _():
                    for copy in weights:
                        copy.wait()

                first_half(b)
        if rows > batch:

            @pl.when(b == rows // batch - 1)
            def _():
                begin_cross(z, at_end(z))

        second_half(b)
        return carry

    lax.fori_loop(0, rows // batch, expert_step, 0)

    if rows == batch and rows > 1:
        begin_cross(z, at_end(z))

    furthest = nth_row(last)
    begin_cross(furthest, furthest != z if rows > 1 else furthest < 0)

    def drain_gather(r, carry):
        for q in range(CHUNKS):

            @pl.when(by_x(r, q))
            def _():
                gather_x(r, q).wait_send()

            gather_core(r, q, 0).wait_send()
            gather_core(r, q, 1).wait_send()

        for side, sent in ((0, (r >= z) & (z > 0)), (1, (r <= z) & (z < last))):

            @pl.when(sent)
            def _():
                gather_meta(r, side).wait_send()
                for q in range(CHUNKS):
                    gather_z(r, q, side).wait_send()

        return carry

    def line_step(t, carry):
        r = nth_row(last - t)
        following = nth_row(last - t - 1)
        down, up = r < z, r > z
        first = (down & (z == last)) | (up & (z == 0))
        is_end = at_end(r)
        here_far = tokens(far_chunk)

        def send_on(q):
            z_out[r, tokens(q)] = total[r, tokens(q)].astype(z_out.dtype)

            @pl.when(down)
            def _():
                reduce_z(r, q, 0).start()

            @pl.when(up)
            def _():
                reduce_z(r, q, 1).start()

        def far_share():
            return kept[r, 1 - x, here_far] + core_in[r, 1 - x, here_far].astype(jnp.float32)

        for i, (end, _, _) in enumerate(ends):

            @pl.when(first & (r == end))
            def _():
                far_out[i] = far_share().astype(far_out.dtype)
                reduce_far(i).start()

        @pl.when(first & is_end)
        def _():
            send_on(far_chunk)

        @pl.when(t < last - 1)
        def _():
            reduce_core(following, 0).wait_recv()
            reduce_core(following, 1).wait_recv()

        for q in reversed(range(CHUNKS)):
            here = tokens(q)
            crosses = by_x(r, q)

            @pl.when(crosses)
            def _():
                reduce_x(r, q).wait_recv()

            @pl.when((t < last - 1) & by_x(following, q))
            def _():
                cross(following, q)

            @pl.when(crosses)
            def _():
                total[r, here] += x_in[r, here].astype(jnp.float32)

            @pl.when(first & crosses)
            def _():
                send_on(q)

        @pl.when(t < last - 1)
        def _():
            total[following] = kept[following, x] + core_in[following, x].astype(jnp.float32)

        for i, (end, _, _) in enumerate(ends):

            @pl.when((r == end) & jnp.logical_not(first))
            def _():
                reduce_far(i).wait_recv()
                far_out[i] = (far_share() + far_in[i].astype(jnp.float32)).astype(far_out.dtype)
                reduce_far(i).start()

        for q in reversed(range(CHUNKS)):
            here = tokens(q)

            @pl.when(down & (z < last))
            def _():
                reduce_z(r, q, 0).wait_recv()
                total[r, here] += z_in[0, r, here].astype(jnp.float32)
                send_on(q)

            @pl.when(up & (z > 0))
            def _():
                reduce_z(r, q, 1).wait_recv()
                total[r, here] += z_in[1, r, here].astype(jnp.float32)
                send_on(q)

        return carry

    lax.fori_loop(0, rows, drain_gather, 0)
    for i, (_, sends, _) in enumerate(ends):

        @pl.when(sends)
        def _():
            gather_far(i).wait_send()

    lax.fori_loop(0, last, line_step, 0)

    if rows > 1:
        here_far = tokens(far_chunk)
        for i, (end, _, _) in enumerate(ends):

            @pl.when(z == end)
            def _():
                reduce_far(i).wait_recv()
                given = kept[z, 1 - x, here_far] + core_in[z, 1 - x, here_far].astype(jnp.float32)
                x_out[z, here_far] = (given + far_in[i].astype(jnp.float32)).astype(x_out.dtype)
                reduce_x(z, far_chunk).start()

    for q in range(CHUNKS):
        here = tokens(q)
        reduce_x(z, q).wait_recv()
        total[z, here] += x_in[z, here].astype(jnp.float32)

        @pl.when(z < last)
        def _():
            reduce_z(z, q, 0).wait_recv()
            total[z, here] += z_in[0, z, here].astype(jnp.float32)

        @pl.when(z > 0)
        def _():
            reduce_z(z, q, 1).wait_recv()
            total[z, here] += z_in[1, z, here].astype(jnp.float32)

        out_ref[here] = total[z, here].astype(out_ref.dtype)

    def drain(r, carry):
        for which in range(2):
            reduce_core(r, which).wait_send()
        for q in range(CHUNKS):

            @pl.when(by_x(r, q))
            def _():
                reduce_x(r, q).wait_send()

            @pl.when(r != z)
            def _():
                reduce_z(r, q, 0).wait_send()

        return carry

    lax.fori_loop(0, rows, drain, 0)
    for i, (_, _, sends) in enumerate(ends):

        @pl.when(sends)
        def _():
            reduce_far(i).wait_send()


def dense_layer(activations, expert_ids, gate_scores, gate_proj, up_proj, down_proj):
    rows = lax.axis_size("row")
    group_rows, width = activations.shape
    model, hidden = gate_proj.shape[1:]
    top = expert_ids.shape[1]
    dtype = activations.dtype
    vmem = pl.BlockSpec(memory_space=pltpu.VMEM)
    anywhere = pl.BlockSpec(memory_space=pl.ANY)
    dma = pltpu.SemaphoreType.DMA
    batch = 2 if rows % 2 == 0 else 1
    flops = 6 * rows * group_rows * model * hidden
    return pl.pallas_call(
        functools.partial(dense_kernel, rows),
        out_shape=jax.ShapeDtypeStruct((group_rows, width), dtype),
        in_specs=[anywhere] * 6,
        out_specs=vmem,
        scratch_shapes=[
            pltpu.VMEM((rows, group_rows, model), dtype),
            pltpu.VMEM((top, group_rows), jnp.int32),
            pltpu.VMEM((rows, 2 * top, group_rows), jnp.float32),
            pltpu.VMEM((model, hidden), dtype),
            pltpu.VMEM((model, hidden), dtype),
            pltpu.VMEM((hidden, model), dtype),
            pltpu.VMEM((batch * group_rows, hidden), jnp.float32),
            pltpu.VMEM((batch * group_rows, hidden), jnp.float32),
            pltpu.VMEM((rows, PAIR, group_rows, width), jnp.float32),
            pltpu.VMEM((rows, PAIR, group_rows, width), dtype),
            pltpu.VMEM((rows, PAIR, group_rows, width), dtype),
            pltpu.VMEM((rows, group_rows, width), jnp.float32),
            pltpu.VMEM((rows, group_rows, width), dtype),
            pltpu.VMEM((rows, group_rows, width), dtype),
            pltpu.VMEM((rows, group_rows, width), dtype),
            pltpu.VMEM((PAIR, rows, group_rows, width), dtype),
            pltpu.VMEM((2, group_rows // CHUNKS, width), dtype),
            pltpu.VMEM((2, group_rows // CHUNKS, width), dtype),
            dma((3,)),
            dma((3,)),
            dma((2, rows, CHUNKS)),
            dma((rows, CHUNKS)),
            dma((2, rows)),
            dma((rows,)),
            dma((rows, CHUNKS)),
            dma((rows, CHUNKS)),
            dma((rows, 2, CHUNKS)),
            dma((rows, 2, CHUNKS)),
            dma((rows, 2)),
            dma((rows, 2)),
            dma((rows, CHUNKS)),
            dma((rows, CHUNKS)),
            dma((rows, CHUNKS)),
            dma((2, rows, CHUNKS)),
            dma((2,)),
            dma((2,)),
            dma((2,)),
            dma((2,)),
        ],
        compiler_params=pltpu.CompilerParams(
            collective_id=0, has_side_effects=True, vmem_limit_bytes=64 * 1024 * 1024
        ),
        cost_estimate=pl.CostEstimate(
            flops=flops, bytes_accessed=6 * model * hidden, transcendentals=rows * group_rows * hidden
        ),
    )(activations, expert_ids.T, gate_scores.T, gate_proj, up_proj, down_proj)


def either_way(*arrays):
    activations, expert_ids = arrays[:2]
    col_count, sub_count = lax.axis_size("col"), lax.axis_size("sub")
    experts = lax.axis_size("row") * col_count
    block_rows = expert_ids.shape[0] // (col_count * sub_count)
    every_row = 2 * block_rows * TOP // experts >= block_rows
    if every_row and sub_count == 1 and col_count == PAIR * PAIR:
        return dense_layer(*arrays)
    return per_device(*arrays)


def solution(mesh):
    placed = (
        P(("parts", "row"), ("col", "sub")),
        P(("parts", "row"), None),
        P(("parts", "row"), None),
        P(("row", "col"), None, "sub"),
        P(("row", "col"), None, "sub"),
        P(("row", "col"), "sub", None),
    )
    return jax.shard_map(
        either_way,
        mesh=mesh,
        in_specs=placed,
        out_specs=P(("parts", "row"), ("col", "sub")),
        check_vma=False,
    )
```

```python
import functools

import jax
import jax.numpy as jnp
from jax import lax
from jax.experimental import pallas as pl
from jax.experimental.pallas import tpu as pltpu
from jax.sharding import PartitionSpec as P

TOP = 8
PAIR = 2
CHUNKS = 2
MESH = pl.DeviceIdType.MESH


def slot_places(chosen, experts, capacity):
    count = chosen.shape[0] * chosen.shape[1]
    flat_ids = chosen.reshape(count)
    onehot = (flat_ids[:, None] == jnp.arange(experts, dtype=jnp.int32)[None, :]).astype(jnp.int32)
    running = jnp.cumsum(onehot, axis=0) - 1
    ranking = jnp.sum(onehot * running, axis=1)
    return flat_ids * capacity + ranking


def fill_slots(row_block, places, experts, capacity, top_count):
    owners = jnp.full((experts * capacity,), row_block.shape[0], jnp.int32)
    owners = owners.at[places].set(jnp.arange(places.shape[0], dtype=jnp.int32) // top_count)
    padded = jnp.concatenate(
        [row_block, jnp.zeros((1, row_block.shape[1]), row_block.dtype)], axis=0
    )
    return padded[owners].reshape(experts, capacity, row_block.shape[1])


def run_expert(stacked, gate_proj, up_proj, down_proj):
    layout = stacked.shape
    inputs = stacked.reshape(-1, layout[-1])
    gate_val = jnp.dot(inputs, gate_proj[0], preferred_element_type=jnp.float32)
    up_val = jnp.dot(inputs, up_proj[0], preferred_element_type=jnp.float32)
    hidden = (jax.nn.silu(gate_val) * up_val).astype(jnp.bfloat16)
    partial_out = jnp.dot(hidden, down_proj[0], preferred_element_type=jnp.float32)
    return partial_out.reshape(layout)


def send_back(stacked, gate_proj, up_proj, down_proj):
    partial_out = run_expert(stacked, gate_proj, up_proj, down_proj)
    landed = lax.all_to_all(partial_out, ("row", "col"), split_axis=1, concat_axis=1, tiled=True)
    return lax.psum_scatter(landed, "sub", scatter_dimension=0, tiled=True).astype(jnp.bfloat16)


def per_device(activations, expert_ids, gate_scores, gate_proj, up_proj, down_proj):
    col_count = lax.axis_size("col")
    sub_count = lax.axis_size("sub")
    experts = lax.axis_size("row") * col_count
    group_rows = expert_ids.shape[0]
    block_rows = group_rows // (col_count * sub_count)
    capacity = max(2, min(block_rows, 2 * block_rows * TOP // experts))
    quarter = sub_count * block_rows
    width = activations.shape[1] * col_count * sub_count
    whole = lax.all_gather(activations, ("col", "sub"), axis=1, tiled=True)
    col_start = lax.axis_index("col") * quarter
    sub_index = lax.axis_index("sub")
    my_rows = lax.dynamic_slice_in_dim(whole, col_start, quarter, 0)
    my_ids = lax.dynamic_slice_in_dim(expert_ids, col_start, quarter, 0)
    own_scores = lax.dynamic_slice_in_dim(
        gate_scores, col_start + sub_index * block_rows, block_rows, 0
    )
    places = []
    for member in range(sub_count):
        lower = member * block_rows
        places.append(slot_places(my_ids[lower : lower + block_rows], experts, capacity))
    own_places = lax.dynamic_index_in_dim(jnp.stack(places), sub_index, 0, keepdims=False)
    buffers = []
    for member in range(sub_count):
        lower = member * block_rows
        buffers.append(
            fill_slots(my_rows[lower : lower + block_rows], places[member], experts, capacity, TOP)
        )
    outgoing = jnp.stack(buffers)
    returned = send_back(
        lax.all_to_all(outgoing, ("row", "col"), split_axis=1, concat_axis=1, tiled=True),
        gate_proj,
        up_proj,
        down_proj,
    )
    picked = returned.reshape(-1, width)[own_places].reshape(block_rows, TOP, width)
    share = jnp.sum(own_scores[:, :, None] * picked.astype(jnp.float32), axis=1)
    return lax.all_to_all(
        share.astype(jnp.bfloat16), ("col", "sub"), split_axis=1, concat_axis=0, tiled=True
    )


def dense_kernel(
    rows,
    acts_hbm,
    ids_hbm,
    scores_hbm,
    gate_hbm,
    up_hbm,
    down_hbm,
    out_ref,
    acts,
    ids,
    meta,
    gate_w,
    up_w,
    down_w,
    gate_sum,
    up_sum,
    kept,
    core_out,
    core_in,
    total,
    x_out,
    x_in,
    z_out,
    z_in,
    far_out,
    far_in,
    weight_sem,
    own_sem,
    ag_z_send,
    ag_z_recv,
    meta_send,
    meta_recv,
    ag_x_send,
    ag_x_recv,
    ag_core_send,
    ag_core_recv,
    rs_core_send,
    rs_core_recv,
    rs_x_send,
    rs_x_recv,
    rs_z_send,
    rs_z_recv,
    ag_far_send,
    ag_far_recv,
    rs_far_send,
    rs_far_recv,
):
    top, group_rows = ids_hbm.shape
    part = group_rows // CHUNKS
    width = acts_hbm.shape[1]
    z = lax.axis_index("row")
    col = lax.axis_index("col")
    x, core = col // PAIR, col % PAIR
    expert = z * lax.axis_size("col") + col
    sibling = {"col": x * PAIR + (1 - core)}
    across = {"col": (1 - x) * PAIR + core}
    last = rows - 1

    far_chunk = CHUNKS - 1
    ends = ((0, z < last, z > 0), (last, z > 0, z < last))

    def at_end(r):
        return (r == 0) | (r == last)

    def by_x(r, q):
        return jnp.logical_not(at_end(r)) | (r == z) if q == far_chunk else r >= 0

    def column(x_of, core_of):
        return pl.ds(pl.multiple_of((x_of * PAIR + core_of) * width, width), width)

    def nth_row(s):
        both = jnp.minimum(z, last - z)
        ahead = jnp.where(z <= last - z, 1, -1)
        near = z + ahead * jnp.where(s % 2 == 1, (s + 1) // 2, -(s // 2))
        rest = jnp.where(z <= last - z, s, last - s)
        return jnp.where(s <= 2 * both, near, rest)

    def remote(src, dst, send, recv, device):
        return pltpu.make_async_remote_copy(
            src_ref=src, dst_ref=dst, send_sem=send, recv_sem=recv, device_id=device, device_id_type=MESH
        )

    def position(r, at):
        lower = at <= last - at
        away = jnp.abs(r - at)
        forward = jnp.where(lower, r > at, r < at)
        both = 2 * away - jnp.where(forward, 1, 0)
        return jnp.where(away <= jnp.minimum(at, last - at), both, jnp.where(lower, r, last - r))

    def tokens(q):
        return pl.ds(q * part, part)

    def place(r, q, x_of, core_of, at=None):
        slot = position(r, z if at is None else at)
        return acts.at[slot, tokens(q), column(x_of, core_of)]

    def chunk_of(q):
        return acts_hbm.at[tokens(q)]

    def gather_z(r, q, side, src=None):
        to = jnp.clip(z + 2 * side - 1, 0, last)
        return remote(
            place(r, q, x, core) if src is None else src,
            place(r, q, x, core, to),
            ag_z_send.at[side, r, q],
            ag_z_recv.at[r, q],
            {"row": z + 2 * side - 1},
        )

    def gather_meta(r, side):
        return remote(
            meta.at[r], meta.at[r], meta_send.at[side, r], meta_recv.at[r], {"row": z + 2 * side - 1}
        )

    def gather_x(r, q, src=None):
        there = place(r, q, x, core)
        return remote(there if src is None else src, there, ag_x_send.at[r, q], ag_x_recv.at[r, q], across)

    def gather_core(r, q, which, src=None):
        there = place(r, q, x if which == 0 else 1 - x, core)
        return remote(
            there if src is None else src,
            there,
            ag_core_send.at[r, which, q],
            ag_core_recv.at[r, which, q],
            sibling,
        )

    def reduce_core(r, which):
        x_of = 1 - x if which == 0 else x
        return remote(
            core_out.at[r, x_of],
            core_in.at[r, x_of],
            rs_core_send.at[r, which],
            rs_core_recv.at[r, which],
            sibling,
        )

    def reduce_x(r, q):
        return remote(
            x_out.at[r, tokens(q)], x_in.at[r, tokens(q)], rs_x_send.at[r, q], rs_x_recv.at[r, q], across
        )

    def reduce_z(r, q, side):
        return remote(
            z_out.at[r, tokens(q)],
            z_in.at[side, r, tokens(q)],
            rs_z_send.at[r, q],
            rs_z_recv.at[side, r, q],
            {"row": z + 2 * side - 1},
        )

    def gather_far(i):
        end, to = ends[i][0], jnp.clip(z + 1 - 2 * i, 0, last)
        here, there = place(end, far_chunk, 1 - x, core), place(end, far_chunk, 1 - x, core, to)
        return remote(here, there, ag_far_send.at[i], ag_far_recv.at[i], {"row": z + 1 - 2 * i})

    def reduce_far(i):
        return remote(
            far_out.at[i], far_in.at[i], rs_far_send.at[i], rs_far_recv.at[i], {"row": z + 2 * i - 1}
        )

    weights = [
        pltpu.make_async_copy(src.at[0], dst, weight_sem.at[i])
        for i, (src, dst) in enumerate(((gate_hbm, gate_w), (up_hbm, up_w), (down_hbm, down_w)))
    ]

    own = pltpu.make_async_copy(acts_hbm, acts.at[0, :, column(x, core)], own_sem.at[0])
    own_ids = pltpu.make_async_copy(ids_hbm, ids, own_sem.at[1])
    own_scores = pltpu.make_async_copy(scores_hbm, meta.at[z, pl.ds(top, top)], own_sem.at[2])
    for copy in [own, own_ids, own_scores] + weights:
        copy.start()

    barrier = pltpu.get_barrier_semaphore()
    pl.semaphore_signal(barrier, inc=1, device_id=sibling, device_id_type=MESH)
    pl.semaphore_signal(barrier, inc=1, device_id=across, device_id_type=MESH)

    @pl.when(z > 0)
    def _():
        pl.semaphore_signal(barrier, inc=1, device_id={"row": z - 1}, device_id_type=MESH)

    @pl.when(z < last)
    def _():
        pl.semaphore_signal(barrier, inc=1, device_id={"row": z + 1}, device_id_type=MESH)

    pl.semaphore_wait(barrier, 2 + jnp.where(z > 0, 1, 0) + jnp.where(z < last, 1, 0))

    for q in range(CHUNKS):
        gather_x(z, q, chunk_of(q)).start()

        @pl.when(z > 0)
        def _():
            gather_z(z, q, 0, chunk_of(q)).start()

        @pl.when(z < last)
        def _():
            gather_z(z, q, 1, chunk_of(q)).start()

    for q in range(CHUNKS):
        gather_core(z, q, 0, chunk_of(q)).start()
    own_ids.wait()
    own_scores.wait()
    meta[z, :top] = ids[...].astype(jnp.float32)

    @pl.when(z > 0)
    def _():
        gather_meta(z, 0).start()

    @pl.when(z < last)
    def _():
        gather_meta(z, 1).start()

    own.wait()

    def pass_on(r, q, side, more):
        gather_z(r, q, side).wait_recv()

        @pl.when(more)
        def _():
            gather_z(r, q, side).start()

        @pl.when(by_x(r, q))
        def _():
            gather_x(r, q).start()

        gather_core(r, q, 0).start()

    def pass_meta(r, side, more):
        gather_meta(r, side).wait_recv()

        @pl.when(more)
        def _():
            gather_meta(r, side).start()

    def cross(r, q):
        here = tokens(q)
        given = kept[r, 1 - x, here] + core_in[r, 1 - x, here].astype(jnp.float32)
        x_out[r, here] = given.astype(x_out.dtype)
        reduce_x(r, q).start()

    def begin_cross(r, skip):
        reduce_core(r, 0).wait_recv()
        for q in reversed(range(CHUNKS)):

            @pl.when(jnp.logical_not(skip) if q == far_chunk else r >= 0)
            def _():
                cross(r, q)

        reduce_core(r, 1).wait_recv()
        total[r] = kept[r, x] + core_in[r, x].astype(jnp.float32)

    batch = 2 if rows % 2 == 0 else 1
    half = PAIR * width

    def product(b, x_of, table):
        features = pl.ds(pl.multiple_of(x_of * half, half), half)
        block = acts[pl.ds(b * batch, batch), :, features].reshape(batch * group_rows, half)
        return jnp.dot(block, table[features, :], preferred_element_type=jnp.float32)

    def first_half(b):
        for j in range(batch):
            for q in range(CHUNKS):
                gather_core(nth_row(b * batch + j), q, 0).wait_recv()
        gate_sum[...] = product(b, x, gate_w)
        up_sum[...] = product(b, x, up_w)

    def second_half(b):
        members = [nth_row(b * batch + j) for j in range(batch)]
        for r in members:
            for q in range(CHUNKS):
                gather_core(r, q, 1).wait_recv()
        gate_val = gate_sum[...] + product(b, 1 - x, gate_w)
        up_val = up_sum[...] + product(b, 1 - x, up_w)
        hidden = (gate_val / (1.0 + jnp.exp(-gate_val)) * up_val).astype(jnp.bfloat16)
        scales = []
        for r in members:
            chosen = jnp.where(meta[r, :top] == expert.astype(jnp.float32), meta[r, top:], 0.0)
            scales.append(jnp.sum(jnp.transpose(chosen), axis=1, keepdims=True))

        def weighted(x_of, core_of):
            result = jnp.dot(hidden, down_w[:, column(x_of, core_of)], preferred_element_type=jnp.float32)
            result = result.reshape(batch, group_rows, width)
            return [(r, result[j] * scales[j]) for j, r in enumerate(members)]

        for which, x_of in enumerate((1 - x, x)):
            for r, result in weighted(x_of, 1 - core):
                core_out[r, x_of] = result.astype(core_out.dtype)
            for r in reversed(members):
                reduce_core(r, which).start()
        for x_of in (1 - x, x):
            for r, result in weighted(x_of, core):
                kept[r, x_of] = result

    def arrivals(s):
        below, above = z - 1 - s, z + 1 + s
        from_below, from_above = below >= 0, above <= last
        for q in range(CHUNKS):

            @pl.when(from_below)
            def _():
                pass_on(below, q, 1, z < last)

            @pl.when(from_above)
            def _():
                pass_on(above, q, 0, z > 0)

        @pl.when(from_below)
        def _():
            pass_meta(below, 1, z < last)

        @pl.when(from_above)
        def _():
            pass_meta(above, 0, z > 0)

        r = nth_row(s)
        for q in range(CHUNKS):

            @pl.when(by_x(r, q))
            def _():
                gather_x(r, q).wait_recv()

                if q == far_chunk:
                    for i, (end, sends, _) in enumerate(ends):

                        @pl.when((s == 0) & (z == end) & sends)
                        def _():
                            gather_far(i).start()

                gather_core(r, q, 1, place(r, q, 1 - x, core)).start()

        for i, (end, sends, _) in enumerate(ends):

            @pl.when((s > 0) & ((z - s == end) if i == 0 else (z + s == end)))
            def _():
                gather_far(i).wait_recv()

                @pl.when(sends)
                def _():
                    gather_far(i).start()

                gather_core(end, far_chunk, 1, place(end, far_chunk, 1 - x, core)).start()

    early = rows > batch
    nearest = nth_row(min(1, last))

    def expert_step(b, carry):
        for j in range(batch):
            arrivals(b * batch + j)
            if j == max(0, batch - 2):

                @pl.when(b == 0)
                def _():
                    for copy in weights:
                        copy.wait()

                first_half(b)
                if early:

                    @pl.when(b == rows // batch - 1)
                    def _():
                        begin_cross(z, at_end(z))
                        begin_cross(nearest, at_end(nearest))

        second_half(b)
        return carry

    lax.fori_loop(0, rows // batch, expert_step, 0)

    if not early and rows > 1:
        begin_cross(z, at_end(z))

    def drain_gather(r, carry):
        for q in range(CHUNKS):

            @pl.when(by_x(r, q))
            def _():
                gather_x(r, q).wait_send()

            gather_core(r, q, 0).wait_send()
            gather_core(r, q, 1).wait_send()

        for side, sent in ((0, (r >= z) & (z > 0)), (1, (r <= z) & (z < last))):

            @pl.when(sent)
            def _():
                gather_meta(r, side).wait_send()
                for q in range(CHUNKS):
                    gather_z(r, q, side).wait_send()

        return carry

    def pass_line(r, following, more):
        down, up = r < z, r > z
        first = (down & (z == last)) | (up & (z == 0))
        is_end = at_end(r)
        here_far = tokens(far_chunk)

        def send_on(q):
            z_out[r, tokens(q)] = total[r, tokens(q)].astype(z_out.dtype)

            @pl.when(down)
            def _():
                reduce_z(r, q, 0).start()

            @pl.when(up)
            def _():
                reduce_z(r, q, 1).start()

        def far_share():
            return kept[r, 1 - x, here_far] + core_in[r, 1 - x, here_far].astype(jnp.float32)

        for i, (end, _, _) in enumerate(ends):

            @pl.when(first & (r == end))
            def _():
                far_out[i] = far_share().astype(far_out.dtype)
                reduce_far(i).start()

        @pl.when(first & is_end)
        def _():
            send_on(far_chunk)

        @pl.when(more)
        def _():
            reduce_core(following, 0).wait_recv()
            reduce_core(following, 1).wait_recv()

        for q in reversed(range(CHUNKS)):
            here = tokens(q)
            crosses = by_x(r, q)

            @pl.when(crosses)
            def _():
                reduce_x(r, q).wait_recv()

            @pl.when(more & by_x(following, q))
            def _():
                cross(following, q)

            @pl.when(crosses)
            def _():
                total[r, here] += x_in[r, here].astype(jnp.float32)

            @pl.when(first & crosses)
            def _():
                send_on(q)

        @pl.when(more)
        def _():
            total[following] = kept[following, x] + core_in[following, x].astype(jnp.float32)

        for i, (end, _, _) in enumerate(ends):

            @pl.when((r == end) & jnp.logical_not(first))
            def _():
                reduce_far(i).wait_recv()
                far_out[i] = (far_share() + far_in[i].astype(jnp.float32)).astype(far_out.dtype)
                reduce_far(i).start()

        for q in reversed(range(CHUNKS)):
            here = tokens(q)

            @pl.when(down & (z < last))
            def _():
                reduce_z(r, q, 0).wait_recv()
                total[r, here] += z_in[0, r, here].astype(jnp.float32)
                send_on(q)

            @pl.when(up & (z > 0))
            def _():
                reduce_z(r, q, 1).wait_recv()
                total[r, here] += z_in[1, r, here].astype(jnp.float32)
                send_on(q)

    final = 1 if early else 0

    def line_step(t, carry):
        here = last - t
        pass_line(nth_row(here), nth_row(here - 1), here - 1 > final)
        return carry

    if early:

        @pl.when(at_end(z))
        def _():
            pass_line(nearest, nearest, nearest < 0)

    furthest = nth_row(last)
    begin_cross(furthest, furthest != z if rows > 1 else furthest < 0)
    lax.fori_loop(0, rows, drain_gather, 0)
    for i, (_, sends, _) in enumerate(ends):

        @pl.when(sends)
        def _():
            gather_far(i).wait_send()

    lax.fori_loop(0, last - final, line_step, 0)
    if early:

        @pl.when(jnp.logical_not(at_end(z)))
        def _():
            pass_line(nearest, nearest, nearest < 0)

    if rows > 1:
        here_far = tokens(far_chunk)
        for i, (end, _, _) in enumerate(ends):

            @pl.when(z == end)
            def _():
                reduce_far(i).wait_recv()
                given = kept[z, 1 - x, here_far] + core_in[z, 1 - x, here_far].astype(jnp.float32)
                x_out[z, here_far] = (given + far_in[i].astype(jnp.float32)).astype(x_out.dtype)
                reduce_x(z, far_chunk).start()

    for q in range(CHUNKS):
        here = tokens(q)
        reduce_x(z, q).wait_recv()
        total[z, here] += x_in[z, here].astype(jnp.float32)

        @pl.when(z < last)
        def _():
            reduce_z(z, q, 0).wait_recv()
            total[z, here] += z_in[0, z, here].astype(jnp.float32)

        @pl.when(z > 0)
        def _():
            reduce_z(z, q, 1).wait_recv()
            total[z, here] += z_in[1, z, here].astype(jnp.float32)

        out_ref[here] = total[z, here].astype(out_ref.dtype)

    def drain(r, carry):
        for which in range(2):
            reduce_core(r, which).wait_send()
        for q in range(CHUNKS):

            @pl.when(by_x(r, q))
            def _():
                reduce_x(r, q).wait_send()

            @pl.when(r != z)
            def _():
                reduce_z(r, q, 0).wait_send()

        return carry

    lax.fori_loop(0, rows, drain, 0)
    for i, (_, _, sends) in enumerate(ends):

        @pl.when(sends)
        def _():
            reduce_far(i).wait_send()


def dense_layer(activations, expert_ids, gate_scores, gate_proj, up_proj, down_proj):
    rows = lax.axis_size("row")
    group_rows, width = activations.shape
    model, hidden = gate_proj.shape[1:]
    top = expert_ids.shape[1]
    dtype = activations.dtype
    vmem = pl.BlockSpec(memory_space=pltpu.VMEM)
    anywhere = pl.BlockSpec(memory_space=pl.ANY)
    dma = pltpu.SemaphoreType.DMA
    batch = 2 if rows % 2 == 0 else 1
    flops = 6 * rows * group_rows * model * hidden
    return pl.pallas_call(
        functools.partial(dense_kernel, rows),
        out_shape=jax.ShapeDtypeStruct((group_rows, width), dtype),
        in_specs=[anywhere] * 6,
        out_specs=vmem,
        scratch_shapes=[
            pltpu.VMEM((rows, group_rows, model), dtype),
            pltpu.VMEM((top, group_rows), jnp.int32),
            pltpu.VMEM((rows, 2 * top, group_rows), jnp.float32),
            pltpu.VMEM((model, hidden), dtype),
            pltpu.VMEM((model, hidden), dtype),
            pltpu.VMEM((hidden, model), dtype),
            pltpu.VMEM((batch * group_rows, hidden), jnp.float32),
            pltpu.VMEM((batch * group_rows, hidden), jnp.float32),
            pltpu.VMEM((rows, PAIR, group_rows, width), jnp.float32),
            pltpu.VMEM((rows, PAIR, group_rows, width), dtype),
            pltpu.VMEM((rows, PAIR, group_rows, width), dtype),
            pltpu.VMEM((rows, group_rows, width), jnp.float32),
            pltpu.VMEM((rows, group_rows, width), dtype),
            pltpu.VMEM((rows, group_rows, width), dtype),
            pltpu.VMEM((rows, group_rows, width), dtype),
            pltpu.VMEM((PAIR, rows, group_rows, width), dtype),
            pltpu.VMEM((2, group_rows // CHUNKS, width), dtype),
            pltpu.VMEM((2, group_rows // CHUNKS, width), dtype),
            dma((3,)),
            dma((3,)),
            dma((2, rows, CHUNKS)),
            dma((rows, CHUNKS)),
            dma((2, rows)),
            dma((rows,)),
            dma((rows, CHUNKS)),
            dma((rows, CHUNKS)),
            dma((rows, 2, CHUNKS)),
            dma((rows, 2, CHUNKS)),
            dma((rows, 2)),
            dma((rows, 2)),
            dma((rows, CHUNKS)),
            dma((rows, CHUNKS)),
            dma((rows, CHUNKS)),
            dma((2, rows, CHUNKS)),
            dma((2,)),
            dma((2,)),
            dma((2,)),
            dma((2,)),
        ],
        compiler_params=pltpu.CompilerParams(
            collective_id=0, has_side_effects=True, vmem_limit_bytes=64 * 1024 * 1024
        ),
        cost_estimate=pl.CostEstimate(
            flops=flops, bytes_accessed=6 * model * hidden, transcendentals=rows * group_rows * hidden
        ),
    )(activations, expert_ids.T, gate_scores.T, gate_proj, up_proj, down_proj)


def either_way(*arrays):
    activations, expert_ids = arrays[:2]
    col_count, sub_count = lax.axis_size("col"), lax.axis_size("sub")
    experts = lax.axis_size("row") * col_count
    block_rows = expert_ids.shape[0] // (col_count * sub_count)
    every_row = 2 * block_rows * TOP // experts >= block_rows
    if every_row and sub_count == 1 and col_count == PAIR * PAIR:
        return dense_layer(*arrays)
    return per_device(*arrays)


def solution(mesh):
    placed = (
        P(("parts", "row"), ("col", "sub")),
        P(("parts", "row"), None),
        P(("parts", "row"), None),
        P(("row", "col"), None, "sub"),
        P(("row", "col"), None, "sub"),
        P(("row", "col"), "sub", None),
    )
    return jax.shard_map(
        either_way,
        mesh=mesh,
        in_specs=placed,
        out_specs=P(("parts", "row"), ("col", "sub")),
        check_vma=False,
    )
```

```python
import functools

import jax
import jax.numpy as jnp
from jax import lax
from jax.experimental import pallas as pl
from jax.experimental.pallas import tpu as pltpu
from jax.sharding import PartitionSpec as P

TOP = 8
PAIR = 2
CHUNKS = 2
MESH = pl.DeviceIdType.MESH


def slot_places(chosen, experts, capacity):
    count = chosen.shape[0] * chosen.shape[1]
    flat_ids = chosen.reshape(count)
    onehot = (flat_ids[:, None] == jnp.arange(experts, dtype=jnp.int32)[None, :]).astype(jnp.int32)
    running = jnp.cumsum(onehot, axis=0) - 1
    ranking = jnp.sum(onehot * running, axis=1)
    return flat_ids * capacity + ranking


def fill_slots(row_block, places, experts, capacity, top_count):
    owners = jnp.full((experts * capacity,), row_block.shape[0], jnp.int32)
    owners = owners.at[places].set(jnp.arange(places.shape[0], dtype=jnp.int32) // top_count)
    padded = jnp.concatenate(
        [row_block, jnp.zeros((1, row_block.shape[1]), row_block.dtype)], axis=0
    )
    return padded[owners].reshape(experts, capacity, row_block.shape[1])


def run_expert(stacked, gate_proj, up_proj, down_proj):
    layout = stacked.shape
    inputs = stacked.reshape(-1, layout[-1])
    gate_val = jnp.dot(inputs, gate_proj[0], preferred_element_type=jnp.float32)
    up_val = jnp.dot(inputs, up_proj[0], preferred_element_type=jnp.float32)
    hidden = (jax.nn.silu(gate_val) * up_val).astype(jnp.bfloat16)
    partial_out = jnp.dot(hidden, down_proj[0], preferred_element_type=jnp.float32)
    return partial_out.reshape(layout)


def send_back(stacked, gate_proj, up_proj, down_proj):
    partial_out = run_expert(stacked, gate_proj, up_proj, down_proj)
    landed = lax.all_to_all(partial_out, ("row", "col"), split_axis=1, concat_axis=1, tiled=True)
    return lax.psum_scatter(landed, "sub", scatter_dimension=0, tiled=True).astype(jnp.bfloat16)


def per_device(activations, expert_ids, gate_scores, gate_proj, up_proj, down_proj):
    col_count = lax.axis_size("col")
    sub_count = lax.axis_size("sub")
    experts = lax.axis_size("row") * col_count
    group_rows = expert_ids.shape[0]
    block_rows = group_rows // (col_count * sub_count)
    capacity = max(2, min(block_rows, 2 * block_rows * TOP // experts))
    quarter = sub_count * block_rows
    width = activations.shape[1] * col_count * sub_count
    whole = lax.all_gather(activations, ("col", "sub"), axis=1, tiled=True)
    col_start = lax.axis_index("col") * quarter
    sub_index = lax.axis_index("sub")
    my_rows = lax.dynamic_slice_in_dim(whole, col_start, quarter, 0)
    my_ids = lax.dynamic_slice_in_dim(expert_ids, col_start, quarter, 0)
    own_scores = lax.dynamic_slice_in_dim(
        gate_scores, col_start + sub_index * block_rows, block_rows, 0
    )
    places = []
    for member in range(sub_count):
        lower = member * block_rows
        places.append(slot_places(my_ids[lower : lower + block_rows], experts, capacity))
    own_places = lax.dynamic_index_in_dim(jnp.stack(places), sub_index, 0, keepdims=False)
    buffers = []
    for member in range(sub_count):
        lower = member * block_rows
        buffers.append(
            fill_slots(my_rows[lower : lower + block_rows], places[member], experts, capacity, TOP)
        )
    outgoing = jnp.stack(buffers)
    returned = send_back(
        lax.all_to_all(outgoing, ("row", "col"), split_axis=1, concat_axis=1, tiled=True),
        gate_proj,
        up_proj,
        down_proj,
    )
    picked = returned.reshape(-1, width)[own_places].reshape(block_rows, TOP, width)
    share = jnp.sum(own_scores[:, :, None] * picked.astype(jnp.float32), axis=1)
    return lax.all_to_all(
        share.astype(jnp.bfloat16), ("col", "sub"), split_axis=1, concat_axis=0, tiled=True
    )


def dense_kernel(
    rows,
    acts_hbm,
    ids_hbm,
    scores_hbm,
    gate_hbm,
    up_hbm,
    down_hbm,
    out_ref,
    acts,
    ids,
    meta,
    gate_w,
    up_w,
    down_w,
    gate_sum,
    up_sum,
    kept,
    core_out,
    core_in,
    total,
    x_out,
    x_in,
    z_out,
    z_in,
    far_out,
    far_in,
    weight_sem,
    own_sem,
    ag_z_send,
    ag_z_recv,
    meta_send,
    meta_recv,
    ag_x_send,
    ag_x_recv,
    ag_core_send,
    ag_core_recv,
    rs_core_send,
    rs_core_recv,
    rs_x_send,
    rs_x_recv,
    rs_z_send,
    rs_z_recv,
    ag_far_send,
    ag_far_recv,
    rs_far_send,
    rs_far_recv,
):
    top, group_rows = ids_hbm.shape
    part = group_rows // CHUNKS
    width = acts_hbm.shape[1]
    z = lax.axis_index("row")
    col = lax.axis_index("col")
    x, core = col // PAIR, col % PAIR
    expert = z * lax.axis_size("col") + col
    sibling = {"col": x * PAIR + (1 - core)}
    across = {"col": (1 - x) * PAIR + core}
    last = rows - 1

    far_chunk = CHUNKS - 1
    ends = ((0, z < last, z > 0), (last, z > 0, z < last))

    def at_end(r):
        return (r == 0) | (r == last)

    def by_x(r, q):
        return jnp.logical_not(at_end(r)) | (r == z) if q == far_chunk else r >= 0

    def column(x_of, core_of):
        return pl.ds(pl.multiple_of((x_of * PAIR + core_of) * width, width), width)

    def nth_row(s):
        both = jnp.minimum(z, last - z)
        ahead = jnp.where(z <= last - z, 1, -1)
        near = z + ahead * jnp.where(s % 2 == 1, (s + 1) // 2, -(s // 2))
        rest = jnp.where(z <= last - z, s, last - s)
        return jnp.where(s <= 2 * both, near, rest)

    def remote(src, dst, send, recv, device):
        return pltpu.make_async_remote_copy(
            src_ref=src, dst_ref=dst, send_sem=send, recv_sem=recv, device_id=device, device_id_type=MESH
        )

    def position(r, at):
        lower = at <= last - at
        away = jnp.abs(r - at)
        forward = jnp.where(lower, r > at, r < at)
        both = 2 * away - jnp.where(forward, 1, 0)
        return jnp.where(away <= jnp.minimum(at, last - at), both, jnp.where(lower, r, last - r))

    def tokens(q):
        return pl.ds(q * part, part)

    def place(r, q, x_of, core_of, at=None):
        slot = position(r, z if at is None else at)
        return acts.at[slot, tokens(q), column(x_of, core_of)]

    def chunk_of(q):
        return acts_hbm.at[tokens(q)]

    def gather_z(r, q, side, src=None):
        to = jnp.clip(z + 2 * side - 1, 0, last)
        return remote(
            place(r, q, x, core) if src is None else src,
            place(r, q, x, core, to),
            ag_z_send.at[side, r, q],
            ag_z_recv.at[r, q],
            {"row": z + 2 * side - 1},
        )

    def gather_meta(r, side):
        return remote(
            meta.at[r], meta.at[r], meta_send.at[side, r], meta_recv.at[r], {"row": z + 2 * side - 1}
        )

    def gather_x(r, q, src=None):
        there = place(r, q, x, core)
        return remote(there if src is None else src, there, ag_x_send.at[r, q], ag_x_recv.at[r, q], across)

    def gather_core(r, q, which, src=None):
        there = place(r, q, x if which == 0 else 1 - x, core)
        return remote(
            there if src is None else src,
            there,
            ag_core_send.at[r, which, q],
            ag_core_recv.at[r, which, q],
            sibling,
        )

    def reduce_core(r, which):
        x_of = 1 - x if which == 0 else x
        return remote(
            core_out.at[r, x_of],
            core_in.at[r, x_of],
            rs_core_send.at[r, which],
            rs_core_recv.at[r, which],
            sibling,
        )

    def reduce_x(r, q):
        return remote(
            x_out.at[r, tokens(q)], x_in.at[r, tokens(q)], rs_x_send.at[r, q], rs_x_recv.at[r, q], across
        )

    def reduce_z(r, q, side):
        return remote(
            z_out.at[r, tokens(q)],
            z_in.at[side, r, tokens(q)],
            rs_z_send.at[r, q],
            rs_z_recv.at[side, r, q],
            {"row": z + 2 * side - 1},
        )

    def gather_far(i):
        end, to = ends[i][0], jnp.clip(z + 1 - 2 * i, 0, last)
        here, there = place(end, far_chunk, 1 - x, core), place(end, far_chunk, 1 - x, core, to)
        return remote(here, there, ag_far_send.at[i], ag_far_recv.at[i], {"row": z + 1 - 2 * i})

    def reduce_far(i):
        return remote(
            far_out.at[i], far_in.at[i], rs_far_send.at[i], rs_far_recv.at[i], {"row": z + 2 * i - 1}
        )

    weights = [
        pltpu.make_async_copy(src.at[0], dst, weight_sem.at[i])
        for i, (src, dst) in enumerate(((gate_hbm, gate_w), (up_hbm, up_w), (down_hbm, down_w)))
    ]

    own = pltpu.make_async_copy(acts_hbm, acts.at[0, :, column(x, core)], own_sem.at[0])
    own_ids = pltpu.make_async_copy(ids_hbm, ids, own_sem.at[1])
    own_scores = pltpu.make_async_copy(scores_hbm, meta.at[z, pl.ds(top, top)], own_sem.at[2])
    for copy in (own, own_ids, own_scores):
        copy.start()

    barrier = pltpu.get_barrier_semaphore()
    pl.semaphore_signal(barrier, inc=1, device_id=sibling, device_id_type=MESH)
    pl.semaphore_signal(barrier, inc=1, device_id=across, device_id_type=MESH)

    @pl.when(z > 0)
    def _():
        pl.semaphore_signal(barrier, inc=1, device_id={"row": z - 1}, device_id_type=MESH)

    @pl.when(z < last)
    def _():
        pl.semaphore_signal(barrier, inc=1, device_id={"row": z + 1}, device_id_type=MESH)

    pl.semaphore_wait(barrier, 2 + jnp.where(z > 0, 1, 0) + jnp.where(z < last, 1, 0))

    for q in range(CHUNKS):
        gather_x(z, q, chunk_of(q)).start()

        @pl.when(z > 0)
        def _():
            gather_z(z, q, 0, chunk_of(q)).start()

        @pl.when(z < last)
        def _():
            gather_z(z, q, 1, chunk_of(q)).start()

    for q in range(CHUNKS):
        gather_core(z, q, 0, chunk_of(q)).start()
    for copy in weights:
        copy.start()
    own_ids.wait()
    own_scores.wait()
    meta[z, :top] = ids[...].astype(jnp.float32)

    @pl.when(z > 0)
    def _():
        gather_meta(z, 0).start()

    @pl.when(z < last)
    def _():
        gather_meta(z, 1).start()

    own.wait()

    def pass_on(r, q, side, more):
        gather_z(r, q, side).wait_recv()

        @pl.when(more)
        def _():
            gather_z(r, q, side).start()

        @pl.when(by_x(r, q))
        def _():
            gather_x(r, q).start()

        gather_core(r, q, 0).start()

    def pass_meta(r, side, more):
        gather_meta(r, side).wait_recv()

        @pl.when(more)
        def _():
            gather_meta(r, side).start()

    def cross(r, q):
        here = tokens(q)
        given = kept[r, 1 - x, here] + core_in[r, 1 - x, here].astype(jnp.float32)
        x_out[r, here] = given.astype(x_out.dtype)
        reduce_x(r, q).start()

    def begin_cross(r, skip):
        reduce_core(r, 0).wait_recv()
        for q in reversed(range(CHUNKS)):

            @pl.when(jnp.logical_not(skip) if q == far_chunk else r >= 0)
            def _():
                cross(r, q)

        reduce_core(r, 1).wait_recv()
        total[r] = kept[r, x] + core_in[r, x].astype(jnp.float32)

    batch = 2 if rows % 2 == 0 else 1
    half = PAIR * width

    def product(b, x_of, table):
        features = pl.ds(pl.multiple_of(x_of * half, half), half)
        block = acts[pl.ds(b * batch, batch), :, features].reshape(batch * group_rows, half)
        return jnp.dot(block, table[features, :], preferred_element_type=jnp.float32)

    def first_half(b):
        for j in range(batch):
            for q in range(CHUNKS):
                gather_core(nth_row(b * batch + j), q, 0).wait_recv()
        gate_sum[...] = product(b, x, gate_w)
        up_sum[...] = product(b, x, up_w)

    def second_half(b):
        members = [nth_row(b * batch + j) for j in range(batch)]
        for r in members:
            for q in range(CHUNKS):
                gather_core(r, q, 1).wait_recv()
        gate_val = gate_sum[...] + product(b, 1 - x, gate_w)
        up_val = up_sum[...] + product(b, 1 - x, up_w)
        hidden = (gate_val / (1.0 + jnp.exp(-gate_val)) * up_val).astype(jnp.bfloat16)
        scales = []
        for r in members:
            chosen = jnp.where(meta[r, :top] == expert.astype(jnp.float32), meta[r, top:], 0.0)
            scales.append(jnp.sum(jnp.transpose(chosen), axis=1, keepdims=True))

        def weighted(x_of, core_of):
            result = jnp.dot(hidden, down_w[:, column(x_of, core_of)], preferred_element_type=jnp.float32)
            result = result.reshape(batch, group_rows, width)
            return [(r, result[j] * scales[j]) for j, r in enumerate(members)]

        for which, x_of in enumerate((1 - x, x)):
            for r, result in weighted(x_of, 1 - core):
                core_out[r, x_of] = result.astype(core_out.dtype)
            for r in reversed(members):
                reduce_core(r, which).start()
        for x_of in (1 - x, x):
            for r, result in weighted(x_of, core):
                kept[r, x_of] = result

    def arrivals(s):
        below, above = z - 1 - s, z + 1 + s
        from_below, from_above = below >= 0, above <= last
        for q in range(CHUNKS):

            @pl.when(from_below)
            def _():
                pass_on(below, q, 1, z < last)

            @pl.when(from_above)
            def _():
                pass_on(above, q, 0, z > 0)

        @pl.when(from_below)
        def _():
            pass_meta(below, 1, z < last)

        @pl.when(from_above)
        def _():
            pass_meta(above, 0, z > 0)

        r = nth_row(s)
        for q in range(CHUNKS):

            @pl.when(by_x(r, q))
            def _():
                gather_x(r, q).wait_recv()

                if q == far_chunk:
                    for i, (end, sends, _) in enumerate(ends):

                        @pl.when((s == 0) & (z == end) & sends)
                        def _():
                            gather_far(i).start()

                gather_core(r, q, 1, place(r, q, 1 - x, core)).start()

        for i, (end, sends, _) in enumerate(ends):

            @pl.when((s > 0) & ((z - s == end) if i == 0 else (z + s == end)))
            def _():
                gather_far(i).wait_recv()

                @pl.when(sends)
                def _():
                    gather_far(i).start()

                gather_core(end, far_chunk, 1, place(end, far_chunk, 1 - x, core)).start()

    def expert_step(b, carry):
        for j in range(batch):
            arrivals(b * batch + j)
            if j == max(0, batch - 2):

                @pl.when(b == 0)
                def _():
                    for copy in weights[:2]:
                        copy.wait()

                first_half(b)
        if rows > batch:

            @pl.when(b == rows // batch - 1)
            def _():
                begin_cross(z, at_end(z))

        @pl.when(b == 0)
        def _():
            weights[2].wait()

        second_half(b)
        return carry

    lax.fori_loop(0, rows // batch, expert_step, 0)

    if rows == batch and rows > 1:
        begin_cross(z, at_end(z))

    furthest = nth_row(last)
    begin_cross(furthest, furthest != z if rows > 1 else furthest < 0)

    def drain_gather(r, carry):
        for q in range(CHUNKS):

            @pl.when(by_x(r, q))
            def _():
                gather_x(r, q).wait_send()

            gather_core(r, q, 0).wait_send()
            gather_core(r, q, 1).wait_send()

        for side, sent in ((0, (r >= z) & (z > 0)), (1, (r <= z) & (z < last))):

            @pl.when(sent)
            def _():
                gather_meta(r, side).wait_send()
                for q in range(CHUNKS):
                    gather_z(r, q, side).wait_send()

        return carry

    def line_step(t, carry):
        r = nth_row(last - t)
        following = nth_row(last - t - 1)
        down, up = r < z, r > z
        first = (down & (z == last)) | (up & (z == 0))
        is_end = at_end(r)
        here_far = tokens(far_chunk)

        def send_on(q):
            z_out[r, tokens(q)] = total[r, tokens(q)].astype(z_out.dtype)

            @pl.when(down)
            def _():
                reduce_z(r, q, 0).start()

            @pl.when(up)
            def _():
                reduce_z(r, q, 1).start()

        def far_share():
            return kept[r, 1 - x, here_far] + core_in[r, 1 - x, here_far].astype(jnp.float32)

        for i, (end, _, _) in enumerate(ends):

            @pl.when(first & (r == end))
            def _():
                far_out[i] = far_share().astype(far_out.dtype)
                reduce_far(i).start()

        @pl.when(first & is_end)
        def _():
            send_on(far_chunk)

        @pl.when(t < last - 1)
        def _():
            reduce_core(following, 0).wait_recv()
            reduce_core(following, 1).wait_recv()

        for q in reversed(range(CHUNKS)):
            here = tokens(q)
            crosses = by_x(r, q)

            @pl.when(crosses)
            def _():
                reduce_x(r, q).wait_recv()

            @pl.when((t < last - 1) & by_x(following, q))
            def _():
                cross(following, q)

            @pl.when(crosses)
            def _():
                total[r, here] += x_in[r, here].astype(jnp.float32)

            @pl.when(first & crosses)
            def _():
                send_on(q)

        @pl.when(t < last - 1)
        def _():
            total[following] = kept[following, x] + core_in[following, x].astype(jnp.float32)

        for i, (end, _, _) in enumerate(ends):

            @pl.when((r == end) & jnp.logical_not(first))
            def _():
                reduce_far(i).wait_recv()
                far_out[i] = (far_share() + far_in[i].astype(jnp.float32)).astype(far_out.dtype)
                reduce_far(i).start()

        for q in reversed(range(CHUNKS)):
            here = tokens(q)

            @pl.when(down & (z < last))
            def _():
                reduce_z(r, q, 0).wait_recv()
                total[r, here] += z_in[0, r, here].astype(jnp.float32)
                send_on(q)

            @pl.when(up & (z > 0))
            def _():
                reduce_z(r, q, 1).wait_recv()
                total[r, here] += z_in[1, r, here].astype(jnp.float32)
                send_on(q)

        return carry

    lax.fori_loop(0, rows, drain_gather, 0)
    for i, (_, sends, _) in enumerate(ends):

        @pl.when(sends)
        def _():
            gather_far(i).wait_send()

    lax.fori_loop(0, last, line_step, 0)

    if rows > 1:
        here_far = tokens(far_chunk)
        for i, (end, _, _) in enumerate(ends):

            @pl.when(z == end)
            def _():
                reduce_far(i).wait_recv()
                given = kept[z, 1 - x, here_far] + core_in[z, 1 - x, here_far].astype(jnp.float32)
                x_out[z, here_far] = (given + far_in[i].astype(jnp.float32)).astype(x_out.dtype)
                reduce_x(z, far_chunk).start()

    for q in range(CHUNKS):
        here = tokens(q)
        reduce_x(z, q).wait_recv()
        total[z, here] += x_in[z, here].astype(jnp.float32)

        @pl.when(z < last)
        def _():
            reduce_z(z, q, 0).wait_recv()
            total[z, here] += z_in[0, z, here].astype(jnp.float32)

        @pl.when(z > 0)
        def _():
            reduce_z(z, q, 1).wait_recv()
            total[z, here] += z_in[1, z, here].astype(jnp.float32)

        out_ref[here] = total[z, here].astype(out_ref.dtype)

    def drain(r, carry):
        for which in range(2):
            reduce_core(r, which).wait_send()
        for q in range(CHUNKS):

            @pl.when(by_x(r, q))
            def _():
                reduce_x(r, q).wait_send()

            @pl.when(r != z)
            def _():
                reduce_z(r, q, 0).wait_send()

        return carry

    lax.fori_loop(0, rows, drain, 0)
    for i, (_, _, sends) in enumerate(ends):

        @pl.when(sends)
        def _():
            reduce_far(i).wait_send()


def dense_layer(activations, expert_ids, gate_scores, gate_proj, up_proj, down_proj):
    rows = lax.axis_size("row")
    group_rows, width = activations.shape
    model, hidden = gate_proj.shape[1:]
    top = expert_ids.shape[1]
    dtype = activations.dtype
    vmem = pl.BlockSpec(memory_space=pltpu.VMEM)
    anywhere = pl.BlockSpec(memory_space=pl.ANY)
    dma = pltpu.SemaphoreType.DMA
    batch = 2 if rows % 2 == 0 else 1
    flops = 6 * rows * group_rows * model * hidden
    return pl.pallas_call(
        functools.partial(dense_kernel, rows),
        out_shape=jax.ShapeDtypeStruct((group_rows, width), dtype),
        in_specs=[anywhere] * 6,
        out_specs=vmem,
        scratch_shapes=[
            pltpu.VMEM((rows, group_rows, model), dtype),
            pltpu.VMEM((top, group_rows), jnp.int32),
            pltpu.VMEM((rows, 2 * top, group_rows), jnp.float32),
            pltpu.VMEM((model, hidden), dtype),
            pltpu.VMEM((model, hidden), dtype),
            pltpu.VMEM((hidden, model), dtype),
            pltpu.VMEM((batch * group_rows, hidden), jnp.float32),
            pltpu.VMEM((batch * group_rows, hidden), jnp.float32),
            pltpu.VMEM((rows, PAIR, group_rows, width), jnp.float32),
            pltpu.VMEM((rows, PAIR, group_rows, width), dtype),
            pltpu.VMEM((rows, PAIR, group_rows, width), dtype),
            pltpu.VMEM((rows, group_rows, width), jnp.float32),
            pltpu.VMEM((rows, group_rows, width), dtype),
            pltpu.VMEM((rows, group_rows, width), dtype),
            pltpu.VMEM((rows, group_rows, width), dtype),
            pltpu.VMEM((PAIR, rows, group_rows, width), dtype),
            pltpu.VMEM((2, group_rows // CHUNKS, width), dtype),
            pltpu.VMEM((2, group_rows // CHUNKS, width), dtype),
            dma((3,)),
            dma((3,)),
            dma((2, rows, CHUNKS)),
            dma((rows, CHUNKS)),
            dma((2, rows)),
            dma((rows,)),
            dma((rows, CHUNKS)),
            dma((rows, CHUNKS)),
            dma((rows, 2, CHUNKS)),
            dma((rows, 2, CHUNKS)),
            dma((rows, 2)),
            dma((rows, 2)),
            dma((rows, CHUNKS)),
            dma((rows, CHUNKS)),
            dma((rows, CHUNKS)),
            dma((2, rows, CHUNKS)),
            dma((2,)),
            dma((2,)),
            dma((2,)),
            dma((2,)),
        ],
        compiler_params=pltpu.CompilerParams(
            collective_id=0, has_side_effects=True, vmem_limit_bytes=64 * 1024 * 1024
        ),
        cost_estimate=pl.CostEstimate(
            flops=flops, bytes_accessed=6 * model * hidden, transcendentals=rows * group_rows * hidden
        ),
    )(activations, expert_ids.T, gate_scores.T, gate_proj, up_proj, down_proj)


def either_way(*arrays):
    activations, expert_ids = arrays[:2]
    col_count, sub_count = lax.axis_size("col"), lax.axis_size("sub")
    experts = lax.axis_size("row") * col_count
    block_rows = expert_ids.shape[0] // (col_count * sub_count)
    every_row = 2 * block_rows * TOP // experts >= block_rows
    if every_row and sub_count == 1 and col_count == PAIR * PAIR:
        return dense_layer(*arrays)
    return per_device(*arrays)


def solution(mesh):
    placed = (
        P(("parts", "row"), ("col", "sub")),
        P(("parts", "row"), None),
        P(("parts", "row"), None),
        P(("row", "col"), None, "sub"),
        P(("row", "col"), None, "sub"),
        P(("row", "col"), "sub", None),
    )
    return jax.shard_map(
        either_way,
        mesh=mesh,
        in_specs=placed,
        out_specs=P(("parts", "row"), ("col", "sub")),
        check_vma=False,
    )
```

```python
import functools

import jax
import jax.numpy as jnp
from jax import lax
from jax.experimental import pallas as pl
from jax.experimental.pallas import tpu as pltpu
from jax.sharding import PartitionSpec as P

TOP = 8
PAIR = 2
CHUNKS = 2
MESH = pl.DeviceIdType.MESH


def slot_places(chosen, experts, capacity):
    count = chosen.shape[0] * chosen.shape[1]
    flat_ids = chosen.reshape(count)
    onehot = (flat_ids[:, None] == jnp.arange(experts, dtype=jnp.int32)[None, :]).astype(jnp.int32)
    running = jnp.cumsum(onehot, axis=0) - 1
    ranking = jnp.sum(onehot * running, axis=1)
    return flat_ids * capacity + ranking


def fill_slots(row_block, places, experts, capacity, top_count):
    owners = jnp.full((experts * capacity,), row_block.shape[0], jnp.int32)
    owners = owners.at[places].set(jnp.arange(places.shape[0], dtype=jnp.int32) // top_count)
    padded = jnp.concatenate(
        [row_block, jnp.zeros((1, row_block.shape[1]), row_block.dtype)], axis=0
    )
    return padded[owners].reshape(experts, capacity, row_block.shape[1])


def run_expert(stacked, gate_proj, up_proj, down_proj):
    layout = stacked.shape
    inputs = stacked.reshape(-1, layout[-1])
    gate_val = jnp.dot(inputs, gate_proj[0], preferred_element_type=jnp.float32)
    up_val = jnp.dot(inputs, up_proj[0], preferred_element_type=jnp.float32)
    hidden = (jax.nn.silu(gate_val) * up_val).astype(jnp.bfloat16)
    partial_out = jnp.dot(hidden, down_proj[0], preferred_element_type=jnp.float32)
    return partial_out.reshape(layout)


def send_back(stacked, gate_proj, up_proj, down_proj):
    partial_out = run_expert(stacked, gate_proj, up_proj, down_proj)
    landed = lax.all_to_all(partial_out, ("row", "col"), split_axis=1, concat_axis=1, tiled=True)
    return lax.psum_scatter(landed, "sub", scatter_dimension=0, tiled=True).astype(jnp.bfloat16)


def per_device(activations, expert_ids, gate_scores, gate_proj, up_proj, down_proj):
    col_count = lax.axis_size("col")
    sub_count = lax.axis_size("sub")
    experts = lax.axis_size("row") * col_count
    group_rows = expert_ids.shape[0]
    block_rows = group_rows // (col_count * sub_count)
    capacity = max(2, min(block_rows, 2 * block_rows * TOP // experts))
    quarter = sub_count * block_rows
    width = activations.shape[1] * col_count * sub_count
    whole = lax.all_gather(activations, ("col", "sub"), axis=1, tiled=True)
    col_start = lax.axis_index("col") * quarter
    sub_index = lax.axis_index("sub")
    my_rows = lax.dynamic_slice_in_dim(whole, col_start, quarter, 0)
    my_ids = lax.dynamic_slice_in_dim(expert_ids, col_start, quarter, 0)
    own_scores = lax.dynamic_slice_in_dim(
        gate_scores, col_start + sub_index * block_rows, block_rows, 0
    )
    places = []
    for member in range(sub_count):
        lower = member * block_rows
        places.append(slot_places(my_ids[lower : lower + block_rows], experts, capacity))
    own_places = lax.dynamic_index_in_dim(jnp.stack(places), sub_index, 0, keepdims=False)
    buffers = []
    for member in range(sub_count):
        lower = member * block_rows
        buffers.append(
            fill_slots(my_rows[lower : lower + block_rows], places[member], experts, capacity, TOP)
        )
    outgoing = jnp.stack(buffers)
    returned = send_back(
        lax.all_to_all(outgoing, ("row", "col"), split_axis=1, concat_axis=1, tiled=True),
        gate_proj,
        up_proj,
        down_proj,
    )
    picked = returned.reshape(-1, width)[own_places].reshape(block_rows, TOP, width)
    share = jnp.sum(own_scores[:, :, None] * picked.astype(jnp.float32), axis=1)
    return lax.all_to_all(
        share.astype(jnp.bfloat16), ("col", "sub"), split_axis=1, concat_axis=0, tiled=True
    )


def dense_kernel(
    rows,
    acts_hbm,
    ids_hbm,
    scores_hbm,
    gate_hbm,
    up_hbm,
    down_hbm,
    out_ref,
    acts,
    ids,
    meta,
    gate_w,
    up_w,
    down_w,
    gate_sum,
    up_sum,
    kept,
    core_out,
    core_in,
    total,
    x_out,
    x_in,
    z_out,
    z_in,
    far_out,
    far_in,
    weight_sem,
    own_sem,
    ag_z_send,
    ag_z_recv,
    meta_send,
    meta_recv,
    ag_x_send,
    ag_x_recv,
    ag_core_send,
    ag_core_recv,
    rs_core_send,
    rs_core_recv,
    rs_x_send,
    rs_x_recv,
    rs_z_send,
    rs_z_recv,
    ag_far_send,
    ag_far_recv,
    rs_far_send,
    rs_far_recv,
):
    top, group_rows = ids_hbm.shape
    part = group_rows // CHUNKS
    width = acts_hbm.shape[1]
    z = lax.axis_index("row")
    col = lax.axis_index("col")
    x, core = col // PAIR, col % PAIR
    expert = z * lax.axis_size("col") + col
    sibling = {"col": x * PAIR + (1 - core)}
    across = {"col": (1 - x) * PAIR + core}
    last = rows - 1

    far_chunk = CHUNKS - 1
    ends = ((0, z < last, z > 0), (last, z > 0, z < last))

    def at_end(r):
        return (r == 0) | (r == last)

    def by_x(r, q):
        return jnp.logical_not(at_end(r)) | (r == z) if q == far_chunk else r >= 0

    def column(x_of, core_of):
        return pl.ds(pl.multiple_of((x_of * PAIR + core_of) * width, width), width)

    def nth_row(s):
        both = jnp.minimum(z, last - z)
        ahead = jnp.where(z <= last - z, 1, -1)
        near = z + ahead * jnp.where(s % 2 == 1, (s + 1) // 2, -(s // 2))
        rest = jnp.where(z <= last - z, s, last - s)
        return jnp.where(s <= 2 * both, near, rest)

    def remote(src, dst, send, recv, device):
        return pltpu.make_async_remote_copy(
            src_ref=src, dst_ref=dst, send_sem=send, recv_sem=recv, device_id=device, device_id_type=MESH
        )

    def position(r, at):
        lower = at <= last - at
        away = jnp.abs(r - at)
        forward = jnp.where(lower, r > at, r < at)
        both = 2 * away - jnp.where(forward, 1, 0)
        return jnp.where(away <= jnp.minimum(at, last - at), both, jnp.where(lower, r, last - r))

    def tokens(q):
        return pl.ds(q * part, part)

    def place(r, q, x_of, core_of, at=None):
        slot = position(r, z if at is None else at)
        return acts.at[slot, tokens(q), column(x_of, core_of)]

    def chunk_of(q):
        return acts_hbm.at[tokens(q)]

    def gather_z(r, q, side, src=None):
        to = jnp.clip(z + 2 * side - 1, 0, last)
        return remote(
            place(r, q, x, core) if src is None else src,
            place(r, q, x, core, to),
            ag_z_send.at[side, r, q],
            ag_z_recv.at[r, q],
            {"row": z + 2 * side - 1},
        )

    def gather_meta(r, side):
        return remote(
            meta.at[r], meta.at[r], meta_send.at[side, r], meta_recv.at[r], {"row": z + 2 * side - 1}
        )

    def gather_x(r, q, src=None):
        there = place(r, q, x, core)
        return remote(there if src is None else src, there, ag_x_send.at[r, q], ag_x_recv.at[r, q], across)

    def gather_core(r, q, which, src=None):
        there = place(r, q, x if which == 0 else 1 - x, core)
        return remote(
            there if src is None else src,
            there,
            ag_core_send.at[r, which, q],
            ag_core_recv.at[r, which, q],
            sibling,
        )

    def reduce_core(r, which):
        x_of = 1 - x if which == 0 else x
        return remote(
            core_out.at[r, x_of],
            core_in.at[r, x_of],
            rs_core_send.at[r, which],
            rs_core_recv.at[r, which],
            sibling,
        )

    def reduce_x(r, q):
        return remote(
            x_out.at[r, tokens(q)], x_in.at[r, tokens(q)], rs_x_send.at[r, q], rs_x_recv.at[r, q], across
        )

    def reduce_z(r, q, side):
        return remote(
            z_out.at[r, tokens(q)],
            z_in.at[side, r, tokens(q)],
            rs_z_send.at[r, q],
            rs_z_recv.at[side, r, q],
            {"row": z + 2 * side - 1},
        )

    def gather_far(i):
        end, to = ends[i][0], jnp.clip(z + 1 - 2 * i, 0, last)
        here, there = place(end, far_chunk, 1 - x, core), place(end, far_chunk, 1 - x, core, to)
        return remote(here, there, ag_far_send.at[i], ag_far_recv.at[i], {"row": z + 1 - 2 * i})

    def reduce_far(i):
        return remote(
            far_out.at[i], far_in.at[i], rs_far_send.at[i], rs_far_recv.at[i], {"row": z + 2 * i - 1}
        )

    weights = [
        pltpu.make_async_copy(src.at[0], dst, weight_sem.at[i])
        for i, (src, dst) in enumerate(((gate_hbm, gate_w), (up_hbm, up_w), (down_hbm, down_w)))
    ]

    own = pltpu.make_async_copy(acts_hbm, acts.at[0, :, column(x, core)], own_sem.at[0])
    own_ids = pltpu.make_async_copy(ids_hbm, ids, own_sem.at[1])
    own_scores = pltpu.make_async_copy(scores_hbm, meta.at[z, pl.ds(top, top)], own_sem.at[2])
    for copy in (own, own_ids, own_scores):
        copy.start()

    barrier = pltpu.get_barrier_semaphore()
    pl.semaphore_signal(barrier, inc=1, device_id=sibling, device_id_type=MESH)
    pl.semaphore_signal(barrier, inc=1, device_id=across, device_id_type=MESH)

    @pl.when(z > 0)
    def _():
        pl.semaphore_signal(barrier, inc=1, device_id={"row": z - 1}, device_id_type=MESH)

    @pl.when(z < last)
    def _():
        pl.semaphore_signal(barrier, inc=1, device_id={"row": z + 1}, device_id_type=MESH)

    pl.semaphore_wait(barrier, 2 + jnp.where(z > 0, 1, 0) + jnp.where(z < last, 1, 0))

    for q in range(CHUNKS):
        gather_x(z, q, chunk_of(q)).start()

        @pl.when(z > 0)
        def _():
            gather_z(z, q, 0, chunk_of(q)).start()

        @pl.when(z < last)
        def _():
            gather_z(z, q, 1, chunk_of(q)).start()

    for q in range(CHUNKS):
        gather_core(z, q, 0, chunk_of(q)).start()
    for copy in weights:
        copy.start()
    own_ids.wait()
    own_scores.wait()
    meta[z, :top] = ids[...].astype(jnp.float32)

    @pl.when(z > 0)
    def _():
        gather_meta(z, 0).start()

    @pl.when(z < last)
    def _():
        gather_meta(z, 1).start()

    own.wait()

    def pass_on(r, q, side, more):
        gather_z(r, q, side).wait_recv()

        @pl.when(more)
        def _():
            gather_z(r, q, side).start()

        @pl.when(by_x(r, q))
        def _():
            gather_x(r, q).start()

        gather_core(r, q, 0).start()

    def pass_meta(r, side, more):
        gather_meta(r, side).wait_recv()

        @pl.when(more)
        def _():
            gather_meta(r, side).start()

    def cross(r, q):
        here = tokens(q)
        given = kept[r, 1 - x, here] + core_in[r, 1 - x, here].astype(jnp.float32)
        x_out[r, here] = given.astype(x_out.dtype)
        reduce_x(r, q).start()

    def begin_cross(r, skip):
        reduce_core(r, 0).wait_recv()
        for q in reversed(range(CHUNKS)):

            @pl.when(jnp.logical_not(skip) if q == far_chunk else r >= 0)
            def _():
                cross(r, q)

        reduce_core(r, 1).wait_recv()
        total[r] = kept[r, x] + core_in[r, x].astype(jnp.float32)

    batch = 2 if rows % 2 == 0 else 1
    half = PAIR * width

    def product(b, x_of, table):
        features = pl.ds(pl.multiple_of(x_of * half, half), half)
        block = acts[pl.ds(b * batch, batch), :, features].reshape(batch * group_rows, half)
        return jnp.dot(block, table[features, :], preferred_element_type=jnp.float32)

    def first_half(b):
        for j in range(batch):
            for q in range(CHUNKS):
                gather_core(nth_row(b * batch + j), q, 0).wait_recv()
        gate_sum[...] = product(b, x, gate_w)
        up_sum[...] = product(b, x, up_w)

    def second_half(b):
        members = [nth_row(b * batch + j) for j in range(batch)]
        for r in members:
            for q in range(CHUNKS):
                gather_core(r, q, 1).wait_recv()
        gate_val = gate_sum[...] + product(b, 1 - x, gate_w)
        up_val = up_sum[...] + product(b, 1 - x, up_w)
        hidden = (gate_val / (1.0 + jnp.exp(-gate_val)) * up_val).astype(jnp.bfloat16)
        scales = []
        for r in members:
            chosen = jnp.where(meta[r, :top] == expert.astype(jnp.float32), meta[r, top:], 0.0)
            scales.append(jnp.sum(jnp.transpose(chosen), axis=1, keepdims=True))

        def weighted(x_of, core_of):
            result = jnp.dot(hidden, down_w[:, column(x_of, core_of)], preferred_element_type=jnp.float32)
            result = result.reshape(batch, group_rows, width)
            return [(r, result[j] * scales[j]) for j, r in enumerate(members)]

        for which, x_of in enumerate((1 - x, x)):
            for r, result in weighted(x_of, 1 - core):
                core_out[r, x_of] = result.astype(core_out.dtype)
            for r in reversed(members):
                reduce_core(r, which).start()
        for x_of in (1 - x, x):
            for r, result in weighted(x_of, core):
                kept[r, x_of] = result

    def arrivals(s):
        below, above = z - 1 - s, z + 1 + s
        from_below, from_above = below >= 0, above <= last
        for q in range(CHUNKS):

            @pl.when(from_below)
            def _():
                pass_on(below, q, 1, z < last)

            @pl.when(from_above)
            def _():
                pass_on(above, q, 0, z > 0)

        @pl.when(from_below)
        def _():
            pass_meta(below, 1, z < last)

        @pl.when(from_above)
        def _():
            pass_meta(above, 0, z > 0)

        r = nth_row(s)
        for q in range(CHUNKS):

            @pl.when(by_x(r, q))
            def _():
                gather_x(r, q).wait_recv()

                if q == far_chunk:
                    for i, (end, sends, _) in enumerate(ends):

                        @pl.when((s == 0) & (z == end) & sends)
                        def _():
                            gather_far(i).start()

                gather_core(r, q, 1, place(r, q, 1 - x, core)).start()

        for i, (end, sends, _) in enumerate(ends):

            @pl.when((s > 0) & ((z - s == end) if i == 0 else (z + s == end)))
            def _():
                gather_far(i).wait_recv()

                @pl.when(sends)
                def _():
                    gather_far(i).start()

                gather_core(end, far_chunk, 1, place(end, far_chunk, 1 - x, core)).start()

    def expert_step(b, carry):
        for j in range(batch):
            arrivals(b * batch + j)
            if j == max(0, batch - 2):

                @pl.when(b == 0)
                def _():
                    for copy in weights[:2]:
                        copy.wait()

                first_half(b)
        if rows > batch:

            @pl.when(b == rows // batch - 1)
            def _():
                begin_cross(z, at_end(z))

        @pl.when(b == 0)
        def _():
            weights[2].wait()

        second_half(b)
        return carry

    lax.fori_loop(0, rows // batch, expert_step, 0)

    if rows == batch and rows > 1:
        begin_cross(z, at_end(z))

    furthest = nth_row(last)
    begin_cross(furthest, furthest != z if rows > 1 else furthest < 0)

    def cross_step(t, carry):
        r = nth_row(last - t)
        begin_cross(r, at_end(r))
        return carry

    lax.fori_loop(1, last, cross_step, 0)

    def drain_gather(r, carry):
        for q in range(CHUNKS):

            @pl.when(by_x(r, q))
            def _():
                gather_x(r, q).wait_send()

            gather_core(r, q, 0).wait_send()
            gather_core(r, q, 1).wait_send()

        for side, sent in ((0, (r >= z) & (z > 0)), (1, (r <= z) & (z < last))):

            @pl.when(sent)
            def _():
                gather_meta(r, side).wait_send()
                for q in range(CHUNKS):
                    gather_z(r, q, side).wait_send()

        return carry

    def line_step(t, carry):
        r = nth_row(last - t)
        down, up = r < z, r > z
        first = (down & (z == last)) | (up & (z == 0))
        is_end = at_end(r)
        here_far = tokens(far_chunk)

        def send_on(q):
            z_out[r, tokens(q)] = total[r, tokens(q)].astype(z_out.dtype)

            @pl.when(down)
            def _():
                reduce_z(r, q, 0).start()

            @pl.when(up)
            def _():
                reduce_z(r, q, 1).start()

        def far_share():
            return kept[r, 1 - x, here_far] + core_in[r, 1 - x, here_far].astype(jnp.float32)

        for i, (end, _, _) in enumerate(ends):

            @pl.when(first & (r == end))
            def _():
                far_out[i] = far_share().astype(far_out.dtype)
                reduce_far(i).start()

        @pl.when(first & is_end)
        def _():
            send_on(far_chunk)

        for q in reversed(range(CHUNKS)):
            here = tokens(q)
            crosses = by_x(r, q)

            @pl.when(crosses)
            def _():
                reduce_x(r, q).wait_recv()

            @pl.when(crosses)
            def _():
                total[r, here] += x_in[r, here].astype(jnp.float32)

            @pl.when(first & crosses)
            def _():
                send_on(q)

        for i, (end, _, _) in enumerate(ends):

            @pl.when((r == end) & jnp.logical_not(first))
            def _():
                reduce_far(i).wait_recv()
                far_out[i] = (far_share() + far_in[i].astype(jnp.float32)).astype(far_out.dtype)
                reduce_far(i).start()

        for q in reversed(range(CHUNKS)):
            here = tokens(q)

            @pl.when(down & (z < last))
            def _():
                reduce_z(r, q, 0).wait_recv()
                total[r, here] += z_in[0, r, here].astype(jnp.float32)
                send_on(q)

            @pl.when(up & (z > 0))
            def _():
                reduce_z(r, q, 1).wait_recv()
                total[r, here] += z_in[1, r, here].astype(jnp.float32)
                send_on(q)

        return carry

    lax.fori_loop(0, rows, drain_gather, 0)
    for i, (_, sends, _) in enumerate(ends):

        @pl.when(sends)
        def _():
            gather_far(i).wait_send()

    lax.fori_loop(0, last, line_step, 0)

    if rows > 1:
        here_far = tokens(far_chunk)
        for i, (end, _, _) in enumerate(ends):

            @pl.when(z == end)
            def _():
                reduce_far(i).wait_recv()
                given = kept[z, 1 - x, here_far] + core_in[z, 1 - x, here_far].astype(jnp.float32)
                x_out[z, here_far] = (given + far_in[i].astype(jnp.float32)).astype(x_out.dtype)
                reduce_x(z, far_chunk).start()

    for q in range(CHUNKS):
        here = tokens(q)
        reduce_x(z, q).wait_recv()
        total[z, here] += x_in[z, here].astype(jnp.float32)

        @pl.when(z < last)
        def _():
            reduce_z(z, q, 0).wait_recv()
            total[z, here] += z_in[0, z, here].astype(jnp.float32)

        @pl.when(z > 0)
        def _():
            reduce_z(z, q, 1).wait_recv()
            total[z, here] += z_in[1, z, here].astype(jnp.float32)

        out_ref[here] = total[z, here].astype(out_ref.dtype)

    def drain(r, carry):
        for which in range(2):
            reduce_core(r, which).wait_send()
        for q in range(CHUNKS):

            @pl.when(by_x(r, q))
            def _():
                reduce_x(r, q).wait_send()

            @pl.when(r != z)
            def _():
                reduce_z(r, q, 0).wait_send()

        return carry

    lax.fori_loop(0, rows, drain, 0)
    for i, (_, _, sends) in enumerate(ends):

        @pl.when(sends)
        def _():
            reduce_far(i).wait_send()


def dense_layer(activations, expert_ids, gate_scores, gate_proj, up_proj, down_proj):
    rows = lax.axis_size("row")
    group_rows, width = activations.shape
    model, hidden = gate_proj.shape[1:]
    top = expert_ids.shape[1]
    dtype = activations.dtype
    vmem = pl.BlockSpec(memory_space=pltpu.VMEM)
    anywhere = pl.BlockSpec(memory_space=pl.ANY)
    dma = pltpu.SemaphoreType.DMA
    batch = 2 if rows % 2 == 0 else 1
    flops = 6 * rows * group_rows * model * hidden
    return pl.pallas_call(
        functools.partial(dense_kernel, rows),
        out_shape=jax.ShapeDtypeStruct((group_rows, width), dtype),
        in_specs=[anywhere] * 6,
        out_specs=vmem,
        scratch_shapes=[
            pltpu.VMEM((rows, group_rows, model), dtype),
            pltpu.VMEM((top, group_rows), jnp.int32),
            pltpu.VMEM((rows, 2 * top, group_rows), jnp.float32),
            pltpu.VMEM((model, hidden), dtype),
            pltpu.VMEM((model, hidden), dtype),
            pltpu.VMEM((hidden, model), dtype),
            pltpu.VMEM((batch * group_rows, hidden), jnp.float32),
            pltpu.VMEM((batch * group_rows, hidden), jnp.float32),
            pltpu.VMEM((rows, PAIR, group_rows, width), jnp.float32),
            pltpu.VMEM((rows, PAIR, group_rows, width), dtype),
            pltpu.VMEM((rows, PAIR, group_rows, width), dtype),
            pltpu.VMEM((rows, group_rows, width), jnp.float32),
            pltpu.VMEM((rows, group_rows, width), dtype),
            pltpu.VMEM((rows, group_rows, width), dtype),
            pltpu.VMEM((rows, group_rows, width), dtype),
            pltpu.VMEM((PAIR, rows, group_rows, width), dtype),
            pltpu.VMEM((2, group_rows // CHUNKS, width), dtype),
            pltpu.VMEM((2, group_rows // CHUNKS, width), dtype),
            dma((3,)),
            dma((3,)),
            dma((2, rows, CHUNKS)),
            dma((rows, CHUNKS)),
            dma((2, rows)),
            dma((rows,)),
            dma((rows, CHUNKS)),
            dma((rows, CHUNKS)),
            dma((rows, 2, CHUNKS)),
            dma((rows, 2, CHUNKS)),
            dma((rows, 2)),
            dma((rows, 2)),
            dma((rows, CHUNKS)),
            dma((rows, CHUNKS)),
            dma((rows, CHUNKS)),
            dma((2, rows, CHUNKS)),
            dma((2,)),
            dma((2,)),
            dma((2,)),
            dma((2,)),
        ],
        compiler_params=pltpu.CompilerParams(
            collective_id=0, has_side_effects=True, vmem_limit_bytes=64 * 1024 * 1024
        ),
        cost_estimate=pl.CostEstimate(
            flops=flops, bytes_accessed=6 * model * hidden, transcendentals=rows * group_rows * hidden
        ),
    )(activations, expert_ids.T, gate_scores.T, gate_proj, up_proj, down_proj)


def either_way(*arrays):
    activations, expert_ids = arrays[:2]
    col_count, sub_count = lax.axis_size("col"), lax.axis_size("sub")
    experts = lax.axis_size("row") * col_count
    block_rows = expert_ids.shape[0] // (col_count * sub_count)
    every_row = 2 * block_rows * TOP // experts >= block_rows
    if every_row and sub_count == 1 and col_count == PAIR * PAIR:
        return dense_layer(*arrays)
    return per_device(*arrays)


def solution(mesh):
    placed = (
        P(("parts", "row"), ("col", "sub")),
        P(("parts", "row"), None),
        P(("parts", "row"), None),
        P(("row", "col"), None, "sub"),
        P(("row", "col"), None, "sub"),
        P(("row", "col"), "sub", None),
    )
    return jax.shard_map(
        either_way,
        mesh=mesh,
        in_specs=placed,
        out_specs=P(("parts", "row"), ("col", "sub")),
        check_vma=False,
    )
```
